32 devices in a mesh: graph: 8 (over y, x, core), col: 4 (over z).
Axes of the slice: x: 2, y: 2, z: 4, core: 2. Of those that a mesh axis runs over, the one named last changes fastest.
Arguments:
- features: float32 [8, 100, 8192], P('graph'), may hold values from -6 to 6
- blocks: int32 [8, 2, 512], P('graph'), may hold values from 0 to 63, as said below
- block_values: float32 [8, 512, 128, 128], P('graph'), may hold values from 0 to 0.001953125
- group_sizes: int32 [8, 2], replicated, may hold values from 8 to 8192, as said below
- labels: int32 [8, 8192], P('graph'), may hold values from 0 to 46
- pair_nodes: int32 [8, 2, 8, 8], P('graph'), may hold values from 0 to 8191, as said below
- weight_first: float32 [2, 100, 256], P(None, None, 'col'), may hold values from -0.4375 to 0.4375
- weight_second: float32 [2, 256, 256], P(None, None, 'col'), may hold values from -0.25 to 0.25
- weight_head: float32 [2, 256, 47], P(None, 'col'), may hold values from -0.25 to 0.25
- norm_params: float32 [2, 2, 256], P(None, None, 'col'), may hold values from 0.5 to 1.5
- momentum_first: float32 [2, 100, 256], P(None, None, 'col'), may hold values from -0.125 to 0.125
- momentum_second: float32 [2, 256, 256], P(None, None, 'col'), may hold values from -0.125 to 0.125
- momentum_head: float32 [2, 256, 47], P(None, 'col'), may hold values from -0.125 to 0.125
- momentum_norms: float32 [2, 2, 256], P(None, None, 'col'), may hold values from -0.5 to 0.5
- average_first: float32 [2, 100, 256], P(None, None, 'col'), may hold values from -0.4375 to 0.4375
- average_second: float32 [2, 256, 256], P(None, None, 'col'), may hold values from -0.25 to 0.25
- average_head: float32 [2, 256, 47], P(None, 'col'), may hold values from -0.25 to 0.25
- average_norms: float32 [2, 2, 256], P(None, None, 'col'), may hold values from 0.5 to 1.5
Outputs:
- loss_sum: float32 [], replicated
- node_count: float32 [], replicated
- momentum_first_new: float32 [2, 100, 256], P(None, None, 'col')
- average_first_new: float32 [2, 100, 256], P(None, None, 'col')
- weight_first_new: float32 [2, 100, 256], P(None, None, 'col')
- momentum_second_new: float32 [2, 256, 256], P(None, None, 'col')
- average_second_new: float32 [2, 256, 256], P(None, None, 'col')
- weight_second_new: float32 [2, 256, 256], P(None, None, 'col')
- momentum_head_new: float32 [2, 256, 47], P(None, 'col')
- average_head_new: float32 [2, 256, 47], P(None, 'col')
- weight_head_new: float32 [2, 256, 47], P(None, 'col')
- momentum_norms_new: float32 [2, 2, 256], P(None, None, 'col')
- average_norms_new: float32 [2, 2, 256], P(None, None, 'col')
- norms_new: float32 [2, 2, 256], P(None, None, 'col')
The draws below stay inside these ranges and needn't reach their ends.
Inputs may be any that keep to these rules, and one draw needn't show every extreme that they name: `group_sizes`: row g gives subgraph g's live nodes, a multiple of 128, then its live blocks, live nodes * 8 / 128; some subgraph has all 8192 nodes live. Both block numbers of subgraph g lie below its live nodes / 128; only the first group_sizes[g,1] blocks count. `pair_nodes`: node numbers of subgraph g lie below its live nodes.
All inputs are finite; a program needn't handle non-finite values.
Results may differ from the reference program's by a relative error of at most 0.0003.
Values sent between devices are 32-bit elements; how exact they have to be, the bound alone decides.
A program may use at most 192 MiB of HBM per device.

```python
from functools import partial
import jax
import jax.numpy as jnp
from jax import lax

FIN = 100
HID = 256
CLS = 47
BS = 128
BLOCKS_ROW = 8
NODES = 8192
PAIR_PEER = 8
BLK = 512
GROUPS = 8


def live_row_blocks(key):
    row_blocks = NODES // BS
    keys = jax.random.split(jax.random.fold_in(key, 101), 3)
    lowest = max(1, row_blocks // 8)
    upper = max(lowest, row_blocks // 4)
    modest = jax.random.randint(keys[0], (GROUPS,), lowest, upper + 1)
    larger = jax.random.randint(keys[1], (GROUPS,), 0, 8) == 0
    chosen = jax.random.permutation(keys[2], GROUPS)[0]
    counts = jnp.where(larger, row_blocks, modest).astype(jnp.int32)
    return (counts.at[chosen].set(row_blocks), chosen)


def draw_group_sizes(key, part):
    counts, chosen = live_row_blocks(key)
    return jnp.stack([counts * BS, counts * BLOCKS_ROW], axis=1).astype(jnp.int32)


def draw_blocks(key, part):
    counts, chosen = live_row_blocks(key)
    key = jax.random.fold_in(key, 5)
    keys = jax.random.split(key, 2)
    row_ids = jax.random.randint(keys[0], (GROUPS, BLK), 0, counts[:, None])
    col_ids = jax.random.randint(keys[1], (GROUPS, BLK), 0, counts[:, None])
    row_ids = row_ids.at[chosen, 0].set(NODES // BS - 1)
    col_ids = col_ids.at[chosen, 0].set(NODES // BS - 1)
    return jnp.stack([row_ids, col_ids], axis=1).astype(jnp.int32)


def draw_pair_nodes(key, part):
    counts, chosen = live_row_blocks(key)
    key = jax.random.fold_in(key, 7)
    limits = (counts * BS)[:, None, None, None]
    result = jax.random.randint(key, (GROUPS, 2, GROUPS, PAIR_PEER), 0, limits)
    return result.at[chosen, 0, 0, 0].set(NODES - 1).astype(jnp.int32)


def touch_ends(drawn, key, least, high):
    longest = drawn.shape.index(max(drawn.shape))
    spots = []
    for shift in (0, 1):
        where = [jax.random.randint(jax.random.fold_in(key, axis), (), 0, length) for axis, length in enumerate(drawn.shape)]
        where[longest] = (where[longest] + shift) % drawn.shape[longest]
        spots.append(tuple(where))
    return drawn.at[spots[0]].set(least).at[spots[1]].set(high)


def block_scale(key, dims, pieces, low, high):
    gain = 1.0
    for position, shards_of in pieces:
        draws = jax.random.uniform(jax.random.fold_in(jax.random.fold_in(key, 6), position), (shards_of,), jnp.float32, low / len(pieces), high / len(pieces))
        gain = gain * jnp.repeat(jnp.exp(draws), dims[position] // shards_of).reshape((-1,) + (1,) * (len(dims) - 1 - position))
    return gain


def bell_draw(rng, extent, scale, bound, cuts=(), kind=jnp.bfloat16):
    level = block_scale(rng, extent, cuts, -0.22, 0.18) if cuts else 1.0
    array = jax.random.normal(rng, extent, jnp.float32) * scale * level
    return jnp.minimum(jnp.maximum(array, -bound), bound).astype(kind)


def setup_inputs(seed: int = 0) -> dict:
    streams_of = jax.random.split(jax.random.key(seed), 19)
    features = bell_draw(streams_of[0], (GROUPS, FIN, NODES), 1.0, 6.0, ((0, 8),), jnp.float32)
    blocks = draw_blocks(jax.random.fold_in(streams_of[18], 71), 0)
    block_values = jnp.clip(0.001953125 * jax.random.uniform(streams_of[2], (GROUPS, BLK, BS, BS), jnp.float32) ** block_scale(streams_of[2], (GROUPS, BLK, BS, BS), ((0, 8),), -0.2, 0.2), 0.0, 0.001953125)
    group_sizes = draw_group_sizes(jax.random.fold_in(streams_of[18], 71), 0)
    labels = touch_ends(jax.random.randint(streams_of[4], (GROUPS, NODES), 0, CLS), jax.random.fold_in(streams_of[4], 1), 0, CLS - 1).astype(jnp.int32)
    pair_nodes = draw_pair_nodes(jax.random.fold_in(streams_of[18], 71), 0)
    weight_first = bell_draw(streams_of[6], (2, FIN, HID), (2 * FIN) ** -0.5, 0.4375, ((2, 4),), jnp.float32)
    weight_second = bell_draw(streams_of[7], (2, HID, HID), (2 * HID) ** -0.5, 0.25, ((2, 4),), jnp.float32)
    weight_head = bell_draw(streams_of[8], (2, HID, CLS), (2 * HID) ** -0.5, 0.25, ((1, 4),), jnp.float32)
    norm_params = jnp.clip(1.0 + 0.1 * jax.random.normal(streams_of[9], (2, 2, HID), jnp.float32), 0.5, 1.5)
    momentum_first = bell_draw(streams_of[10], (2, FIN, HID), (2.0 * (NODES * GROUPS) ** -0.5), 0.125, ((2, 4),), jnp.float32)
    momentum_second = bell_draw(streams_of[11], (2, HID, HID), (2.0 * (NODES * GROUPS) ** -0.5), 0.125, ((2, 4),), jnp.float32)
    momentum_head = bell_draw(streams_of[12], (2, HID, CLS), (2.0 * (NODES * GROUPS) ** -0.5), 0.125, ((1, 4),), jnp.float32)
    momentum_norms = bell_draw(streams_of[13], (2, 2, HID), (8.0 * (NODES * GROUPS) ** -0.5), 0.5, ((2, 4),), jnp.float32)
    average_first = bell_draw(streams_of[14], (2, FIN, HID), (2 * FIN) ** -0.5, 0.4375, ((2, 4),), jnp.float32)
    average_second = bell_draw(streams_of[15], (2, HID, HID), (2 * HID) ** -0.5, 0.25, ((2, 4),), jnp.float32)
    average_head = bell_draw(streams_of[16], (2, HID, CLS), (2 * HID) ** -0.5, 0.25, ((1, 4),), jnp.float32)
    average_norms = jnp.clip(1.0 + 0.1 * jax.random.normal(streams_of[17], (2, 2, HID), jnp.float32), 0.5, 1.5)
    return {"features": features, "blocks": blocks, "block_values": block_values, "group_sizes": group_sizes, "labels": labels, "pair_nodes": pair_nodes, "weight_first": weight_first, "weight_second": weight_second, "weight_head": weight_head, "norm_params": norm_params, "momentum_first": momentum_first, "momentum_second": momentum_second, "momentum_head": momentum_head, "momentum_norms": momentum_norms, "average_first": average_first, "average_second": average_second, "average_head": average_head, "average_norms": average_norms}


PRECISE = lax.Precision.HIGHEST
NORM_EPS = 1e-05
MOMENTUM = 0.9
STEP_RATE = 2.0
AVERAGE_KEEP = 0.9
PAIR_WEIGHT = 0.5

@jax.custom_vjp
def low(v):
    return lax.optimization_barrier(v.astype(jnp.bfloat16)).astype(jnp.float32)

@jax.custom_vjp
def low_back(v):
    return v

def low_keep(v):
    return (low(v), None)

def low_pass(kept, grad):
    return (grad,)

def back_keep(v):
    return (v, None)

def back_low(kept, grad):
    return (low(grad),)
low.defvjp(low_keep, low_pass)
low_back.defvjp(back_keep, back_low)

def aggregate(source, coords, values, live_blocks):
    channels, node_total = source.shape
    row_blocks = node_total // BS
    picked = source.reshape(channels, row_blocks, BS)[:, coords[1], :]
    alive_blocks = (jnp.arange(coords.shape[1], dtype=jnp.int32) < live_blocks).astype(jnp.float32)
    product = jnp.einsum('cbj,bji->cbi', picked, values, precision=PRECISE) * alive_blocks[None, :, None]
    onehot = (coords[0][:, None] == jnp.arange(row_blocks, dtype=jnp.int32)[None, :]).astype(jnp.float32)
    return jnp.einsum('cbi,br->cri', product, onehot, precision=PRECISE).reshape(channels, node_total)

def project(weight, direct, spread):
    return jnp.einsum('fo,fn->on', weight[0], direct, precision=PRECISE) + jnp.einsum('fo,fn->on', weight[1], spread, precision=PRECISE)

def norm_act(pre_act, gain_bias, live_mask, live_count):
    average = lax.optimization_barrier(jnp.sum(pre_act * live_mask, axis=1, keepdims=True)) / live_count
    centred = pre_act - average
    variance = lax.optimization_barrier(jnp.sum(centred * centred * live_mask, axis=1, keepdims=True)) / live_count
    scaled = centred * lax.rsqrt(variance + NORM_EPS) * gain_bias[0][:, None] + gain_bias[1][:, None]
    return jax.nn.gelu(scaled, approximate=True)

def group_forward(weights, inputs):
    weight_first, weight_second, weight_head, norm_params = weights
    features, coords, values, counts, labels = inputs
    node_total = features.shape[1]
    live_mask = (jnp.arange(node_total, dtype=jnp.int32) < counts[0]).astype(jnp.float32)
    live_count = counts[0].astype(jnp.float32)

    def spread_of(source):
        return aggregate(source, coords, values, counts[1])
    hidden_one = norm_act(project(weight_first, features, spread_of(features)), norm_params[0], live_mask, live_count)
    hidden_two = norm_act(project(weight_second, hidden_one, spread_of(hidden_one)), norm_params[1], live_mask, live_count)
    logits = project(weight_head, hidden_two, spread_of(hidden_two))
    largest = lax.optimization_barrier(jnp.max(logits, axis=0, keepdims=True))
    log_total = largest[0] + jnp.log(lax.optimization_barrier(jnp.sum(jnp.exp(logits - largest), axis=0)))
    onehot = (labels[None, :] == jnp.arange(logits.shape[0], dtype=jnp.int32)[:, None]).astype(jnp.float32)
    target = lax.optimization_barrier(jnp.sum(onehot * logits, axis=0))
    return (logits, jnp.sum((log_total - target) * live_mask))

def loss_of(weights, features, blocks, block_values, group_sizes, labels, pair_nodes):
    logits, cross_sum = lax.map(jax.checkpoint(partial(group_forward, weights)), (features, blocks, block_values, group_sizes, labels))
    group_count = logits.shape[0]
    classes = logits.shape[1]
    sent_logits = jax.vmap(lambda table, ids: table[:, ids.reshape(-1)])(logits, pair_nodes[:, 0])
    sent_logits = sent_logits.reshape(group_count, classes, group_count, -1).transpose(2, 1, 0, 3)
    local_logits = jax.vmap(lambda table, ids: table[:, ids.reshape(-1)])(logits, pair_nodes[:, 1])
    local_logits = local_logits.reshape(group_count, classes, group_count, -1)
    difference = local_logits - sent_logits
    return jnp.sum(cross_sum) + PAIR_WEIGHT * jnp.sum(difference * difference)

def renew(weight, momentum, average, gradient):
    momentum_new = MOMENTUM * momentum + gradient
    weight_new = weight - STEP_RATE * (gradient + MOMENTUM * momentum_new)
    average_new = AVERAGE_KEEP * average + (1.0 - AVERAGE_KEEP) * weight_new
    return (momentum_new, average_new, weight_new)

def reference(features, blocks, block_values, group_sizes, labels, pair_nodes, weight_first, weight_second, weight_head, norm_params, momentum_first, momentum_second, momentum_head, momentum_norms, average_first, average_second, average_head, average_norms):
    total_nodes = jnp.sum(group_sizes[:, 0]).astype(jnp.float32)
    weights = (weight_first, weight_second, weight_head, norm_params)

    def objective(params):
        return loss_of(params, features, blocks, block_values, group_sizes, labels, pair_nodes)
    loss_sum, pullback = jax.vjp(objective, weights)
    gradients = pullback(jnp.ones((), jnp.float32) / total_nodes)[0]
    first = renew(weight_first, momentum_first, average_first, gradients[0])
    second = renew(weight_second, momentum_second, average_second, gradients[1])
    head = renew(weight_head, momentum_head, average_head, gradients[2])
    norms = renew(norm_params, momentum_norms, average_norms, gradients[3])
    return (loss_sum, total_nodes, first[0], first[1], first[2], second[0], second[1], second[2], head[0], head[1], head[2], norms[0], norms[1], norms[2])
```

```python
import functools
import jax, jax.numpy as jnp
from jax import lax
from jax.experimental import pallas as pl
from jax.experimental.pallas import tpu as pltpu
BF=jnp.bfloat16; F32=jnp.float32; I32=jnp.int32
VLIM=60<<20
def dot(a,b): return jnp.dot(a,b,preferred_element_type=F32)
def dot_nt(a,b): return lax.dot_general(a,b,(((1,),(1,)),((),())),preferred_element_type=F32)
def split(x):
    h=x.astype(BF); return h,(x-h.astype(F32)).astype(BF)
GROUP=16

def make_lists(blk_l, blk_c, lb, NB, L):
    BLK=blk_l.shape[1]
    b_c=lax.broadcasted_iota(I32,(BLK,1),0); b_l=lax.broadcasted_iota(I32,(1,BLK),1)
    live=b_c<lb
    r_l=lax.broadcasted_iota(I32,(1,128),1)
    p_l=lax.broadcasted_iota(I32,(1,L),1)
    outs=[];counts=[]
    for k in range(2):
        kc=blk_c[:,k:k+1]; oc=blk_c[:,1-k:2-k]; kl=blk_l[k:k+1,:]
        before=jnp.where((kl==kc)&(b_l<b_c),1.0,0.0)
        rank=jnp.sum(before,axis=1,keepdims=True)
        cnt=jnp.sum(jnp.where((kc==r_l)&live,1.0,0.0),axis=0,keepdims=True)
        half=jnp.floor(cnt*0.5)
        pc=cnt+(cnt-2.0*half)
        start=jnp.sum(jnp.where(r_l<kc,pc,0.0),axis=1,keepdims=True)
        pos=jnp.where(live,(start+rank).astype(I32),-1)
        null=BLK+NB*(1<<20)
        enc=b_c+oc*(1<<12)+kc*(1<<20)-null
        lo=jnp.where(pos==p_l,(enc&0xfff).astype(F32),0.0); hi=jnp.where(pos==p_l,(enc>>12).astype(F32),0.0)
        lo=jnp.sum(lo,axis=0,keepdims=True).astype(I32); hi=jnp.sum(hi,axis=0,keepdims=True).astype(I32)
        outs.append(hi*4096+lo+null)
        counts.append(jnp.broadcast_to(jnp.sum(pc,axis=1,keepdims=True).astype(I32),(1,L)))
    return jnp.concatenate(outs+counts+[jnp.zeros((4,L),I32)],axis=0)

def pair_fields(lists, which, q):
    e0=lists[which,2*q]; e1=lists[which,2*q+1]
    return e0>>20, (e0>>12)&0xff, (e1>>12)&0xff, e0&0xfff, e1&0xfff

def agg_nodes(lists, which, S, v, acc):
    n=lists[2+which,0]//2
    def step(s,_):
        for u in range(GROUP):
            r,c0,c1,b0,b1=pair_fields(lists,which,s*GROUP+u)
            lhs=jnp.concatenate([S[b0],S[b1]],axis=1)
            rhs=jnp.concatenate([v[c0],v[c1]],axis=0)
            acc[r]+=dot(lhs,rhs)
        return 0
    lax.fori_loop(0,pl.cdiv(n,GROUP),step,0)

def k0(sizes, blk_l, blk_c, feat, vals, S_out, lists_out, fth_out, ftl_out, af_out,
       S, lists_v, lists_s, ft_v, fth, ftl, acc, af, buf, sem_in, sem_f, sem_l, sem_o, sem_S, CH, NBUF):
    nb=sizes[0]; lb=sizes[1]
    NB=acc.shape[0]-1; BLK=vals.shape[0]; FIN=feat.shape[0]
    L=lists_v.shape[1]
    nch=pl.cdiv(lb,CH)
    def chunk_in(i,slot): return pltpu.make_async_copy(vals.at[pl.ds(i*CH,CH)],buf.at[slot],sem_in.at[slot])
    def chunk_out(i): return pltpu.make_async_copy(S.at[pl.ds(i*CH,CH)],S_out.at[pl.ds(i*CH,CH)],sem_S.at[i])
    for i in range(NBUF):
        @pl.when(i<nch)
        def _(): chunk_in(i,i).start()
    cf=pltpu.make_async_copy(feat,ft_v,sem_f); cf.start()
    lists_v[...]=make_lists(blk_l[...],blk_c[...],lb,NB,L)
    cl=pltpu.make_async_copy(lists_v,lists_s,sem_l.at[0]); cl.start()
    co=pltpu.make_async_copy(lists_v,lists_out,sem_l.at[1]); co.start()
    S[BLK]=jnp.zeros((128,128),BF)
    acc[...]=jnp.zeros(acc.shape,F32)
    cf.wait()
    per=CH*NB//BLK
    def conv(i,_):
        slot=lax.rem(i,NBUF)
        chunk_in(i,slot).wait()
        for k in range(CH):
            S[i*CH+k]=buf[slot,k].T.astype(BF)
        for k in range(per):
            b=i*per+k
            x=ft_v[:,pl.ds(pl.multiple_of(b*128,128),128)]
            x=jnp.concatenate([x,jnp.zeros((128-FIN,128),F32)],axis=0).T
            h,l=split(x); fth[b]=h; ftl[b]=l
        @pl.when(i+NBUF<nch)
        def _(): chunk_in(i+NBUF,slot).start()
        chunk_out(i).start()
        return 0
    lax.fori_loop(0,nch,conv,0)
    c1=pltpu.make_async_copy(fth,fth_out,sem_o.at[0]); c1.start()
    c2=pltpu.make_async_copy(ftl,ftl_out,sem_o.at[1]); c2.start()
    cl.wait()
    agg_nodes(lists_s,0,S,fth,acc)
    def fin(b,_):
        af[b]=acc[b].astype(BF); return 0
    lax.fori_loop(0,nb,fin,0)
    c3=pltpu.make_async_copy(af,af_out,sem_o.at[2]); c3.start()
    lax.fori_loop(0,nch,lambda i,_:(chunk_out(i).wait(),0)[1],0)
    c1.wait();c2.wait();c3.wait();co.wait()

def call_k0(sizes, blk, feat, vals, CH=16, NBUF=12):
    FIN,N=feat.shape; NB=N//128; BLK=vals.shape[0]; L=pl.cdiv(BLK+NB,128)*128
    CH=min(CH,BLK)
    sds=jax.ShapeDtypeStruct
    ANY=pl.BlockSpec(memory_space=pl.ANY); VM=pl.BlockSpec(memory_space=pltpu.VMEM); SM=pl.BlockSpec(memory_space=pltpu.SMEM)
    return pl.pallas_call(functools.partial(k0,CH=CH,NBUF=NBUF),
        out_shape=(sds((BLK,128,128),BF),sds((8,L),I32),sds((NB,128,128),BF),sds((NB,128,128),BF),sds((NB,128,128),BF)),
        in_specs=[SM,VM,VM,ANY,ANY],out_specs=[ANY]*5,
        scratch_shapes=[pltpu.VMEM((BLK+1,128,128),BF),pltpu.VMEM((8,L),I32),pltpu.SMEM((8,L),I32),pltpu.VMEM((FIN,N),F32),
            pltpu.VMEM((NB,128,128),BF),pltpu.VMEM((NB,128,128),BF),pltpu.VMEM((NB+1,128,128),F32),pltpu.VMEM((NB,128,128),BF),
            pltpu.VMEM((NBUF,CH,128,128),F32),
            pltpu.SemaphoreType.DMA((NBUF,)),pltpu.SemaphoreType.DMA(()),pltpu.SemaphoreType.DMA((2,)),pltpu.SemaphoreType.DMA((3,)),pltpu.SemaphoreType.DMA((pl.cdiv(BLK,CH),))],
        compiler_params=pltpu.CompilerParams(vmem_limit_bytes=VLIM))(sizes,blk,blk.T,feat,vals)
G0=0.7978845608; G1=0.044715
EPS=1e-5
def for_blocks(nb,U,fn):
    full=nb//U
    def many(s,_): fn(s*U,U); return 0
    def one(b,_): fn(b,1); return 0
    lax.fori_loop(0,full,many,0)
    if U>1: lax.fori_loop(full*U,nb,one,0)
def rows8(x): return jnp.sum(x.reshape(x.shape[0]//8,8,x.shape[1]),axis=0)
def blk(ref,b0,U):
    x=ref[pl.ds(b0,U)]; return x.reshape(U*x.shape[1],x.shape[2])
def put_blk(ref,b0,U,x): ref[pl.ds(b0,U)]=x.reshape((U,)+ref.shape[1:])
def gelu(u):
    return (0.5*u)*(1.0+jnp.tanh(u*(G0+(G0*G1)*(u*u))))

def norm_stats(pre,nb,count,sums,st,row):
    mean=jnp.sum(sums[0],axis=0,keepdims=True)/count
    sums[1]=jnp.zeros_like(sums[1])
    def var(b0,U):
        x=blk(pre,b0,U)-mean
        sums[1]+=rows8(x*x)
    for_blocks(nb,4,var)
    v=jnp.sum(sums[1],axis=0,keepdims=True)/count
    inv=lax.rsqrt(v+EPS)
    st[row:row+1,:]=mean; st[row+1:row+2,:]=inv
    return mean,inv

def kb(sizes,lists,S_in,fth_in,ftl_in,af_in,w1,w2,wh,npar,pairs,
       h1h_out,h1l_out,ah_out,pre_out,st_out,h2t_out,lg_out,own_out,
       S,fth,ftl,af,h1h,h1l,acc,pre,zz,acc2,lg,h2t,sums,st,sem_i,sem_o):
    nb=sizes[0]; NB=fth.shape[0]; BLK=S_in.shape[0]; KC=lg.shape[1]; MY=h2t.shape[1]//2
    count=(nb*128).astype(F32)
    cs=[pltpu.make_async_copy(a,b,sem_i.at[i]) for i,(a,b) in enumerate(((fth_in,fth),(ftl_in,ftl),(af_in,af),(S_in,S.at[pl.ds(0,BLK)])))]
    for c in cs: c.start()
    S[BLK]=jnp.zeros((128,128),BF)
    sums[...]=jnp.zeros_like(sums)
    for c in cs[:3]: c.wait()
    def p1(b0,U):
        h=blk(fth,b0,U)
        x=jnp.concatenate([h,blk(ftl,b0,U),h,blk(af,b0,U)],axis=1)
        y=dot(x,w1[...])
        put_blk(pre,b0,U,y)
        sums[0]+=rows8(y)
    for_blocks(nb,4,p1)
    mean,inv=norm_stats(pre,nb,count,sums,st,0)
    a=npar[0:1,:]*inv; c=npar[1:2,:]-mean*a
    def n1(b0,U):
        h,l=split(gelu(blk(pre,b0,U)*a+c))
        put_blk(h1h,b0,U,h); put_blk(h1l,b0,U,l)
        put_blk(acc,b0,U,jnp.zeros((U*128,acc.shape[2]),F32))
    for_blocks(nb,4,n1)
    acc[NB]=jnp.zeros(acc.shape[1:],F32)
    oh=[pltpu.make_async_copy(h1h,h1h_out,sem_o.at[0]),pltpu.make_async_copy(h1l,h1l_out,sem_o.at[1])]
    for o in oh: o.start()
    cs[3].wait()
    agg_nodes(lists,0,S,h1h,acc)
    oa=pltpu.make_async_copy(acc.at[pl.ds(0,NB)],ah_out,sem_o.at[2]); oa.start()
    sums[...]=jnp.zeros_like(sums)
    def p2(b0,U):
        h=blk(h1h,b0,U); l=blk(h1l,b0,U); ah,al=split(blk(acc,b0,U))
        y=dot(jnp.concatenate([h,l,h,ah,al,ah],axis=1),w2[...])
        put_blk(pre,b0,U,y)
        sums[0]+=rows8(y)
    for_blocks(nb,2,p2)
    op=pltpu.make_async_copy(pre,pre_out,sem_o.at[3]); op.start()
    mean2,inv2=norm_stats(pre,nb,count,sums,st,2)
    a2=npar[2:3,:]*inv2; c2=npar[3:4,:]-mean2*a2
    def n2(b0,U):
        h,l=split(gelu(blk(pre,b0,U)*a2+c2))
        r=dot_nt(wh[...],h); r2=dot_nt(wh[0:KC,:],l)
        d=r[0:KC]+r[2*KC:3*KC]+r2
        zh,zl=split(r[KC:2*KC]+r[3*KC:4*KC])
        t=jnp.concatenate([h[:,:MY],l[:,:MY]],axis=1)
        for k in range(U):
            w=slice(k*128,k*128+128)
            lg[b0+k]=d[:,w]
            zz[b0+k]=jnp.concatenate([zh[:,w],zl[:,w]],axis=0)
            h2t[b0+k]=t[w].T
            acc2[b0+k]=jnp.zeros(acc2.shape[1:],F32)
    for_blocks(nb,2,n2)
    acc2[NB]=jnp.zeros(acc2.shape[1:],F32)
    ot=pltpu.make_async_copy(h2t,h2t_out,sem_o.at[4]); ot.start()
    agg_rows(lists,0,S,zz,acc2,True)
    own_out[...]=jnp.zeros_like(own_out)
    def fin(b0,U):
        parts=[]; hot=[]
        for k in range(U):
            x=acc2[b0+k]; y=lg[b0+k]+x[:KC]+x[KC:]; lg[b0+k]=y
            h,l=split(y); parts.append(jnp.concatenate([h,l],axis=0)); hot.append(one_hot(pairs,b0+k))
        r=dot_nt(jnp.concatenate(parts,axis=1),jnp.concatenate(hot,axis=1))
        own_out[...]+=r[:KC]+r[KC:]
    for_blocks(nb,4,fin)
    ol=pltpu.make_async_copy(lg,lg_out,sem_o.at[5]); ol.start()
    st_out[...]=st[...]
    for o in (*oh,oa,op,ot,ol): o.wait()

def one_hot(pairs,b):
    return jnp.where(pairs[...]==lax.broadcasted_iota(I32,(1,128),1)+b*128,1.0,0.0).astype(BF)

def agg_rows(lists,which,S,v,acc,nt):
    n=lists[2+which,0]//2
    def step(s,_):
        for u in range(GROUP):
            r,c0,c1,b0,b1=pair_fields(lists,which,s*GROUP+u)
            lhs=jnp.concatenate([v[c0],v[c1]],axis=1)
            if nt: acc[r]+=dot_nt(lhs,jnp.concatenate([S[b0],S[b1]],axis=1))
            else: acc[r]+=dot(lhs,jnp.concatenate([S[b0],S[b1]],axis=0))
        return 0
    lax.fori_loop(0,pl.cdiv(n,GROUP),step,0)

def call_kb(sizes,lists,S,fth,ftl,af,w1,w2,wh,npar,pairs,MY):
    NB=fth.shape[0]; BLK=S.shape[0]; H=w2.shape[1]; KC=wh.shape[0]//4
    sds=jax.ShapeDtypeStruct
    ANY=pl.BlockSpec(memory_space=pl.ANY); VM=pl.BlockSpec(memory_space=pltpu.VMEM); SM=pl.BlockSpec(memory_space=pltpu.SMEM)
    V=pltpu.VMEM
    return pl.pallas_call(kb,
        out_shape=(sds((NB,128,H),BF),sds((NB,128,H),BF),sds((NB,128,H),F32),sds((NB,128,H),F32),sds((8,H),F32),sds((NB,2*MY,128),BF),sds((NB,KC,128),F32),sds((KC,pairs.shape[0]),F32)),
        in_specs=[SM,SM]+[ANY]*4+[VM]*5,out_specs=[ANY]*4+[VM]+[ANY]*2+[VM],
        scratch_shapes=[V((BLK+1,128,128),BF)]+[V((NB,128,128),BF)]*3+[V((NB,128,H),BF)]*2+[V((NB+1,128,H),F32),V((NB,128,H),F32),
            V((NB,2*KC,128),BF),V((NB+1,2*KC,128),F32),V((NB,KC,128),F32),V((NB,2*MY,128),BF),V((2,8,H),F32),V((8,H),F32),
            pltpu.SemaphoreType.DMA((4,)),pltpu.SemaphoreType.DMA((6,))],
        compiler_params=pltpu.CompilerParams(vmem_limit_bytes=VLIM))(sizes,lists,S,fth,ftl,af,w1,w2,wh,npar,pairs)

def split_x(x):
    h=lax.reduce_precision(x,8,7); return h.astype(BF),(x-h).astype(BF)
def prep_weights(wf,ws,wh,npar,MY):
    FIN=wf.shape[1]; C=wh.shape[2]; CP=-(-C//16)*16
    def padk(w): return jnp.pad(w,((0,128-FIN),(0,0)))
    f0h,f0l=split_x(padk(wf[0])); f1h=padk(wf[1]).astype(BF)
    w1=jnp.concatenate([f0h,f0h,f0l,f1h],axis=0)
    (ah,al),(bh,bl)=split_x(ws[0]),split_x(ws[1])
    w2=jnp.concatenate([ah,ah,al,bh,bh,bl],axis=0)
    hp=jnp.pad(wh,((0,0),(0,0),(0,CP-C))).transpose(0,2,1)
    (ch,cl),(dh,dl)=split_x(hp[0]),split_x(hp[1])
    whc=jnp.concatenate([ch,dh,cl,dl],axis=0)
    n8=jnp.concatenate([npar.reshape(4,-1),jnp.zeros((4,npar.shape[2]),F32)],axis=0)
    m0h=f0h[:,:MY].T; m0l=f0l[:,:MY].T
    w1m=jnp.concatenate([m0h,m0h,m0l,f1h[:,:MY].T],axis=1)
    z=jnp.zeros((128-2*CP,hp.shape[2]),BF)
    th=jnp.concatenate([ch,dh,z],axis=0); tl=jnp.concatenate([cl,dl,z],axis=0)
    wt=jnp.concatenate([th,th,tl],axis=0)
    w2m=jnp.concatenate([ah[:MY],al[:MY],bh[:MY],bl[:MY]],axis=0)
    nc=n8[:,:MY].T
    return (w1,w2,whc,n8),(w1m,wt,w2m,n8,nc)
def dgelu(u):
    q=u*u
    t=jnp.tanh(u*(G0+(G0*G1)*q))
    return 0.5*(1.0+t)+(0.5*u)*(1.0-t*t)*(G0+(3.0*G0*G1)*q)

def kc(sizes,lists,S_in,fth_in,ftl_in,af_in,h1h_in,h1l_in,ah_in,pre_in,h2t_in,lg_in,st,own,recv,labels,pairs,w1m,wt,w2m,npar,ncol,
       g_out,
       S,fth,ftl,af,rh,rl,ra,pre,du,h2t,lg,gz,acc3,d0,t1,pre1,sums,cross,RH,RS,RL,R1,R2,colsum,sem_i,sem_r,CLS):
    nb=sizes[0]; BLK=S_in.shape[0]; NB=fth.shape[0]; CP=lg.shape[1]; MY=t1.shape[1]; P2=own.shape[1]; H=pre.shape[2]; NS=rh.shape[0]
    count=(nb*128).astype(F32); total=sizes[2].astype(F32)
    ins=((lg_in,lg),(S_in,S.at[pl.ds(0,BLK)]),(pre_in,pre),(h2t_in,h2t),(fth_in,fth),(ftl_in,ftl),(af_in,af))
    cs=[pltpu.make_async_copy(a,b,sem_i.at[i]) for i,(a,b) in enumerate(ins)]
    for c in cs: c.start()
    nch=pl.cdiv(nb,2)
    def ring(i):
        s=lax.rem(i,NS)
        return [pltpu.make_async_copy(a.at[pl.ds(i*2,2)],b.at[s],sem_r.at[s,k]) for k,(a,b) in enumerate(((h1h_in,rh),(h1l_in,rl),(ah_in,ra)))]
    for i in range(NS):
        @pl.when(i<nch)
        def _():
            for c in ring(i): c.start()
    S[BLK]=jnp.zeros((128,128),BF)
    for r in (sums,cross,RH,RS,RL,R1,R2,colsum): r[...]=jnp.zeros_like(r)
    acc3[NB]=jnp.zeros(acc3.shape[1:],F32)
    half=P2//2
    o=own[...]; r=recv[...]
    D=o-jnp.concatenate([r[:,half:],r[:,:half]],axis=1)
    pair_loss=0.5*jnp.sum(D[:,half:]*D[:,half:])
    Dh,Dl=split(D/total); D2=jnp.concatenate([Dh,Dl],axis=0)
    cs[0].wait()
    def soft(b0,U):
        hot=jnp.concatenate([one_hot(pairs,b0+k) for k in range(U)],axis=1)
        add=dot(D2,hot); add=add[:CP]+add[CP:]
        x=jnp.concatenate([lg[b0+k] for k in range(U)],axis=1)
        lab=jnp.concatenate([labels[b0+k] for k in range(U)],axis=1)
        row=lax.broadcasted_iota(I32,(CP,1),0)
        xm=jnp.where(row<CLS,x,-1e30)
        mx=jnp.max(xm,axis=0,keepdims=True)
        e=jnp.exp(xm-mx); s=jnp.sum(e,axis=0,keepdims=True)
        hit=jnp.where(row==lab,1.0,0.0)
        c=mx+jnp.log(s)-jnp.sum(hit*x,axis=0,keepdims=True)
        g=(e/s-hit)/total+add
        h,l=split(g)
        for k in range(U):
            w=slice(k*128,k*128+128)
            cross[...]+=c[:,w]
            lg[b0+k]=g[:,w]
            gz[b0+k]=jnp.concatenate([h[:,w],l[:,w]],axis=0)
            acc3[b0+k]=jnp.zeros(acc3.shape[1:],F32)
    for_blocks(nb,4,soft)
    cs[1].wait()
    agg_rows(lists,1,S,gz,acc3,False)
    for c in cs[2:]: c.wait()
    mean2=st[2:3,:]; inv2=st[3:4,:]
    gain2=npar[2:3,:]; a2=gain2*inv2; c2=npar[3:4,:]-mean2*a2
    def back2(b0,U):
        T=[];ads=[]
        for k in range(U):
            ad=acc3[b0+k]; ad=ad[:CP]+ad[CP:]
            T.append(jnp.concatenate([lg[b0+k],ad,jnp.zeros((128-2*CP,128),F32)],axis=0).T)
            ads.append(ad.astype(BF))
        th,tl=split(jnp.concatenate(T,axis=0))
        gh=dot(jnp.concatenate([th,tl,th],axis=1),wt[...])
        hh=jnp.concatenate([h2t[b0+k] for k in range(U)],axis=1)
        gg=jnp.concatenate([jnp.concatenate([gz[b0+k] for k in range(U)],axis=1),jnp.concatenate(ads,axis=1)],axis=0)
        RH[...]+=dot_nt(hh,gg)
        y=blk(pre,b0,U)
        d=gh*dgelu(y*a2+c2)
        put_blk(du,b0,U,d)
        sums[0]+=rows8(d); sums[1]+=rows8(d*((y-mean2)*inv2))
    for_blocks(nb,2,back2)
    sb2=jnp.sum(sums[0],axis=0,keepdims=True); sg2=jnp.sum(sums[1],axis=0,keepdims=True)
    A2=-a2*inv2*sg2/count; C2=-a2*sb2/count-A2*mean2
    def proj(b0,U):
        i=b0//2; s=lax.rem(i,NS)
        for c in ring(i): c.wait()
        gp=blk(du,b0,U)*a2+blk(pre,b0,U)*A2+C2
        h,l=split(gp)
        r=dot_nt(w2m[...],h); rl2=dot_nt(w2m[0:MY,:],l)
        d=r[:MY]+r[MY:2*MY]+rl2; t=(r[2*MY:3*MY]+r[3*MY:]).astype(BF)
        for k in range(U):
            w=slice(k*128,k*128+128)
            d0[b0+k]=d[:,w]; t1[b0+k]=t[:,w]
        gt=jnp.concatenate([h[:,:MY],l[:,:MY]],axis=1)
        gt=jnp.concatenate([gt[k*128:k*128+128].T for k in range(U)],axis=1)
        f=lambda ref: ref[s,0:U].reshape(U*128,H)
        ah,al=split(f(ra))
        RS[...]+=dot(gt,jnp.concatenate([f(rh),ah],axis=1))
        RL[...]+=dot(gt[:MY],jnp.concatenate([f(rl),al],axis=1))
        @pl.when(i+NS<nch)
        def _():
            for c in ring(i+NS): c.start()
    for_blocks(nb,2,proj)
    d0[NB]=jnp.zeros(d0.shape[1:],F32)
    agg_rows(lists,1,S,t1,d0,False)
    def pre_one(b0,U):
        h=blk(fth,b0,U)
        y=dot_nt(w1m[...],jnp.concatenate([h,blk(ftl,b0,U),h,blk(af,b0,U)],axis=1))
        for k in range(U):
            p=y[:,k*128:k*128+128]
            pre1[b0+k]=p; colsum[0]+=p
    for_blocks(nb,2,pre_one)
    lane=lambda x: jnp.sum(x,axis=1,keepdims=True)
    mean1=lane(colsum[0])/count
    def var1(b0,U):
        for k in range(U):
            p=pre1[b0+k]-mean1; colsum[1]+=p*p
    for_blocks(nb,4,var1)
    inv1=lax.rsqrt(lane(colsum[1])/count+EPS)
    a1=ncol[:,0:1]*inv1; c1=ncol[:,1:2]-mean1*a1
    def back1(b0,U):
        for k in range(U):
            p=pre1[b0+k]
            d=d0[b0+k]*dgelu(p*a1+c1)
            d0[b0+k]=d
            colsum[2]+=d; colsum[3]+=d*((p-mean1)*inv1)
    for_blocks(nb,4,back1)
    sb1=lane(colsum[2]); sg1=lane(colsum[3])
    A1=-a1*inv1*sg1/count; C1=-a1*sb1/count-A1*mean1
    def first(b0,U):
        h,l=split(jnp.concatenate([d0[b0+k]*a1+pre1[b0+k]*A1+C1 for k in range(U)],axis=1))
        R1[...]+=dot(jnp.concatenate([h,l],axis=0),blk(fth,b0,U))
        R2[...]+=dot(h,jnp.concatenate([blk(ftl,b0,U),blk(af,b0,U)],axis=1))
    for_blocks(nb,2,first)
    RSv=RS[...]; gs=RSv[:MY]+RSv[MY:]+RL[...]
    nh=2*H//128
    for k in range(nh): g_out[k*MY:(k+1)*MY,:]=gs[:,k*128:k*128+128]
    R1v=R1[...]; R2v=R2[...]
    q=nh*MY
    g_out[q:q+MY,:]=R1v[:MY]+R1v[MY:]+R2v[:,:128]
    g_out[q+MY:q+2*MY,:]=R2v[:,128:]
    RHv=RH[...]; gh=RHv[:MY]+RHv[MY:]
    gh=jnp.concatenate([RHv[:MY,:CP]+RHv[:MY,CP:2*CP]+RHv[MY:,:CP],gh[:,2*CP:3*CP],sg1,sb1,jnp.zeros((MY,128-2*CP-2),F32)],axis=1)
    g_out[q+2*MY:q+3*MY,:]=gh
    loss=jnp.sum(cross[...])+pair_loss
    tail=jnp.concatenate([jnp.concatenate([sg2[:,:MY],sb2[:,:MY]]+([jnp.zeros((1,128-2*MY),F32)] if MY<64 else []),axis=1),jnp.broadcast_to(loss,(1,128)),jnp.zeros((6,128),F32)],axis=0)
    g_out[q+3*MY:,:]=tail

def call_kc(sizes,lists,S,fth,ftl,af,h1h,h1l,ah,pre,h2t,lg,st,own,recv,labels,pairs,w1m,wt,w2m,npar,ncol,CLS):
    NB=fth.shape[0]; BLK=S.shape[0]; H=pre.shape[2]; CP=lg.shape[1]; MY=ncol.shape[0]; NS=min(8,NB//2)
    sds=jax.ShapeDtypeStruct
    ANY=pl.BlockSpec(memory_space=pl.ANY); VM=pl.BlockSpec(memory_space=pltpu.VMEM); SM=pl.BlockSpec(memory_space=pltpu.SMEM)
    V=pltpu.VMEM
    rows=2*H//128*MY+3*MY+8
    return pl.pallas_call(functools.partial(kc,CLS=CLS),out_shape=sds((rows,128),F32),
        in_specs=[SM,SM]+[ANY]*10+[VM]*10,out_specs=VM,
        scratch_shapes=[V((BLK+1,128,128),BF)]+[V((NB,128,128),BF)]*3+[V((NS,2,128,H),BF)]*2+[V((NS,2,128,H),F32),
            V((NB,128,H),F32),V((NB,128,H),F32),V((NB,2*MY,128),BF),V((NB,CP,128),F32),V((NB,2*CP,128),BF),V((NB+1,2*CP,128),F32),
            V((NB+1,MY,128),F32),V((NB,MY,128),BF),V((NB,MY,128),F32),
            V((2,8,H),F32),V((1,128),F32),V((2*MY,3*CP),F32),V((2*MY,2*H),F32),V((MY,2*H),F32),V((2*MY,128),F32),V((MY,256),F32),V((4,MY,128),F32),
            pltpu.SemaphoreType.DMA((7,)),pltpu.SemaphoreType.DMA((NS,3))],
        compiler_params=pltpu.CompilerParams(vmem_limit_bytes=VLIM))(sizes,lists,S,fth,ftl,af,h1h,h1l,ah,pre,h2t,lg,st,own,recv,labels,pairs,w1m,wt,w2m,npar,ncol)

MOMENTUM=0.9; STEP_RATE=2.0; AVERAGE_KEEP=0.9

def renew(weight, momentum, average, gradient):
    momentum_new = MOMENTUM * momentum + gradient
    weight_new = weight - STEP_RATE * (gradient + MOMENTUM * momentum_new)
    average_new = AVERAGE_KEEP * average + (1.0 - AVERAGE_KEEP) * weight_new
    return momentum_new, average_new, weight_new

def turn(x, axis, by):
    return lax.dynamic_slice_in_dim(jnp.concatenate([x,x],axis=axis),by,x.shape[axis],axis)

def per_device(n_col, features, blocks, block_values, group_sizes, labels, pair_nodes, weight_first, weight_second, weight_head,
               norm_params, momentum_first, momentum_second, momentum_head, momentum_norms, average_first, average_second,
               average_head, average_norms):
    col=lax.axis_index("col")
    MY=weight_first.shape[2]; H=MY*n_col; FIN=weight_first.shape[1]; CLS=weight_head.shape[2]; CP=-(-CLS//16)*16
    G=group_sizes.shape[0]; N=features.shape[2]; NB=N//128
    shards=(weight_first,weight_second,weight_head,norm_params)
    flat=jnp.concatenate([x.reshape(-1) for x in shards])
    parts=[flat]+[lax.ppermute(flat,"col",[((j+k)%n_col,j) for j in range(n_col)]) for k in range(1,n_col)]
    own_sizes=lax.dynamic_slice_in_dim(group_sizes,lax.axis_index("graph"),1,0)[0]
    total=jnp.sum(group_sizes[:,0])
    sizes=jnp.stack([own_sizes[0]//128,own_sizes[1],total])
    S,lists,fth,ftl,af=call_k0(sizes,blocks[0],features[0],block_values[0])
    def whole(i,axis):
        start=sum(x.size for x in shards[:i]); x=shards[i]
        return jnp.concatenate([p[start:start+x.size].reshape(x.shape) for p in parts],axis=axis)
    wf=whole(0,2); ws=turn(whole(1,2),1,col*MY); wh=whole(2,1); npar=whole(3,2)
    wb,wc=prep_weights(wf,ws,wh,npar,MY)
    pairs=pair_nodes[0].reshape(-1,1)
    h1h,h1l,ah,pre,st,h2t,lg,own=call_kb(sizes,lists,S,fth,ftl,af,*wb,pairs,MY=MY)
    P2=own.shape[1]
    recv=lax.all_to_all(own.reshape(CP,2,G,P2//2//G),"graph",split_axis=2,concat_axis=2,tiled=True).reshape(CP,P2)
    g=call_kc(sizes,lists,S,fth,ftl,af,h1h,h1l,ah,pre,h2t,lg,st,own,recv,labels[0].reshape(NB,1,128),pairs,*wc,CLS=CLS)
    g=lax.psum(g,"graph")
    nh=2*H//128; q=nh*MY
    gs=g[:q].reshape(2,H//128,MY,128).transpose(0,1,3,2).reshape(2,H,MY)
    gs=turn(gs,1,(n_col-col)%n_col*MY)
    gf=g[q:q+2*MY].reshape(2,MY,128)[:,:,:FIN].transpose(0,2,1)
    hd=g[q+2*MY:q+3*MY]; tail=g[q+3*MY:]
    gh=jnp.stack([hd[:,:CLS],hd[:,CP:CP+CLS]])
    gn=jnp.stack([hd[:,2*CP:2*CP+2].T,tail[0,:2*MY].reshape(2,MY)])
    first=renew(weight_first,momentum_first,average_first,gf)
    second=renew(weight_second,momentum_second,average_second,gs)
    head=renew(weight_head,momentum_head,average_head,gh)
    norms=renew(norm_params,momentum_norms,average_norms,gn)
    return (tail[1,0],total.astype(F32),*first,*second,*head,*norms)

def solution(mesh):
    P=jax.sharding.PartitionSpec
    unit=P(None,None,"col"); head=P(None,"col",None)
    weights=(unit,unit,head,unit)
    in_specs=(P("graph",None,None),P("graph",None,None),P("graph",None,None,None),P(),P("graph",None),P("graph",None,None,None))+weights*3
    out_specs=(P(),P())+(unit,)*6+(head,)*3+(unit,)*3
    return jax.shard_map(functools.partial(per_device,mesh.shape["col"]),mesh=mesh,in_specs=in_specs,out_specs=out_specs,check_vma=False)
```

```python
import functools
import jax, jax.numpy as jnp
from jax import lax
from jax.experimental import pallas as pl
from jax.experimental.pallas import tpu as pltpu
BF=jnp.bfloat16; F32=jnp.float32; I32=jnp.int32
VLIM=60<<20
def dot(a,b): return jnp.dot(a,b,preferred_element_type=F32)
def dot_nt(a,b): return lax.dot_general(a,b,(((1,),(1,)),((),())),preferred_element_type=F32)
def split(x):
    h=x.astype(BF); return h,(x-h.astype(F32)).astype(BF)
GROUP=16

def my_sizes(sizes):
    me=lax.axis_index("graph")
    total=sizes[0,0]
    for g in range(1,sizes.shape[1]): total+=sizes[0,g]
    return sizes[0,me]>>7, sizes[1,me], total

def make_lists(blk_l, blk_c, lb, NB, L):
    BLK=blk_l.shape[1]
    b_c=lax.broadcasted_iota(I32,(BLK,1),0); b_l=lax.broadcasted_iota(I32,(1,BLK),1)
    live=b_c<lb
    r_l=lax.broadcasted_iota(I32,(1,128),1)
    p_l=lax.broadcasted_iota(I32,(1,L),1)
    outs=[];counts=[]
    for k in range(2):
        kc=blk_c[:,k:k+1]; oc=blk_c[:,1-k:2-k]; kl=blk_l[k:k+1,:]
        before=jnp.where((kl==kc)&(b_l<b_c),1.0,0.0)
        rank=jnp.sum(before,axis=1,keepdims=True)
        cnt=jnp.sum(jnp.where((kc==r_l)&live,1.0,0.0),axis=0,keepdims=True)
        half=jnp.floor(cnt*0.5)
        pc=cnt+(cnt-2.0*half)
        start=jnp.sum(jnp.where(r_l<kc,pc,0.0),axis=1,keepdims=True)
        pos=jnp.where(live,(start+rank).astype(I32),-1)
        null=BLK+NB*(1<<20)
        enc=b_c+oc*(1<<12)+kc*(1<<20)-null
        lo=jnp.where(pos==p_l,(enc&0xfff).astype(F32),0.0); hi=jnp.where(pos==p_l,(enc>>12).astype(F32),0.0)
        lo=jnp.sum(lo,axis=0,keepdims=True).astype(I32); hi=jnp.sum(hi,axis=0,keepdims=True).astype(I32)
        outs.append(hi*4096+lo+null)
        counts.append(jnp.broadcast_to(jnp.sum(pc,axis=1,keepdims=True).astype(I32),(1,L)))
    return jnp.concatenate(outs+counts+[jnp.zeros((4,L),I32)],axis=0)

def pair_fields(lists, which, q):
    e0=lists[which,2*q]; e1=lists[which,2*q+1]
    return e0>>20, (e0>>12)&0xff, (e1>>12)&0xff, e0&0xfff, e1&0xfff

def agg_nodes(lists, which, S, v, acc):
    n=lists[2+which,0]//2
    def step(s,_):
        for u in range(GROUP):
            r,c0,c1,b0,b1=pair_fields(lists,which,s*GROUP+u)
            lhs=jnp.concatenate([S[b0],S[b1]],axis=1)
            rhs=jnp.concatenate([v[c0],v[c1]],axis=0)
            acc[r]+=dot(lhs,rhs)
        return 0
    lax.fori_loop(0,pl.cdiv(n,GROUP),step,0)

def k0(sizes, blk_l, feat, vals, S_out, lists_out, fth_out, ftl_out, af_out,
       S, lists_v, lists_s, ft_v, fth, ftl, acc, af, buf, sem_in, sem_f, sem_l, sem_o, sem_S, CH, NBUF):
    nb,lb,_=my_sizes(sizes)
    NB=acc.shape[0]-1; BLK=vals.shape[0]; FIN=feat.shape[0]
    L=lists_v.shape[1]
    nch=pl.cdiv(lb,CH)
    def chunk_in(i,slot): return pltpu.make_async_copy(vals.at[pl.ds(i*CH,CH)],buf.at[slot],sem_in.at[slot])
    def chunk_out(i): return pltpu.make_async_copy(S.at[pl.ds(i*CH,CH)],S_out.at[pl.ds(i*CH,CH)],sem_S.at[i])
    for i in range(NBUF):
        @pl.when(i<nch)
        def _(): chunk_in(i,i).start()
    cf=pltpu.make_async_copy(feat.at[:,0],ft_v,sem_f); cf.start()
    ids=blk_l[...]
    columns=jnp.concatenate([ids.astype(F32),jnp.zeros((6,BLK),F32)],axis=0).T.astype(I32)
    lists_v[...]=make_lists(ids,columns,lb,NB,L)
    cl=pltpu.make_async_copy(lists_v,lists_s,sem_l.at[0]); cl.start()
    co=pltpu.make_async_copy(lists_v,lists_out,sem_l.at[1]); co.start()
    S[BLK]=jnp.zeros((128,128),BF)
    acc[...]=jnp.zeros(acc.shape,F32)
    cf.wait()
    per=CH*NB//BLK
    def conv(i,_):
        slot=lax.rem(i,NBUF)
        chunk_in(i,slot).wait()
        for k in range(CH):
            S[i*CH+k]=buf[slot,k].T.astype(BF)
        for k in range(per):
            b=i*per+k
            x=ft_v[:,pl.ds(pl.multiple_of(b*128,128),128)]
            x=jnp.concatenate([x,jnp.zeros((128-FIN,128),F32)],axis=0).T
            h,l=split(x); fth[b]=h; ftl[b]=l
        @pl.when(i+NBUF<nch)
        def _(): chunk_in(i+NBUF,slot).start()
        chunk_out(i).start()
        return 0
    lax.fori_loop(0,nch,conv,0)
    c1=pltpu.make_async_copy(fth,fth_out,sem_o.at[0]); c1.start()
    c2=pltpu.make_async_copy(ftl,ftl_out,sem_o.at[1]); c2.start()
    cl.wait()
    agg_nodes(lists_s,0,S,fth,acc)
    def fin(b,_):
        af[b]=acc[b].astype(BF); return 0
    lax.fori_loop(0,nb,fin,0)
    c3=pltpu.make_async_copy(af,af_out,sem_o.at[2]); c3.start()
    lax.fori_loop(0,nch,lambda i,_:(chunk_out(i).wait(),0)[1],0)
    c1.wait();c2.wait();c3.wait();co.wait()

def call_k0(sizes, blk, feat, vals, CH=16, NBUF=12):
    FIN,_,N=feat.shape; NB=N//128; BLK=vals.shape[0]; L=pl.cdiv(BLK+NB,128)*128
    CH=min(CH,BLK)
    sds=jax.ShapeDtypeStruct
    ANY=pl.BlockSpec(memory_space=pl.ANY); VM=pl.BlockSpec(memory_space=pltpu.VMEM); SM=pl.BlockSpec(memory_space=pltpu.SMEM)
    return pl.pallas_call(functools.partial(k0,CH=CH,NBUF=NBUF),
        out_shape=(sds((BLK,128,128),BF),sds((8,L),I32),sds((NB,128,128),BF),sds((NB,128,128),BF),sds((NB,128,128),BF)),
        in_specs=[SM,VM,ANY,ANY],out_specs=[ANY]*5,
        scratch_shapes=[pltpu.VMEM((BLK+1,128,128),BF),pltpu.VMEM((8,L),I32),pltpu.SMEM((8,L),I32),pltpu.VMEM((FIN,N),F32),
            pltpu.VMEM((NB,128,128),BF),pltpu.VMEM((NB,128,128),BF),pltpu.VMEM((NB+1,128,128),F32),pltpu.VMEM((NB,128,128),BF),
            pltpu.VMEM((NBUF,CH,128,128),F32),
            pltpu.SemaphoreType.DMA((NBUF,)),pltpu.SemaphoreType.DMA(()),pltpu.SemaphoreType.DMA((2,)),pltpu.SemaphoreType.DMA((3,)),pltpu.SemaphoreType.DMA((pl.cdiv(BLK,CH),))],
        compiler_params=pltpu.CompilerParams(vmem_limit_bytes=VLIM))(sizes,blk,feat,vals)
G0=0.7978845608; G1=0.044715
EPS=1e-5
def for_blocks(nb,U,fn):
    full=nb//U
    def many(s,_): fn(s*U,U); return 0
    def one(b,_): fn(b,1); return 0
    lax.fori_loop(0,full,many,0)
    if U>1: lax.fori_loop(full*U,nb,one,0)
def rows8(x): return jnp.sum(x.reshape(x.shape[0]//8,8,x.shape[1]),axis=0)
def blk(ref,b0,U):
    x=ref[pl.ds(b0,U)]; return x.reshape(U*x.shape[1],x.shape[2])
def put_blk(ref,b0,U,x): ref[pl.ds(b0,U)]=x.reshape((U,)+ref.shape[1:])
def gelu(u):
    return (0.5*u)*(1.0+jnp.tanh(u*(G0+(G0*G1)*(u*u))))

def norm_stats(pre,nb,count,sums,st,row):
    mean=jnp.sum(sums[0],axis=0,keepdims=True)/count
    sums[1]=jnp.zeros_like(sums[1])
    def var(b0,U):
        x=blk(pre,b0,U)-mean
        sums[1]+=rows8(x*x)
    for_blocks(nb,4,var)
    v=jnp.sum(sums[1],axis=0,keepdims=True)/count
    inv=lax.rsqrt(v+EPS)
    st[row:row+1,:]=mean; st[row+1:row+2,:]=inv
    return mean,inv

def kb(sizes,lists,S_in,fth_in,ftl_in,af_in,w1,w2,wh,npar,pairs,
       h1h_out,h1l_out,ah_out,pre_out,st_out,h2t_out,lg_out,own_out,
       S,fth,ftl,af,h1h,h1l,acc,pre,zz,acc2,lg,h2t,sums,st,sem_i,sem_o):
    nb,_,_=my_sizes(sizes); NB=fth.shape[0]; BLK=S_in.shape[0]; KC=lg.shape[1]; MY=h2t.shape[1]//2
    count=(nb*128).astype(F32)
    cs=[pltpu.make_async_copy(a,b,sem_i.at[i]) for i,(a,b) in enumerate(((fth_in,fth),(ftl_in,ftl),(af_in,af),(S_in,S.at[pl.ds(0,BLK)])))]
    for c in cs: c.start()
    S[BLK]=jnp.zeros((128,128),BF)
    sums[...]=jnp.zeros_like(sums)
    for c in cs[:3]: c.wait()
    def p1(b0,U):
        h=blk(fth,b0,U)
        x=jnp.concatenate([h,blk(ftl,b0,U),h,blk(af,b0,U)],axis=1)
        y=dot_nt(x,w1[...])
        put_blk(pre,b0,U,y)
        sums[0]+=rows8(y)
    for_blocks(nb,4,p1)
    mean,inv=norm_stats(pre,nb,count,sums,st,0)
    a=npar[0:1,:]*inv; c=npar[1:2,:]-mean*a
    def n1(b0,U):
        h,l=split(gelu(blk(pre,b0,U)*a+c))
        put_blk(h1h,b0,U,h); put_blk(h1l,b0,U,l)
        put_blk(acc,b0,U,jnp.zeros((U*128,acc.shape[2]),F32))
    for_blocks(nb,4,n1)
    acc[NB]=jnp.zeros(acc.shape[1:],F32)
    oh=[pltpu.make_async_copy(h1h,h1h_out,sem_o.at[0]),pltpu.make_async_copy(h1l,h1l_out,sem_o.at[1])]
    for o in oh: o.start()
    cs[3].wait()
    agg_nodes(lists,0,S,h1h,acc)
    oa=pltpu.make_async_copy(acc.at[pl.ds(0,NB)],ah_out,sem_o.at[2]); oa.start()
    sums[...]=jnp.zeros_like(sums)
    def p2(b0,U):
        h=blk(h1h,b0,U); l=blk(h1l,b0,U); ah,al=split(blk(acc,b0,U))
        y=dot_nt(jnp.concatenate([h,l,h,ah,al,ah],axis=1),w2[...])
        put_blk(pre,b0,U,y)
        sums[0]+=rows8(y)
    for_blocks(nb,2,p2)
    op=pltpu.make_async_copy(pre,pre_out,sem_o.at[3]); op.start()
    mean2,inv2=norm_stats(pre,nb,count,sums,st,2)
    a2=npar[2:3,:]*inv2; c2=npar[3:4,:]-mean2*a2
    def n2(b0,U):
        h,l=split(gelu(blk(pre,b0,U)*a2+c2))
        r=dot_nt(wh[...],h); r2=dot_nt(wh[0:KC,:],l)
        d=r[0:KC]+r[2*KC:3*KC]+r2
        zh,zl=split(r[KC:2*KC]+r[3*KC:4*KC])
        t=jnp.concatenate([h[:,:MY],l[:,:MY]],axis=1)
        for k in range(U):
            w=slice(k*128,k*128+128)
            lg[b0+k]=d[:,w]
            zz[b0+k]=jnp.concatenate([zh[:,w],zl[:,w]],axis=0)
            h2t[b0+k]=t[w].T
            acc2[b0+k]=jnp.zeros(acc2.shape[1:],F32)
    for_blocks(nb,2,n2)
    acc2[NB]=jnp.zeros(acc2.shape[1:],F32)
    ot=pltpu.make_async_copy(h2t,h2t_out,sem_o.at[4]); ot.start()
    agg_rows(lists,0,S,zz,acc2,True)
    own_out[...]=jnp.zeros_like(own_out)
    slots=slot_nodes(pairs)
    def fin(b0,U):
        parts=[]; hot=[]
        for k in range(U):
            x=acc2[b0+k]; y=lg[b0+k]+x[:KC]+x[KC:]; lg[b0+k]=y
            h,l=split(y); parts.append(jnp.concatenate([h,l],axis=0)); hot.append(one_hot(slots,b0+k))
        r=dot_nt(jnp.concatenate(hot,axis=1),jnp.concatenate(parts,axis=1))
        own_out[:,:KC]+=r[:,:KC]+r[:,KC:]
    for_blocks(nb,4,fin)
    ol=pltpu.make_async_copy(lg,lg_out,sem_o.at[5]); ol.start()
    st_out[...]=st[...]
    for o in (*oh,oa,op,ot,ol): o.wait()

def slot_nodes(pairs):
    R,K=pairs.shape; G=R//2
    x=jnp.concatenate([pairs[...].astype(F32),jnp.zeros((R,128-K),F32)],axis=1)
    if R%128: x=jnp.concatenate([x,jnp.zeros((128-R%128,128),F32)],axis=0)
    x=x.T[:K].astype(I32)
    return jnp.concatenate([x[:,t*G+g:t*G+g+1] for g in range(G) for t in range(2)],axis=0)
def one_hot(slots,b):
    return jnp.where(slots==lax.broadcasted_iota(I32,(1,128),1)+b*128,1.0,0.0).astype(BF)

def agg_rows(lists,which,S,v,acc,nt):
    n=lists[2+which,0]//2
    def step(s,_):
        for u in range(GROUP):
            r,c0,c1,b0,b1=pair_fields(lists,which,s*GROUP+u)
            lhs=jnp.concatenate([v[c0],v[c1]],axis=1)
            if nt: acc[r]+=dot_nt(lhs,jnp.concatenate([S[b0],S[b1]],axis=1))
            else: acc[r]+=dot(lhs,jnp.concatenate([S[b0],S[b1]],axis=0))
        return 0
    lax.fori_loop(0,pl.cdiv(n,GROUP),step,0)

def call_kb(sizes,lists,S,fth,ftl,af,w1,w2,wh,npar,pairs,MY):
    NB=fth.shape[0]; BLK=S.shape[0]; H=w2.shape[0]; KC=wh.shape[0]//4
    sds=jax.ShapeDtypeStruct
    ANY=pl.BlockSpec(memory_space=pl.ANY); VM=pl.BlockSpec(memory_space=pltpu.VMEM); SM=pl.BlockSpec(memory_space=pltpu.SMEM)
    V=pltpu.VMEM
    return pl.pallas_call(kb,
        out_shape=(sds((NB,128,H),BF),sds((NB,128,H),BF),sds((NB,128,H),F32),sds((NB,128,H),F32),sds((8,H),F32),sds((NB,2*MY,128),BF),sds((NB,KC,128),F32),sds((pairs.size,128),F32)),
        in_specs=[SM,SM]+[ANY]*4+[VM]*5,out_specs=[ANY]*4+[VM]+[ANY]*2+[VM],
        scratch_shapes=[V((BLK+1,128,128),BF)]+[V((NB,128,128),BF)]*3+[V((NB,128,H),BF)]*2+[V((NB+1,128,H),F32),V((NB,128,H),F32),
            V((NB,2*KC,128),BF),V((NB+1,2*KC,128),F32),V((NB,KC,128),F32),V((NB,2*MY,128),BF),V((2,8,H),F32),V((8,H),F32),
            pltpu.SemaphoreType.DMA((4,)),pltpu.SemaphoreType.DMA((6,))],
        compiler_params=pltpu.CompilerParams(vmem_limit_bytes=VLIM))(sizes,lists,S,fth,ftl,af,w1,w2,wh,npar,pairs)

def dgelu(u):
    q=u*u
    t=jnp.tanh(u*(G0+(G0*G1)*q))
    return 0.5*(1.0+t)+(0.5*u)*(1.0-t*t)*(G0+(3.0*G0*G1)*q)

def kc(sizes,lists,S_in,fth_in,ftl_in,af_in,h1h_in,h1l_in,ah_in,pre_in,h2t_in,lg_in,st,own,recv,labels,pairs,w1m,wt,w2m,npar,ncol,
       g_out,
       S,fth,ftl,af,rh,rl,ra,pre,du,h2t,lg,gz,acc3,d0,t1,pre1,sums,cross,RH,RS,RL,R1,R2,colsum,sem_i,sem_r,CLS):
    nb,_,nodes=my_sizes(sizes); BLK=S_in.shape[0]; NB=fth.shape[0]; CP=lg.shape[1]; MY=t1.shape[1]; H=pre.shape[2]; NS=rh.shape[0]
    count=(nb*128).astype(F32); total=nodes.astype(F32)
    ins=((lg_in,lg),(S_in,S.at[pl.ds(0,BLK)]),(pre_in,pre),(h2t_in,h2t),(fth_in,fth),(ftl_in,ftl),(af_in,af))
    cs=[pltpu.make_async_copy(a,b,sem_i.at[i]) for i,(a,b) in enumerate(ins)]
    for c in cs: c.start()
    nch=pl.cdiv(nb,2)
    def ring(i):
        s=lax.rem(i,NS)
        return [pltpu.make_async_copy(a.at[pl.ds(i*2,2)],b.at[s],sem_r.at[s,k]) for k,(a,b) in enumerate(((h1h_in,rh),(h1l_in,rl),(ah_in,ra)))]
    for i in range(NS):
        @pl.when(i<nch)
        def _():
            for c in ring(i): c.start()
    S[BLK]=jnp.zeros((128,128),BF)
    for r in (sums,cross,RH,RS,RL,R1,R2,colsum): r[...]=jnp.zeros_like(r)
    acc3[NB]=jnp.zeros(acc3.shape[1:],F32)
    half=pairs.shape[1]
    G=pairs.shape[0]//2
    r=recv[...]
    D=own[...].reshape(G,2*half,128)-jnp.concatenate([r[:,half:],r[:,:half]],axis=1)
    pair_loss=0.5*jnp.sum(D[:,half:]*D[:,half:])
    Dh,Dl=split((D.reshape(2*G*half,128).T)[:CP]/total); D2=jnp.concatenate([Dh,Dl],axis=0)
    slots=slot_nodes(pairs)
    cs[0].wait()
    def soft(b0,U):
        hot=jnp.concatenate([one_hot(slots,b0+k) for k in range(U)],axis=1)
        add=dot(D2,hot); add=add[:CP]+add[CP:]
        x=jnp.concatenate([lg[b0+k] for k in range(U)],axis=1)
        lab=jnp.concatenate([labels[b0+k] for k in range(U)],axis=1)
        row=lax.broadcasted_iota(I32,(CP,1),0)
        xm=jnp.where(row<CLS,x,-1e30)
        mx=jnp.max(xm,axis=0,keepdims=True)
        e=jnp.exp(xm-mx); s=jnp.sum(e,axis=0,keepdims=True)
        hit=jnp.where(row==lab,1.0,0.0)
        c=mx+jnp.log(s)-jnp.sum(hit*x,axis=0,keepdims=True)
        g=(e/s-hit)/total+add
        h,l=split(g)
        for k in range(U):
            w=slice(k*128,k*128+128)
            cross[...]+=c[:,w]
            lg[b0+k]=g[:,w]
            gz[b0+k]=jnp.concatenate([h[:,w],l[:,w]],axis=0)
            acc3[b0+k]=jnp.zeros(acc3.shape[1:],F32)
    for_blocks(nb,4,soft)
    cs[1].wait()
    agg_rows(lists,1,S,gz,acc3,False)
    for c in cs[2:]: c.wait()
    mean2=st[2:3,:]; inv2=st[3:4,:]
    gain2=npar[2:3,:]; a2=gain2*inv2; c2=npar[3:4,:]-mean2*a2
    def back2(b0,U):
        T=[];ads=[]
        for k in range(U):
            ad=acc3[b0+k]; ad=ad[:CP]+ad[CP:]
            T.append(jnp.concatenate([lg[b0+k],ad,jnp.zeros((128-2*CP,128),F32)],axis=0).T)
            ads.append(ad.astype(BF))
        th,tl=split(jnp.concatenate(T,axis=0))
        gh=dot(jnp.concatenate([th,tl,th],axis=1),wt[...])
        hh=jnp.concatenate([h2t[b0+k] for k in range(U)],axis=1)
        gg=jnp.concatenate([jnp.concatenate([gz[b0+k] for k in range(U)],axis=1),jnp.concatenate(ads,axis=1)],axis=0)
        RH[...]+=dot_nt(hh,gg)
        y=blk(pre,b0,U)
        d=gh*dgelu(y*a2+c2)
        put_blk(du,b0,U,d)
        sums[0]+=rows8(d); sums[1]+=rows8(d*((y-mean2)*inv2))
    for_blocks(nb,2,back2)
    sb2=jnp.sum(sums[0],axis=0,keepdims=True); sg2=jnp.sum(sums[1],axis=0,keepdims=True)
    A2=-a2*inv2*sg2/count; C2=-a2*sb2/count-A2*mean2
    def proj(b0,U):
        i=b0//2; s=lax.rem(i,NS)
        for c in ring(i): c.wait()
        gp=blk(du,b0,U)*a2+blk(pre,b0,U)*A2+C2
        h,l=split(gp)
        r=dot_nt(w2m[...],h); rl2=dot_nt(w2m[0:MY,:],l)
        d=r[:MY]+r[MY:2*MY]+rl2; t=(r[2*MY:3*MY]+r[3*MY:]).astype(BF)
        for k in range(U):
            w=slice(k*128,k*128+128)
            d0[b0+k]=d[:,w]; t1[b0+k]=t[:,w]
        gt=jnp.concatenate([h[:,:MY],l[:,:MY]],axis=1)
        gt=jnp.concatenate([gt[k*128:k*128+128].T for k in range(U)],axis=1)
        f=lambda ref: ref[s,0:U].reshape(U*128,H)
        ah,al=split(f(ra))
        RS[...]+=dot(gt,jnp.concatenate([f(rh),ah],axis=1))
        RL[...]+=dot(gt[:MY],jnp.concatenate([f(rl),al],axis=1))
        @pl.when(i+NS<nch)
        def _():
            for c in ring(i+NS): c.start()
    for_blocks(nb,2,proj)
    d0[NB]=jnp.zeros(d0.shape[1:],F32)
    agg_rows(lists,1,S,t1,d0,False)
    def pre_one(b0,U):
        h=blk(fth,b0,U)
        y=dot_nt(w1m[0:MY,:],jnp.concatenate([h,blk(ftl,b0,U),h,blk(af,b0,U)],axis=1))
        for k in range(U):
            p=y[:,k*128:k*128+128]
            pre1[b0+k]=p; colsum[0]+=p
    for_blocks(nb,2,pre_one)
    lane=lambda x: jnp.sum(x,axis=1,keepdims=True)
    mean1=lane(colsum[0])/count
    def var1(b0,U):
        for k in range(U):
            p=pre1[b0+k]-mean1; colsum[1]+=p*p
    for_blocks(nb,4,var1)
    inv1=lax.rsqrt(lane(colsum[1])/count+EPS)
    a1=ncol[:,0:1]*inv1; c1=ncol[:,1:2]-mean1*a1
    def back1(b0,U):
        for k in range(U):
            p=pre1[b0+k]
            d=d0[b0+k]*dgelu(p*a1+c1)
            d0[b0+k]=d
            colsum[2]+=d; colsum[3]+=d*((p-mean1)*inv1)
    for_blocks(nb,4,back1)
    sb1=lane(colsum[2]); sg1=lane(colsum[3])
    A1=-a1*inv1*sg1/count; C1=-a1*sb1/count-A1*mean1
    def first(b0,U):
        h,l=split(jnp.concatenate([d0[b0+k]*a1+pre1[b0+k]*A1+C1 for k in range(U)],axis=1))
        R1[...]+=dot(jnp.concatenate([h,l],axis=0),blk(fth,b0,U))
        R2[...]+=dot(h,jnp.concatenate([blk(ftl,b0,U),blk(af,b0,U)],axis=1))
    for_blocks(nb,2,first)
    RSv=RS[...]; gs=RSv[:MY]+RSv[MY:]+RL[...]
    nh=2*H//128
    for k in range(nh): g_out[k*MY:(k+1)*MY,:]=gs[:,k*128:k*128+128]
    R1v=R1[...]; R2v=R2[...]
    q=nh*MY
    g_out[q:q+MY,:]=R1v[:MY]+R1v[MY:]+R2v[:,:128]
    g_out[q+MY:q+2*MY,:]=R2v[:,128:]
    RHv=RH[...]; gh=RHv[:MY]+RHv[MY:]
    gh=jnp.concatenate([RHv[:MY,:CP]+RHv[:MY,CP:2*CP]+RHv[MY:,:CP],gh[:,2*CP:3*CP],sg1,sb1,jnp.zeros((MY,128-2*CP-2),F32)],axis=1)
    g_out[q+2*MY:q+3*MY,:]=gh
    loss=jnp.sum(cross[...])+pair_loss
    pad=[jnp.zeros((1,128-MY),F32)]
    g_out[q+3*MY:,:]=jnp.zeros((g_out.shape[0]-q-3*MY,128),F32)
    g_out[q+3*MY:q+3*MY+8,:]=jnp.concatenate([jnp.concatenate([sg2[:,:MY]]+pad,axis=1),jnp.concatenate([sb2[:,:MY]]+pad,axis=1),jnp.broadcast_to(loss,(1,128)),jnp.zeros((5,128),F32)],axis=0)

def call_kc(sizes,lists,S,fth,ftl,af,h1h,h1l,ah,pre,h2t,lg,st,own,recv,labels,pairs,w1m,wt,w2m,npar,ncol,CLS,rows):
    NB=fth.shape[0]; BLK=S.shape[0]; H=pre.shape[2]; CP=lg.shape[1]; MY=ncol.shape[0]; NS=min(8,NB//2)
    sds=jax.ShapeDtypeStruct
    ANY=pl.BlockSpec(memory_space=pl.ANY); VM=pl.BlockSpec(memory_space=pltpu.VMEM); SM=pl.BlockSpec(memory_space=pltpu.SMEM)
    V=pltpu.VMEM
    return pl.pallas_call(functools.partial(kc,CLS=CLS),out_shape=sds((rows,128),F32),
        in_specs=[SM,SM]+[ANY]*10+[VM]*10,out_specs=VM,
        scratch_shapes=[V((BLK+1,128,128),BF)]+[V((NB,128,128),BF)]*3+[V((NS,2,128,H),BF)]*2+[V((NS,2,128,H),F32),
            V((NB,128,H),F32),V((NB,128,H),F32),V((NB,2*MY,128),BF),V((NB,CP,128),F32),V((NB,2*CP,128),BF),V((NB+1,2*CP,128),F32),
            V((NB+1,MY,128),F32),V((NB,MY,128),BF),V((NB,MY,128),F32),
            V((2,8,H),F32),V((1,128),F32),V((2*MY,3*CP),F32),V((2*MY,2*H),F32),V((MY,2*H),F32),V((2*MY,128),F32),V((MY,256),F32),V((4,MY,128),F32),
            pltpu.SemaphoreType.DMA((7,)),pltpu.SemaphoreType.DMA((NS,3))],
        compiler_params=pltpu.CompilerParams(vmem_limit_bytes=VLIM))(sizes,lists,S,fth,ftl,af,h1h,h1l,ah,pre,h2t,lg,st,own,recv,labels,pairs,w1m,wt,w2m,npar,ncol)

def at(index): return {"graph": index}
def meet(n):
    me=lax.axis_index("graph")
    barrier=pltpu.get_barrier_semaphore()
    for k in range(1,n):
        pl.semaphore_signal(barrier,inc=1,device_id=at(lax.rem(me+k,n)),device_id_type=pl.DeviceIdType.MESH)
    pl.semaphore_wait(barrier,n-1)

def kx(own,out,send,recv,n):
    me=lax.axis_index("graph")
    meet(n)
    copies=[]
    for k in range(1,n):
        peer=lax.rem(me+k,n)
        c=pltpu.make_async_remote_copy(src_ref=own.at[peer],dst_ref=out.at[me],send_sem=send.at[k-1],recv_sem=recv.at[k-1],
            device_id=at(peer),device_id_type=pl.DeviceIdType.MESH)
        c.start(); copies.append(c)
    out[me]=own[me]
    for c in copies: c.wait()

def call_kx(own,n):
    VM=pl.BlockSpec(memory_space=pltpu.VMEM)
    return pl.pallas_call(functools.partial(kx,n=n),out_shape=jax.ShapeDtypeStruct(own.shape,own.dtype),in_specs=[VM],out_specs=VM,
        scratch_shapes=[pltpu.SemaphoreType.DMA((n-1,)),pltpu.SemaphoreType.DMA((n-1,))],
        compiler_params=pltpu.CompilerParams(collective_id=1,has_side_effects=True))(own)

def kr(g,out,parts,send1,recv1,send2,recv2,n):
    me=lax.axis_index("graph")
    piece=g.shape[0]//n
    def rows(i): return pl.ds(pl.multiple_of(i*piece,8),piece)
    meet(n)
    copies=[]
    for k in range(1,n):
        peer=lax.rem(me+k,n)
        c=pltpu.make_async_remote_copy(src_ref=g.at[rows(peer)],dst_ref=parts.at[k-1],send_sem=send1.at[k-1],recv_sem=recv1.at[k-1],
            device_id=at(peer),device_id_type=pl.DeviceIdType.MESH)
        c.start(); copies.append(c)
    total=g[rows(me),:]
    for k,c in enumerate(copies):
        c.wait_recv(); total+=parts[k]
    out[rows(me),:]=total
    back=[]
    for k in range(1,n):
        peer=lax.rem(me+k,n)
        c=pltpu.make_async_remote_copy(src_ref=out.at[rows(me)],dst_ref=out.at[rows(me)],send_sem=send2.at[k-1],recv_sem=recv2.at[k-1],
            device_id=at(peer),device_id_type=pl.DeviceIdType.MESH)
        c.start(); back.append(c)
    for c in copies: c.wait_send()
    for c in back: c.wait()

def call_kr(g,n):
    VM=pl.BlockSpec(memory_space=pltpu.VMEM); D=pltpu.SemaphoreType.DMA((n-1,))
    return pl.pallas_call(functools.partial(kr,n=n),out_shape=jax.ShapeDtypeStruct(g.shape,g.dtype),in_specs=[VM],out_specs=VM,
        scratch_shapes=[pltpu.VMEM((n-1,g.shape[0]//n,128),F32),D,D,D,D],
        compiler_params=pltpu.CompilerParams(collective_id=2,has_side_effects=True))(g)

def kp(wf,ws,wh,npar,out):
    _,MY,FIN=wf.shape; H=ws.shape[2]; CLS=wh.shape[0]; CP=-(-CLS//16)*16; nk=H//128
    out[...]=jnp.zeros_like(out)
    for h in range(2):
        for k in range(nk):
            r=(h*nk+k)*MY; out[r:r+MY,:]=ws[h,:,k*128:k*128+128]
        r=2*nk*MY+h*MY; out[r:r+MY,:FIN]=wf[h]
        r=2*nk*MY+2*MY+h*CP; out[r:r+CLS,:MY]=wh[:,h,:]
        r=2*nk*MY+2*MY+2*CP+2*h; out[r:r+2,:MY]=npar[h]

def call_kp(wf,ws,wh,npar,n_col):
    _,MY,FIN=wf.shape; H=ws.shape[2]; CP=-(-wh.shape[0]//16)*16
    rows=max(2*H//128*MY+2*MY+2*CP+8,2048//n_col)
    VM=pl.BlockSpec(memory_space=pltpu.VMEM)
    return pl.pallas_call(kp,out_shape=jax.ShapeDtypeStruct((rows,128),F32),in_specs=[VM]*4,out_specs=VM)(wf,ws,wh,npar)

def kw(x,w1_out,w2_out,wh_out,npar_out,wt_out,w2m_out,ncol_out,n_col):
    H=w1_out.shape[0]; MY=H//n_col; CP=wh_out.shape[0]//4; nk=H//128
    col=lax.axis_index("col")
    back=lax.rem(H-col*MY,H)
    heads=([],[]); norms=[]; mine=([],[])
    for k in range(n_col):
        j=lax.rem(col+k,n_col); r=slice(k*MY,k*MY+MY)
        q=2*nk*MY
        h,l=split(x[j,q:q+MY,:])
        w1_out[r,:]=jnp.concatenate([h,h,l,x[j,q+MY:q+2*MY,:].astype(BF)],axis=1)
        two=[]
        for half in range(2):
            w=jnp.concatenate([x[j,(half*nk+i)*MY:(half*nk+i+1)*MY,:] for i in range(nk)],axis=1)
            w=pltpu.roll(w,back,1)
            mine[half].append(w[:,:128])
            h,l=split(w); two+=[h,h,l]
            heads[half].append(x[j,q+2*MY+half*CP:q+2*MY+(half+1)*CP,:MY])
        w2_out[r,:]=jnp.concatenate(two,axis=1)
        norms.append(x[j,q+2*MY+2*CP:q+2*MY+2*CP+8,:MY])
    npar=jnp.concatenate(norms,axis=1)
    npar_out[...]=npar
    ncol_out[...]=npar[:,:128].T[:MY]
    (ch,cl),(dh,dl)=[split(jnp.concatenate(p,axis=1)) for p in heads]
    wh_out[...]=jnp.concatenate([ch,dh,cl,dl],axis=0)
    z=jnp.zeros((128-2*CP,H),BF)
    th=jnp.concatenate([ch,dh,z],axis=0); tl=jnp.concatenate([cl,dl,z],axis=0)
    wt_out[...]=jnp.concatenate([th,th,tl],axis=0)
    for half in range(2):
        h,l=split(jnp.concatenate(mine[half],axis=0).T[:MY])
        w2m_out[2*half*MY:(2*half+2)*MY,:]=jnp.concatenate([h,l],axis=0)

def call_kw(x,n_col,H,CP):
    MY=H//n_col; sds=jax.ShapeDtypeStruct; VM=pl.BlockSpec(memory_space=pltpu.VMEM)
    return pl.pallas_call(functools.partial(kw,n_col=n_col),
        out_shape=(sds((H,512),BF),sds((H,6*H),BF),sds((4*CP,H),BF),sds((8,H),F32),sds((384,H),BF),sds((4*MY,H),BF),sds((MY,8),F32)),
        in_specs=[VM],out_specs=[VM]*7)(x)

def renew(weight, momentum, average, gradient):
    momentum_new = MOMENTUM * momentum + gradient
    weight_new = weight - STEP_RATE * (gradient + MOMENTUM * momentum_new)
    average_new = AVERAGE_KEEP * average + (1.0 - AVERAGE_KEEP) * weight_new
    return momentum_new, average_new, weight_new

def ku(g,*refs):
    weights,momenta,averages,outs,loss=refs[:4],refs[4:8],refs[8:12],refs[12:24],refs[24]
    _,MY,FIN=weights[0].shape; H=weights[1].shape[2]; CLS=weights[2].shape[0]; CP=-(-CLS//16)*16; nk=H//128
    q=2*nk*MY
    shift=lax.axis_index("col")*MY
    def store(i,where,grad):
        for o,v in zip(outs[3*i:3*i+3],renew(weights[i][where],momenta[i][where],averages[i][where],grad)): o[where]=v
    head=g[q+2*MY:q+3*MY,:].T
    for h in range(2):
        x=jnp.concatenate([g[(h*nk+k)*MY:(h*nk+k+1)*MY,:] for k in range(nk)],axis=1)
        store(1,(h,),pltpu.roll(x,shift,1))
        store(0,(h,),g[q+h*MY:q+h*MY+MY,:FIN])
        store(2,(slice(None),h,slice(None)),head[h*CP:h*CP+CLS,:MY])
    store(3,(0,),head[2*CP:2*CP+2,:MY])
    store(3,(1,),g[q+3*MY:q+3*MY+2,:MY])
    loss[0,0]=g[q+3*MY+2,0]

def call_ku(g,weights,momenta,averages):
    VM=pl.BlockSpec(memory_space=pltpu.VMEM); SM=pl.BlockSpec(memory_space=pltpu.SMEM)
    shapes=[jax.ShapeDtypeStruct(w.shape,F32) for w in weights for _ in range(3)]
    return pl.pallas_call(ku,out_shape=(*shapes,jax.ShapeDtypeStruct((1,1),F32)),in_specs=[VM]*13,out_specs=[VM]*12+[SM])(g,*weights,*momenta,*averages)

MOMENTUM=0.9; STEP_RATE=2.0; AVERAGE_KEEP=0.9

def per_device(n_graph, n_col, features, blocks, block_values, group_sizes, labels, pair_nodes, weight_first, weight_second, weight_head,
               norm_params, momentum_first, momentum_second, momentum_head, momentum_norms, average_first, average_second,
               average_head, average_norms):
    MY=weight_first.shape[2]; H=MY*n_col; CLS=weight_head.shape[2]; CP=-(-CLS//16)*16
    G=group_sizes.shape[0]; N=features.shape[2]; NB=N//128; PEER=pair_nodes.shape[3]
    def native(first,second,head,norms):
        return first.transpose(0,2,1),second.transpose(0,2,1),head.transpose(2,0,1),norms
    weights=native(weight_first,weight_second,weight_head,norm_params)
    momenta=native(momentum_first,momentum_second,momentum_head,momentum_norms)
    averages=native(average_first,average_second,average_head,average_norms)
    packed=lax.all_gather(call_kp(*weights,n_col),"col")
    sizes=group_sizes.T
    S,lists,fth,ftl,af=call_k0(sizes,blocks[0],features.transpose(1,0,2),block_values[0])
    w1,w2,wh,npar,wt,w2m,ncol=call_kw(packed,n_col,H,CP)
    pairs=pair_nodes[0].reshape(2*G,PEER)
    h1h,h1l,ah,pre,st,h2t,lg,own=call_kb(sizes,lists,S,fth,ftl,af,w1,w2,wh,npar,pairs,MY=MY)
    recv=call_kx(own.reshape(G,2*PEER,128),n_graph)
    unit=8*n_graph; rows=-(-(2*H//128*MY+3*MY+8)//unit)*unit
    g=call_kc(sizes,lists,S,fth,ftl,af,h1h,h1l,ah,pre,h2t,lg,st,own,recv,labels[0].reshape(NB,1,128),pairs,w1,wt,w2m,npar,ncol,CLS=CLS,rows=rows)
    g=call_kr(g,n_graph)
    *new,loss=call_ku(g,weights,momenta,averages)
    first=[x.transpose(0,2,1) for x in new[0:3]]
    second=[x.transpose(0,2,1) for x in new[3:6]]
    head=[x.transpose(1,2,0) for x in new[6:9]]
    return (loss[0,0],jnp.sum(group_sizes[:,0]).astype(F32),*first,*second,*head,*new[9:12])

def solution(mesh):
    P=jax.sharding.PartitionSpec
    unit=P(None,None,"col"); head=P(None,"col",None)
    weights=(unit,unit,head,unit)
    in_specs=(P("graph",None,None),P("graph",None,None),P("graph",None,None,None),P(),P("graph",None),P("graph",None,None,None))+weights*3
    out_specs=(P(),P())+(unit,)*6+(head,)*3+(unit,)*3
    return jax.shard_map(functools.partial(per_device,mesh.shape["graph"],mesh.shape["col"]),mesh=mesh,in_specs=in_specs,out_specs=out_specs,check_vma=False)
```

```python
import functools
import jax, jax.numpy as jnp
from jax import lax
from jax.experimental import pallas as pl
from jax.experimental.pallas import tpu as pltpu
BF=jnp.bfloat16; F32=jnp.float32; I32=jnp.int32
VLIM=60<<20
def dot(a,b): return jnp.dot(a,b,preferred_element_type=F32)
def dot_nt(a,b): return lax.dot_general(a,b,(((1,),(1,)),((),())),preferred_element_type=F32)
def split(x):
    h=x.astype(BF); return h,(x-h.astype(F32)).astype(BF)
GROUP=32

def my_sizes(sizes):
    me=lax.axis_index("graph")
    total=sizes[0,0]
    for g in range(1,sizes.shape[1]): total+=sizes[0,g]
    return sizes[0,me]>>7, sizes[1,me], total

def make_lists(blk_l, blk_c, lb, NB, L):
    BLK=blk_l.shape[1]
    b_c=lax.broadcasted_iota(I32,(BLK,1),0); b_l=lax.broadcasted_iota(I32,(1,BLK),1)
    live=b_c<lb
    r_l=lax.broadcasted_iota(I32,(1,128),1)
    p_l=lax.broadcasted_iota(I32,(1,L),1)
    outs=[];counts=[]
    for k in range(2):
        kc=blk_c[:,k:k+1]; oc=blk_c[:,1-k:2-k]; kl=blk_l[k:k+1,:]
        before=jnp.where((kl==kc)&(b_l<b_c),1.0,0.0)
        rank=jnp.sum(before,axis=1,keepdims=True)
        cnt=jnp.sum(jnp.where((kc==r_l)&live,1.0,0.0),axis=0,keepdims=True)
        half=jnp.floor(cnt*0.5)
        pc=cnt+(cnt-2.0*half)
        start=jnp.sum(jnp.where(r_l<kc,pc,0.0),axis=1,keepdims=True)
        pos=jnp.where(live,(start+rank).astype(I32),-1)
        null=BLK+NB*(1<<20)
        enc=b_c+oc*(1<<12)+kc*(1<<20)-null
        lo=jnp.where(pos==p_l,(enc&0xfff).astype(F32),0.0); hi=jnp.where(pos==p_l,(enc>>12).astype(F32),0.0)
        lo=jnp.sum(lo,axis=0,keepdims=True).astype(I32); hi=jnp.sum(hi,axis=0,keepdims=True).astype(I32)
        outs.append(hi*4096+lo+null)
        counts.append(jnp.broadcast_to(jnp.sum(pc,axis=1,keepdims=True).astype(I32),(1,L)))
    return jnp.concatenate(outs+counts+[jnp.zeros((4,L),I32)],axis=0)

def pair_fields(lists, which, q):
    e0=lists[which,2*q]; e1=lists[which,2*q+1]
    return e0>>20, (e0>>12)&0xff, (e1>>12)&0xff, e0&0xfff, e1&0xfff

def agg_nodes(lists, which, S, v, acc, lanes=slice(None)):
    n=lists[2+which,0]//2
    def step(s,_):
        for u in range(GROUP):
            r,c0,c1,b0,b1=pair_fields(lists,which,s*GROUP+u)
            lhs=jnp.concatenate([S[b0],S[b1]],axis=1)
            rhs=jnp.concatenate([v[c0],v[c1]],axis=0)
            acc[r,:,lanes]+=dot(lhs,rhs)
        return 0
    lax.fori_loop(0,pl.cdiv(n,GROUP),step,0)

def agg_rows(lists, which, S, v, acc, rows=slice(None)):
    n=lists[2+which,0]//2
    def step(s,_):
        for u in range(GROUP):
            r,c0,c1,b0,b1=pair_fields(lists,which,s*GROUP+u)
            lhs=jnp.concatenate([v[c0],v[c1]],axis=1)
            acc[r,rows]+=dot(lhs,jnp.concatenate([S[b0],S[b1]],axis=0))
        return 0
    lax.fori_loop(0,pl.cdiv(n,GROUP),step,0)

def k0(sizes, blk_l, feat, vals, S_out, lists_out, fth_out, ftl_out, af_out,
       S, lists_v, lists_s, ft_v, fth, ftl, acc, af, buf, sem_in, sem_f, sem_l, sem_o, sem_S, CH, NBUF):
    nb,lb,_=my_sizes(sizes)
    NB=acc.shape[0]-1; BLK=vals.shape[0]; FIN=feat.shape[0]
    L=lists_v.shape[1]
    nch=pl.cdiv(lb,CH)
    def chunk_in(i,slot): return pltpu.make_async_copy(vals.at[pl.ds(i*CH,CH)],buf.at[slot],sem_in.at[slot])
    def chunk_out(i): return pltpu.make_async_copy(S.at[pl.ds(i*CH,CH)],S_out.at[pl.ds(i*CH,CH)],sem_S.at[i])
    for i in range(NBUF):
        @pl.when(i<nch)
        def _(): chunk_in(i,i).start()
    cf=pltpu.make_async_copy(feat.at[:,0],ft_v,sem_f); cf.start()
    ids=blk_l[...]
    columns=jnp.concatenate([ids.astype(F32),jnp.zeros((6,BLK),F32)],axis=0).T.astype(I32)
    lists_v[...]=make_lists(ids,columns,lb,NB,L)
    cl=pltpu.make_async_copy(lists_v,lists_s,sem_l.at[0]); cl.start()
    co=pltpu.make_async_copy(lists_v,lists_out,sem_l.at[1]); co.start()
    S[BLK]=jnp.zeros((128,128),BF)
    acc[...]=jnp.zeros(acc.shape,F32)
    cf.wait()
    per=CH*NB//BLK
    def conv(i,_):
        slot=lax.rem(i,NBUF)
        chunk_in(i,slot).wait()
        for k in range(CH):
            S[i*CH+k]=buf[slot,k].T.astype(BF)
        for k in range(per):
            b=i*per+k
            x=ft_v[:,pl.ds(pl.multiple_of(b*128,128),128)]
            x=jnp.concatenate([x,jnp.zeros((128-FIN,128),F32)],axis=0).T
            h,l=split(x); fth[b]=h; ftl[b]=l
        @pl.when(i+NBUF<nch)
        def _(): chunk_in(i+NBUF,slot).start()
        chunk_out(i).start()
        return 0
    lax.fori_loop(0,nch,conv,0)
    c1=pltpu.make_async_copy(fth,fth_out,sem_o.at[0]); c1.start()
    c2=pltpu.make_async_copy(ftl,ftl_out,sem_o.at[1]); c2.start()
    cl.wait()
    agg_nodes(lists_s,0,S,fth,acc)
    def fin(b,_):
        af[b]=acc[b].astype(BF); return 0
    lax.fori_loop(0,nb,fin,0)
    c3=pltpu.make_async_copy(af,af_out,sem_o.at[2]); c3.start()
    lax.fori_loop(0,nch,lambda i,_:(chunk_out(i).wait(),0)[1],0)
    c1.wait();c2.wait();c3.wait();co.wait()

def call_k0(sizes, blk, feat, vals, CH=16, NBUF=12):
    FIN,_,N=feat.shape; NB=N//128; BLK=vals.shape[0]; L=pl.cdiv(BLK+NB,128)*128
    CH=min(CH,BLK)
    sds=jax.ShapeDtypeStruct
    ANY=pl.BlockSpec(memory_space=pl.ANY); VM=pl.BlockSpec(memory_space=pltpu.VMEM); SM=pl.BlockSpec(memory_space=pltpu.SMEM)
    return pl.pallas_call(functools.partial(k0,CH=CH,NBUF=NBUF),
        out_shape=(sds((BLK,128,128),BF),sds((8,L),I32),sds((NB,128,128),BF),sds((NB,128,128),BF),sds((NB,128,128),BF)),
        in_specs=[SM,VM,ANY,ANY],out_specs=[ANY]*5,
        scratch_shapes=[pltpu.VMEM((BLK+1,128,128),BF),pltpu.VMEM((8,L),I32),pltpu.SMEM((8,L),I32),pltpu.VMEM((FIN,N),F32),
            pltpu.VMEM((NB,128,128),BF),pltpu.VMEM((NB,128,128),BF),pltpu.VMEM((NB+1,128,128),F32),pltpu.VMEM((NB,128,128),BF),
            pltpu.VMEM((NBUF,CH,128,128),F32),
            pltpu.SemaphoreType.DMA((NBUF,)),pltpu.SemaphoreType.DMA(()),pltpu.SemaphoreType.DMA((2,)),pltpu.SemaphoreType.DMA((3,)),pltpu.SemaphoreType.DMA((pl.cdiv(BLK,CH),))],
        compiler_params=pltpu.CompilerParams(vmem_limit_bytes=VLIM))(sizes,blk,feat,vals)
G0=0.7978845608; G1=0.044715
EPS=1e-5
HP=64
def for_blocks(nb,U,fn,start=0):
    full=nb//U
    def many(s,_): fn(s*U,U); return 0
    def one(b,_): fn(b,1); return 0
    lax.fori_loop(start,full,many,0)
    if U>1: lax.fori_loop(full*U,nb,one,0)
def rows8(x): return jnp.sum(x.reshape(x.shape[0]//8,8,x.shape[1]),axis=0)
def blk(ref,b0,U):
    x=ref[pl.ds(b0,U)]; return x.reshape(U*x.shape[1],x.shape[2])
def put_blk(ref,b0,U,x): ref[pl.ds(b0,U)]=x.reshape((U,)+ref.shape[1:])
def gelu_half(w):
    return w+w*jnp.tanh(w*(2.0*G0+(8.0*G0*G1)*(w*w)))
def dgelu_half(w):
    q=w*w
    t=jnp.tanh(w*(2.0*G0+(8.0*G0*G1)*q))
    return (1.0+t)*(0.5+(w*(G0+(12.0*G0*G1)*q))*(1.0-t))

def moments(sums,shift,count):
    d=jnp.sum(sums[0],axis=0,keepdims=True)/count
    v=jnp.sum(sums[1],axis=0,keepdims=True)/count-d*d
    return shift+d,lax.rsqrt(v+EPS)

def slot_nodes(pairs):
    R,K=pairs.shape; G=R//2
    x=jnp.concatenate([pairs[...].astype(F32),jnp.zeros((R,128-K),F32)],axis=1)
    if R%128: x=jnp.concatenate([x,jnp.zeros((128-R%128,128),F32)],axis=0)
    x=x.T[:K].astype(I32)
    return jnp.concatenate([x[:,t*G+g:t*G+g+1] for g in range(G) for t in range(2)],axis=0)
def one_hot(slots,b):
    return jnp.where(slots==lax.broadcasted_iota(I32,(1,128),1)+b*128,1.0,0.0).astype(BF)

def kb(sizes,lists,pairs,S_in,fth_in,ftl_in,af_in,w1,w2,wh,npar,
       h1h_out,h1l_out,pre_out,pre1_out,st_out,h2t_out,lg_out,own_out,
       S,fth,ftl,af,h1h,h1l,acc,pre,zz,lg,h2t,pre1,sums,st,sem_i,sem_o):
    nb,_,_=my_sizes(sizes); NB=fth.shape[0]; BLK=S_in.shape[0]; CP=lg.shape[1]; MY=pre1.shape[1]
    count=(nb*128).astype(F32)
    cs=[pltpu.make_async_copy(a,b,sem_i.at[i]) for i,(a,b) in enumerate(((fth_in,fth),(ftl_in,ftl),(af_in,af),(S_in,S.at[pl.ds(0,BLK)])))]
    for c in cs: c.start()
    S[BLK]=jnp.zeros((128,128),BF)
    st[...]=jnp.zeros_like(st)
    for c in cs[:3]: c.wait()
    def first(b0,U):
        h=blk(fth,b0,U)
        x=jnp.concatenate([h,blk(ftl,b0,U),h,blk(af,b0,U)],axis=1)
        return dot_nt(x,w1[...])
    def second(b0,U):
        h=blk(h1h,b0,U); l=blk(h1l,b0,U); ah,al=split(blk(acc,b0,U))
        return dot_nt(jnp.concatenate([h,l,h,ah,al,ah],axis=1),w2[...])
    def layer(fn,mine):
        shift=jnp.sum(fn(0,1),axis=0,keepdims=True)/128.0
        sums[...]=jnp.zeros_like(sums)
        def tile(b0,U):
            y=fn(b0,U)
            put_blk(pre,b0,U,y)
            if mine:
                for k in range(U): pre1[b0+k]=y[k*128:k*128+128,:MY].T
            d=y-shift
            sums[0]+=rows8(d); sums[1]+=rows8(d*d)
        for_blocks(nb,8,tile)
        return moments(sums,shift,count)
    mean,inv=layer(first,True)
    st[0:1,:]=mean; st[1:2,:]=inv
    a=npar[0:1,:]*inv; c=npar[1:2,:]-mean*a
    a=0.5*a; c=0.5*c
    def n1(b0,U):
        h,l=split(gelu_half(blk(pre,b0,U)*a+c))
        put_blk(h1h,b0,U,h); put_blk(h1l,b0,U,l)
        put_blk(acc,b0,U,jnp.zeros((U*128,acc.shape[2]),F32))
    for_blocks(nb,4,n1)
    acc[NB]=jnp.zeros(acc.shape[1:],F32)
    outs=[pltpu.make_async_copy(x,y,sem_o.at[i]) for i,(x,y) in enumerate(((h1h,h1h_out),(h1l,h1l_out),(pre1,pre1_out)))]
    for o in outs: o.start()
    cs[3].wait()
    agg_nodes(lists,0,S,h1h,acc)
    mean2,inv2=layer(second,False)
    st[2:3,:]=mean2; st[3:4,:]=inv2
    outs.append(pltpu.make_async_copy(pre,pre_out,sem_o.at[3])); outs[-1].start()
    a2=npar[2:3,:]*inv2; c2=npar[3:4,:]-mean2*a2
    a2=0.5*a2; c2=0.5*c2
    def n2(b0,U):
        h,l=split(gelu_half(blk(pre,b0,U)*a2+c2))
        r=dot_nt(h,wh[...])
        dz=r[:,:2*HP]+r[:,2*HP:]+dot_nt(l,wh[0:2*HP,:])
        zh,zl=split(dz)
        put_blk(zz,b0,U,jnp.concatenate([zh[:,HP:],zl[:,HP:]],axis=1))
        put_blk(acc,b0,U,jnp.concatenate([dz,jnp.zeros_like(dz)],axis=1))
        t=jnp.concatenate([h[:,:MY],l[:,:MY]],axis=1)
        for k in range(U): h2t[b0+k]=t[k*128:k*128+128].T
    for_blocks(nb,8,n2)
    outs.append(pltpu.make_async_copy(h2t,h2t_out,sem_o.at[4])); outs[-1].start()
    agg_nodes(lists,0,S,zz,acc,slice(2*HP,4*HP))
    def fin(b0,U):
        for k in range(U):
            x=acc[b0+k]; s=x[:,2*HP:]
            y=x[:,:2*HP]+s+pltpu.roll(s,HP,1)
            acc[b0+k,:,:2*HP]=y
            lg[b0+k]=y.T[:CP]
    for_blocks(nb,8,fin)
    outs.append(pltpu.make_async_copy(lg,lg_out,sem_o.at[5])); outs[-1].start()
    G=pairs.shape[0]//2; K=pairs.shape[1]
    lane=lax.broadcasted_iota(I32,(1,128),1); sub=lax.broadcasted_iota(I32,(8,1),0)
    def slot(g,_):
        for t in range(2):
            for k0 in range(0,K,8):
                o=jnp.zeros((8,128),F32)
                for k in range(8):
                    n=pairs[t*G+g,k0+k]
                    x=acc[n>>7,pl.ds(pl.multiple_of(((n>>3)&15)*8,8),8),:2*HP]
                    o=jnp.where(sub==k,jnp.sum(jnp.where(sub==(n&7),x,0.0),axis=0,keepdims=True),o)
                own_out[pl.ds(pl.multiple_of((g*2+t)*K+k0,8),8),:]=jnp.where(lane<CP,o,0.0)
        return 0
    lax.fori_loop(0,G,slot,0)
    st_out[...]=st[...]
    for o in outs: o.wait()

def call_kb(sizes,lists,S,fth,ftl,af,w1,w2,wh,npar,pairs,MY,CP):
    NB=fth.shape[0]; BLK=S.shape[0]; H=w2.shape[0]
    sds=jax.ShapeDtypeStruct
    ANY=pl.BlockSpec(memory_space=pl.ANY); VM=pl.BlockSpec(memory_space=pltpu.VMEM); SM=pl.BlockSpec(memory_space=pltpu.SMEM)
    V=pltpu.VMEM
    return pl.pallas_call(kb,
        out_shape=(sds((NB,128,H),BF),sds((NB,128,H),BF),sds((NB,128,H),F32),sds((NB,MY,128),F32),sds((8,H),F32),sds((NB,2*MY,128),BF),sds((NB,CP,128),F32),sds((pairs.size,128),F32)),
        in_specs=[SM]*3+[ANY]*4+[VM]*4,out_specs=[ANY]*4+[VM]+[ANY]*2+[VM],
        scratch_shapes=[V((BLK+1,128,128),BF)]+[V((NB,128,128),BF)]*3+[V((NB,128,H),BF)]*2+[V((NB+1,128,H),F32),V((NB,128,H),F32),
            V((NB,128,2*HP),BF),V((NB,CP,128),F32),V((NB,2*MY,128),BF),V((NB,MY,128),F32),V((2,8,H),F32),V((8,H),F32),
            pltpu.SemaphoreType.DMA((4,)),pltpu.SemaphoreType.DMA((6,))],
        compiler_params=pltpu.CompilerParams(vmem_limit_bytes=VLIM))(sizes,lists,pairs,S,fth,ftl,af,w1,w2,wh,npar)


def kc(sizes,lists,S_in,fth_in,ftl_in,af_in,h1h_in,h1l_in,pre_in,pre1_in,h2t_in,lg_in,st,own,recv,labels,pairs,wt,w2m,npar,ncol,
       g_out,
       S,rfh,rfl,raf,rh,rl,pre,du,h2t,lg,gz,acc,v4,pre1,sums,cross,RH,RS,RL,R1,R2,colsum,sem_i,sem_r,CLS):
    nb,_,nodes=my_sizes(sizes); BLK=S_in.shape[0]; NB=pre.shape[0]; CP=lg.shape[1]; MY=ncol.shape[0]; H=pre.shape[2]; NS=rh.shape[0]; U8=rh.shape[1]
    count=(nb*128).astype(F32); total=nodes.astype(F32)
    ins=((lg_in,lg),(S_in,S.at[pl.ds(0,BLK)]),(pre_in,pre),(h2t_in,h2t),(pre1_in,pre1))
    cs=[pltpu.make_async_copy(a,b,sem_i.at[i]) for i,(a,b) in enumerate(ins)]
    for c in cs[:2]: c.start()
    nch=pl.cdiv(nb,U8)
    def ring(i):
        s=lax.rem(i,NS)
        return [pltpu.make_async_copy(a.at[pl.ds(i*U8,U8)],b.at[s],sem_r.at[s,k]) for k,(a,b) in enumerate(((h1h_in,rh),(h1l_in,rl),(fth_in,rfh),(ftl_in,rfl),(af_in,raf)))]
    S[BLK]=jnp.zeros((128,128),BF)
    for r in (sums,cross,RH,RS,RL,R1,R2,colsum): r[...]=jnp.zeros_like(r)
    acc[NB]=jnp.zeros(acc.shape[1:],F32)
    half=pairs.shape[1]
    G=pairs.shape[0]//2
    r=recv[...]
    D=own[...].reshape(G,2*half,128)-jnp.concatenate([r[:,half:],r[:,:half]],axis=1)
    pair_loss=0.5*jnp.sum(D[:,half:]*D[:,half:])
    Dh,Dl=split((D.reshape(2*G*half,128).T)[:CP]/total); D2=jnp.concatenate([Dh,Dl],axis=0)
    slots=slot_nodes(pairs)
    cs[0].wait()
    def soft(b0,U):
        hot=jnp.concatenate([one_hot(slots,b0+k) for k in range(U)],axis=1)
        add=dot(D2,hot); add=add[:CP]+add[CP:]
        x=jnp.concatenate([lg[b0+k] for k in range(U)],axis=1)
        lab=jnp.concatenate([labels[b0+k] for k in range(U)],axis=1)
        row=lax.broadcasted_iota(I32,(CP,1),0)
        xm=jnp.where(row<CLS,x,-1e30)
        mx=jnp.max(xm,axis=0,keepdims=True)
        e=jnp.exp(xm-mx); s=jnp.sum(e,axis=0,keepdims=True)
        hit=jnp.where(row==lab,1.0,0.0)
        c=mx+jnp.log(s)-jnp.sum(hit*x,axis=0,keepdims=True)
        g=(e/s-hit)/total+add
        h,l=split(g)
        for k in range(U):
            w=slice(k*128,k*128+128)
            cross[...]+=c[:,w]
            gz[b0+k]=jnp.concatenate([h[:,w],l[:,w]],axis=0)
            acc[b0+k,:2*CP]=jnp.zeros((2*CP,128),F32)
    for_blocks(nb,4,soft)
    cs[1].wait()
    for c in cs[2:]: c.start()
    agg_rows(lists,1,S,gz,acc,slice(0,2*CP))
    for i in range(NS):
        @pl.when(i<nch)
        def _():
            for c in ring(i): c.start()
    for c in cs[2:]: c.wait()
    mean2=st[2:3,:]; inv2=st[3:4,:]
    a2=npar[2:3,:]*inv2; c2=npar[3:4,:]-mean2*a2
    ha2=0.5*a2; hc2=0.5*c2
    def back2(b0,U):
        th=[];tl=[];ads=[]
        z=jnp.zeros((128-2*CP,128),BF)
        for k in range(U):
            ad=acc[b0+k,:2*CP]; ah,al=split(ad[:CP]+ad[CP:]); gk=gz[b0+k]
            th.append(jnp.concatenate([gk[:CP],ah,z],axis=0).T); tl.append(jnp.concatenate([gk[CP:],al,z],axis=0).T)
            ads.append(ah)
        th=jnp.concatenate(th,axis=0); tl=jnp.concatenate(tl,axis=0)
        gh=dot(jnp.concatenate([th,tl,th],axis=1),wt[...])
        hh=jnp.concatenate([h2t[b0+k] for k in range(U)],axis=1)
        gg=jnp.concatenate([jnp.concatenate([gz[b0+k] for k in range(U)],axis=1),jnp.concatenate(ads,axis=1)],axis=0)
        RH[...]+=dot_nt(hh,gg)
        y=blk(pre,b0,U)
        d=gh*dgelu_half(y*ha2+hc2)
        put_blk(du,b0,U,d)
        sums[0]+=rows8(d); sums[1]+=rows8(d*(y-mean2))
    for_blocks(nb,8,back2)
    sb2=jnp.sum(sums[0],axis=0,keepdims=True); sg2=jnp.sum(sums[1],axis=0,keepdims=True)*inv2
    A2=-a2*inv2*sg2/count; C2=-a2*sb2/count-A2*mean2
    def proj(b0,U):
        h,l=split(blk(du,b0,U)*a2+blk(pre,b0,U)*A2+C2)
        r=dot_nt(w2m[...],h); rl2=dot_nt(w2m[0:MY,:],l)
        d=r[:MY]+r[MY:2*MY]+rl2; t=(r[2*MY:3*MY]+r[3*MY:]).astype(BF)
        gt=jnp.concatenate([h[:,:MY],l[:,:MY]],axis=1)
        for k in range(U):
            w=slice(k*128,k*128+128)
            acc[b0+k]=jnp.concatenate([d[:,w],jnp.zeros((2*MY,128),F32)],axis=0)
            v4[b0+k]=jnp.concatenate([t[:,w],gt[w].T],axis=0)
    for_blocks(nb,8,proj)
    acc[NB]=jnp.zeros(acc.shape[1:],F32)
    agg_rows(lists,1,S,v4,acc)
    lane=lambda x: jnp.sum(x,axis=1,keepdims=True)
    stc=st[:,:128].T[:MY]
    mean1=stc[:,0:1]; inv1=stc[:,1:2]
    a1=ncol[:,0:1]*inv1; c1=ncol[:,1:2]-mean1*a1
    ha1=0.5*a1; hc1=0.5*c1
    def back1(b0,U):
        for k in range(U):
            p=pre1[b0+k]
            d=acc[b0+k,:MY]*dgelu_half(p*ha1+hc1)
            acc[b0+k,:MY]=d
            colsum[0]+=d; colsum[1]+=d*(p-mean1)
    for_blocks(nb,4,back1)
    sb1=lane(colsum[0]); sg1=lane(colsum[1])*inv1
    A1=-a1*inv1*sg1/count; C1=-a1*sb1/count-A1*mean1
    def last(i,_):
        s=lax.rem(i,NS)
        for c in ring(i): c.wait()
        def part(b0,off,U):
            f=lambda ref: ref[s,pl.ds(off,U)].reshape(U*128,ref.shape[3])
            x=[acc[b0+k] for k in range(U)]
            gh,gl=split(jnp.concatenate([x[k][:MY]*a1+pre1[b0+k]*A1+C1 for k in range(U)],axis=1))
            R1[...]+=dot(jnp.concatenate([gh,gl],axis=0),f(rfh))
            R2[...]+=dot(gh,jnp.concatenate([f(rfl),f(raf)],axis=1))
            ah,al=split(jnp.concatenate([x[k][MY:2*MY]+x[k][2*MY:] for k in range(U)],axis=1))
            gt=jnp.concatenate([v4[b0+k,MY:] for k in range(U)],axis=1)
            RS[...]+=dot(jnp.concatenate([gt,ah,al],axis=0),f(rh))
            RL[...]+=dot(jnp.concatenate([gt[:MY],ah],axis=0),f(rl))
        @pl.when((i+1)*U8<=nb)
        def _(): part(i*U8,0,U8)
        @pl.when((i+1)*U8>nb)
        def _():
            lax.fori_loop(0,nb-i*U8,lambda k,_:(part(i*U8+k,k,1),0)[1],0)
        @pl.when(i+NS<nch)
        def _():
            for c in ring(i+NS): c.start()
        return 0
    lax.fori_loop(0,nch,last,0)
    RSv=RS[...]; RLv=RL[...]; nk=H//128
    for h in range(2):
        gs=RSv[2*h*MY:(2*h+1)*MY]+RSv[(2*h+1)*MY:(2*h+2)*MY]+RLv[h*MY:(h+1)*MY]
        for k in range(nk): g_out[(h*nk+k)*MY:(h*nk+k+1)*MY,:]=gs[:,k*128:k*128+128]
    R1v=R1[...]; R2v=R2[...]
    q=2*nk*MY
    g_out[q:q+MY,:]=R1v[:MY]+R1v[MY:]+R2v[:,:128]
    g_out[q+MY:q+2*MY,:]=R2v[:,128:]
    RHv=RH[...]; gh=RHv[:MY]+RHv[MY:]
    gh=jnp.concatenate([RHv[:MY,:CP]+RHv[:MY,CP:2*CP]+RHv[MY:,:CP],gh[:,2*CP:3*CP],sg1,sb1,jnp.zeros((MY,128-2*CP-2),F32)],axis=1)
    g_out[q+2*MY:q+3*MY,:]=gh
    loss=jnp.sum(cross[...])+pair_loss
    pad=[jnp.zeros((1,128-MY),F32)]
    g_out[q+3*MY:,:]=jnp.zeros((g_out.shape[0]-q-3*MY,128),F32)
    g_out[q+3*MY:q+3*MY+8,:]=jnp.concatenate([jnp.concatenate([sg2[:,:MY]]+pad,axis=1),jnp.concatenate([sb2[:,:MY]]+pad,axis=1),jnp.broadcast_to(loss,(1,128)),jnp.zeros((5,128),F32)],axis=0)

def call_kc(sizes,lists,S,fth,ftl,af,h1h,h1l,pre,pre1,h2t,lg,st,own,recv,labels,pairs,wt,w2m,npar,ncol,CLS,rows):
    NB=fth.shape[0]; BLK=S.shape[0]; H=pre.shape[2]; CP=lg.shape[1]; MY=ncol.shape[0]; NS=3; U8=8
    sds=jax.ShapeDtypeStruct
    ANY=pl.BlockSpec(memory_space=pl.ANY); VM=pl.BlockSpec(memory_space=pltpu.VMEM); SM=pl.BlockSpec(memory_space=pltpu.SMEM)
    V=pltpu.VMEM
    return pl.pallas_call(functools.partial(kc,CLS=CLS),out_shape=sds((rows,128),F32),
        in_specs=[SM,SM]+[ANY]*10+[VM]*9,out_specs=VM,
        scratch_shapes=[V((BLK+1,128,128),BF)]+[V((NS,U8,128,128),BF)]*3+[V((NS,U8,128,H),BF)]*2+[
            V((NB,128,H),F32),V((NB,128,H),F32),V((NB,2*MY,128),BF),V((NB,CP,128),F32),V((NB,2*CP,128),BF),V((NB+1,max(3*MY,2*CP),128),F32),
            V((NB,3*MY,128),BF),V((NB,MY,128),F32),
            V((2,8,H),F32),V((1,128),F32),V((2*MY,3*CP),F32),V((4*MY,H),F32),V((2*MY,H),F32),V((2*MY,128),F32),V((MY,256),F32),V((2,MY,128),F32),
            pltpu.SemaphoreType.DMA((5,)),pltpu.SemaphoreType.DMA((NS,5))],
        compiler_params=pltpu.CompilerParams(vmem_limit_bytes=VLIM))(sizes,lists,S,fth,ftl,af,h1h,h1l,pre,pre1,h2t,lg,st,own,recv,labels,pairs,wt,w2m,npar,ncol)

def at(index): return {"graph": index}
def meet(n):
    me=lax.axis_index("graph")
    barrier=pltpu.get_barrier_semaphore()
    for k in range(1,n):
        pl.semaphore_signal(barrier,inc=1,device_id=at(lax.rem(me+k,n)),device_id_type=pl.DeviceIdType.MESH)
    pl.semaphore_wait(barrier,n-1)

def kx(own,out,send,recv,n):
    me=lax.axis_index("graph")
    meet(n)
    copies=[]
    for k in range(1,n):
        peer=lax.rem(me+k,n)
        c=pltpu.make_async_remote_copy(src_ref=own.at[peer],dst_ref=out.at[me],send_sem=send.at[k-1],recv_sem=recv.at[k-1],
            device_id=at(peer),device_id_type=pl.DeviceIdType.MESH)
        c.start(); copies.append(c)
    out[me]=own[me]
    for c in copies: c.wait()

def call_kx(own,n):
    VM=pl.BlockSpec(memory_space=pltpu.VMEM)
    return pl.pallas_call(functools.partial(kx,n=n),out_shape=jax.ShapeDtypeStruct(own.shape,own.dtype),in_specs=[VM],out_specs=VM,
        scratch_shapes=[pltpu.SemaphoreType.DMA((n-1,)),pltpu.SemaphoreType.DMA((n-1,))],
        compiler_params=pltpu.CompilerParams(collective_id=1,has_side_effects=True))(own)

def kr(g,out,parts,send1,recv1,send2,recv2,n):
    me=lax.axis_index("graph")
    piece=g.shape[0]//n
    def rows(i): return pl.ds(pl.multiple_of(i*piece,8),piece)
    meet(n)
    copies=[]
    for k in range(1,n):
        peer=lax.rem(me+k,n)
        c=pltpu.make_async_remote_copy(src_ref=g.at[rows(peer)],dst_ref=parts.at[k-1],send_sem=send1.at[k-1],recv_sem=recv1.at[k-1],
            device_id=at(peer),device_id_type=pl.DeviceIdType.MESH)
        c.start(); copies.append(c)
    total=g[rows(me),:]
    for k,c in enumerate(copies):
        c.wait_recv(); total+=parts[k]
    out[rows(me),:]=total
    back=[]
    for k in range(1,n):
        peer=lax.rem(me+k,n)
        c=pltpu.make_async_remote_copy(src_ref=out.at[rows(me)],dst_ref=out.at[rows(me)],send_sem=send2.at[k-1],recv_sem=recv2.at[k-1],
            device_id=at(peer),device_id_type=pl.DeviceIdType.MESH)
        c.start(); back.append(c)
    for c in copies: c.wait_send()
    for c in back: c.wait()

def call_kr(g,n):
    VM=pl.BlockSpec(memory_space=pltpu.VMEM); D=pltpu.SemaphoreType.DMA((n-1,))
    return pl.pallas_call(functools.partial(kr,n=n),out_shape=jax.ShapeDtypeStruct(g.shape,g.dtype),in_specs=[VM],out_specs=VM,
        scratch_shapes=[pltpu.VMEM((n-1,g.shape[0]//n,128),F32),D,D,D,D],
        compiler_params=pltpu.CompilerParams(collective_id=2,has_side_effects=True))(g)

def kp(wf,ws,wh,npar,out,half):
    _,MY,FIN=wf.shape; H=ws.shape[2]; CLS=wh.shape[0]; CP=-(-CLS//16)*16; nk=H//128
    out[...]=jnp.zeros_like(out)
    for h in range(2):
        for k in range(nk):
            r=(h*nk+k)*MY; out[r:r+MY,:]=ws[h,:,k*128:k*128+128]
        r=2*nk*MY+h*MY; out[r:r+MY,:FIN]=wf[h]
        r=2*nk*MY+2*MY+h*CP; out[r:r+CLS,:MY]=wh[:,h,:]
        r=2*nk*MY+2*MY+2*CP+2*h; out[r:r+2,:MY]=npar[h]
    core=lax.rem(lax.axis_index("graph"),2); n=half.shape[0]
    half[...]=out[pl.ds(pl.multiple_of(core*n,8),n),:]

def call_kp(wf,ws,wh,npar):
    _,MY,FIN=wf.shape; H=ws.shape[2]; CP=-(-wh.shape[0]//16)*16
    rows=-(-(2*H//128*MY+2*MY+2*CP+8)//16)*16
    VM=pl.BlockSpec(memory_space=pltpu.VMEM)
    return pl.pallas_call(kp,out_shape=(jax.ShapeDtypeStruct((rows,128),F32),jax.ShapeDtypeStruct((rows//2,128),F32)),in_specs=[VM]*4,out_specs=[VM]*2)(wf,ws,wh,npar)

def kw(own,*refs,n_col,CP):
    halves=refs[:n_col-1]; w1_out,w2_out,wh_out,npar_out,wt_out,w2m_out,ncol_out,x,send,recv=refs[n_col-1:]
    me=lax.axis_index("graph"); core=lax.rem(me,2); twin=me+1-2*core
    barrier=pltpu.get_barrier_semaphore()
    pl.semaphore_signal(barrier,inc=1,device_id=at(twin),device_id_type=pl.DeviceIdType.MESH)
    n=own.shape[0]//2; rows=pl.ds(pl.multiple_of(core*n,8),n)
    pl.semaphore_wait(barrier,1)
    copies=[]
    for k in range(1,n_col):
        c=pltpu.make_async_remote_copy(src_ref=halves[k-1],dst_ref=x.at[k,rows],send_sem=send.at[k-1],recv_sem=recv.at[k-1],
            device_id=at(twin),device_id_type=pl.DeviceIdType.MESH)
        c.start(); copies.append(c)
    x[0]=own[...]
    for k in range(1,n_col): x[k,rows,:]=halves[k-1][...]
    for c in copies: c.wait()
    H=w1_out.shape[0]; MY=H//n_col; nk=H//128
    col=lax.axis_index("col")
    back=lax.rem(H-col*MY,H)
    heads=([],[]); norms=[]; mine=([],[])
    for k in range(n_col):
        j=k; r=slice(k*MY,k*MY+MY)
        q=2*nk*MY
        h,l=split(x[j,q:q+MY,:])
        w1_out[r,:]=jnp.concatenate([h,h,l,x[j,q+MY:q+2*MY,:].astype(BF)],axis=1)
        two=[]
        for half in range(2):
            w=jnp.concatenate([x[j,(half*nk+i)*MY:(half*nk+i+1)*MY,:] for i in range(nk)],axis=1)
            w=pltpu.roll(w,back,1)
            mine[half].append(w[:,:128])
            h,l=split(w); two+=[h,h,l]
            heads[half].append(x[j,q+2*MY+half*CP:q+2*MY+(half+1)*CP,:MY])
        w2_out[r,:]=jnp.concatenate(two,axis=1)
        norms.append(x[j,q+2*MY+2*CP:q+2*MY+2*CP+8,:MY])
    npar=jnp.concatenate(norms,axis=1)
    npar_out[...]=npar
    ncol_out[...]=npar[:,:128].T[:MY]
    (ch,cl),(dh,dl)=[split(jnp.concatenate(p,axis=1)) for p in heads]
    z=jnp.zeros((HP-CP,H),BF)
    wh_out[...]=jnp.concatenate([ch,z,dh,z,cl,z,dl,z],axis=0)
    z=jnp.zeros((128-2*CP,H),BF)
    th=jnp.concatenate([ch,dh,z],axis=0); tl=jnp.concatenate([cl,dl,z],axis=0)
    wt_out[...]=jnp.concatenate([th,th,tl],axis=0)
    for half in range(2):
        h,l=split(jnp.concatenate(mine[half],axis=0).T[:MY])
        w2m_out[2*half*MY:(2*half+2)*MY,:]=jnp.concatenate([h,l],axis=0)

def call_kw(own,halves,H,CP):
    n_col=1+len(halves); MY=H//n_col; sds=jax.ShapeDtypeStruct; VM=pl.BlockSpec(memory_space=pltpu.VMEM)
    return pl.pallas_call(functools.partial(kw,n_col=n_col,CP=CP),
        out_shape=(sds((H,512),BF),sds((H,6*H),BF),sds((4*HP,H),BF),sds((8,H),F32),sds((384,H),BF),sds((4*MY,H),BF),sds((MY,8),F32)),
        in_specs=[VM]*n_col,out_specs=[VM]*7,
        scratch_shapes=[pltpu.VMEM((n_col,)+own.shape,F32),pltpu.SemaphoreType.DMA((n_col-1,)),pltpu.SemaphoreType.DMA((n_col-1,))],
        compiler_params=pltpu.CompilerParams(collective_id=3,has_side_effects=True))(own,*halves)

def renew(weight, momentum, average, gradient):
    momentum_new = MOMENTUM * momentum + gradient
    weight_new = weight - STEP_RATE * (gradient + MOMENTUM * momentum_new)
    average_new = AVERAGE_KEEP * average + (1.0 - AVERAGE_KEEP) * weight_new
    return momentum_new, average_new, weight_new

def ku(sizes,g,*refs):
    weights,momenta,averages,outs,loss,count=refs[:4],refs[4:8],refs[8:12],refs[12:24],refs[24],refs[25]
    _,MY,FIN=weights[0].shape; H=weights[1].shape[2]; CLS=weights[2].shape[0]; CP=-(-CLS//16)*16; nk=H//128
    q=2*nk*MY
    shift=lax.axis_index("col")*MY
    def store(i,where,grad):
        for o,v in zip(outs[3*i:3*i+3],renew(weights[i][where],momenta[i][where],averages[i][where],grad)): o[where]=v
    head=g[q+2*MY:q+3*MY,:].T
    for h in range(2):
        x=jnp.concatenate([g[(h*nk+k)*MY:(h*nk+k+1)*MY,:] for k in range(nk)],axis=1)
        store(1,(h,),pltpu.roll(x,shift,1))
        store(0,(h,),g[q+h*MY:q+h*MY+MY,:FIN])
        store(2,(slice(None),h,slice(None)),head[h*CP:h*CP+CLS,:MY])
    store(3,(0,),head[2*CP:2*CP+2,:MY])
    store(3,(1,),g[q+3*MY:q+3*MY+2,:MY])
    loss[0,0]=g[q+3*MY+2,0]
    count[0,0]=my_sizes(sizes)[2].astype(F32)

def call_ku(sizes,g,weights,momenta,averages):
    VM=pl.BlockSpec(memory_space=pltpu.VMEM); SM=pl.BlockSpec(memory_space=pltpu.SMEM)
    shapes=[jax.ShapeDtypeStruct(w.shape,F32) for w in weights for _ in range(3)]
    return pl.pallas_call(ku,out_shape=(*shapes,*[jax.ShapeDtypeStruct((1,1),F32)]*2),in_specs=[SM]+[VM]*13,out_specs=[VM]*12+[SM]*2)(sizes,g,*weights,*momenta,*averages)

MOMENTUM=0.9; STEP_RATE=2.0; AVERAGE_KEEP=0.9

def per_device(n_graph, n_col, features, blocks, block_values, group_sizes, labels, pair_nodes, weight_first, weight_second, weight_head,
               norm_params, momentum_first, momentum_second, momentum_head, momentum_norms, average_first, average_second,
               average_head, average_norms):
    MY=weight_first.shape[2]; H=MY*n_col; CLS=weight_head.shape[2]; CP=-(-CLS//16)*16
    G=group_sizes.shape[0]; N=features.shape[2]; NB=N//128; PEER=pair_nodes.shape[3]
    def native(first,second,head,norms):
        return first.transpose(0,2,1),second.transpose(0,2,1),head.transpose(2,0,1),norms
    weights=native(weight_first,weight_second,weight_head,norm_params)
    momenta=native(momentum_first,momentum_second,momentum_head,momentum_norms)
    averages=native(average_first,average_second,average_head,average_norms)
    packed,half=call_kp(*weights)
    halves=[lax.ppermute(half,"col",[((j+k)%n_col,j) for j in range(n_col)]) for k in range(1,n_col)]
    sizes=group_sizes.T
    S,lists,fth,ftl,af=call_k0(sizes,blocks[0],features.transpose(1,0,2),block_values[0])
    w1,w2,wh,npar,wt,w2m,ncol=call_kw(packed,halves,H,CP)
    pairs=pair_nodes[0].reshape(2*G,PEER)
    h1h,h1l,pre,pre1,st,h2t,lg,own=call_kb(sizes,lists,S,fth,ftl,af,w1,w2,wh,npar,pairs,MY=MY,CP=CP)
    recv=call_kx(own.reshape(G,2*PEER,128),n_graph)
    unit=8*n_graph; rows=-(-(2*H//128*MY+3*MY+8)//unit)*unit
    g=call_kc(sizes,lists,S,fth,ftl,af,h1h,h1l,pre,pre1,h2t,lg,st,own,recv,labels[0].reshape(NB,1,128),pairs,wt,w2m,npar,ncol,CLS=CLS,rows=rows)
    g=call_kr(g,n_graph)
    *new,loss,count=call_ku(sizes,g,weights,momenta,averages)
    first=[x.transpose(0,2,1) for x in new[0:3]]
    second=[x.transpose(0,2,1) for x in new[3:6]]
    head=[x.transpose(1,2,0) for x in new[6:9]]
    return (loss[0,0],count[0,0],*first,*second,*head,*new[9:12])

def solution(mesh):
    P=jax.sharding.PartitionSpec
    unit=P(None,None,"col"); head=P(None,"col",None)
    weights=(unit,unit,head,unit)
    in_specs=(P("graph",None,None),P("graph",None,None),P("graph",None,None,None),P(),P("graph",None),P("graph",None,None,None))+weights*3
    out_specs=(P(),P())+(unit,)*6+(head,)*3+(unit,)*3
    return jax.shard_map(functools.partial(per_device,mesh.shape["graph"],mesh.shape["col"]),mesh=mesh,in_specs=in_specs,out_specs=out_specs,check_vma=False)
```

```python
import functools
import jax, jax.numpy as jnp
from jax import lax
from jax.experimental import pallas as pl
from jax.experimental.pallas import tpu as pltpu
BF=jnp.bfloat16; F32=jnp.float32; I32=jnp.int32
VLIM0=58<<20
VLIM=31<<20
def dot(a,b): return jnp.dot(a,b,preferred_element_type=F32)
def dot_nt(a,b): return lax.dot_general(a,b,(((1,),(1,)),((),())),preferred_element_type=F32)
def split(x):
    h=x.astype(BF); return h,(x-h.astype(F32)).astype(BF)
GROUP=32
GP=16

def my_sizes(sizes):
    me=lax.axis_index("graph")
    total=sizes[0,0]
    for g in range(1,sizes.shape[1]): total+=sizes[0,g]
    return sizes[0,me]>>7, sizes[1,me], total

def sort_list(keys_l, keys_c, enc, lb, null, L):
    BLK=keys_l.shape[1]
    b_c=lax.broadcasted_iota(I32,(BLK,1),0); b_l=lax.broadcasted_iota(I32,(1,BLK),1)
    live=b_c<lb
    r_l=lax.broadcasted_iota(I32,(1,128),1); p_l=lax.broadcasted_iota(I32,(1,L),1)
    rank=jnp.sum(jnp.where((keys_l==keys_c)&(b_l<b_c),1.0,0.0),axis=1,keepdims=True)
    cnt=jnp.sum(jnp.where((keys_c==r_l)&live,1.0,0.0),axis=0,keepdims=True)
    even=2.0*jnp.floor(0.5*cnt+0.5)
    start=jnp.sum(jnp.where(r_l<keys_c,even,0.0),axis=1,keepdims=True)
    pos=jnp.where(live,(start+rank).astype(I32),-1)
    enc=enc-null; here=pos==p_l
    lo=jnp.sum(jnp.where(here,(enc&0xfff).astype(F32),0.0),axis=0,keepdims=True).astype(I32)
    hi=jnp.sum(jnp.where(here,(enc>>12).astype(F32),0.0),axis=0,keepdims=True).astype(I32)
    return hi*4096+lo+null,pos,jnp.sum(even,axis=1,keepdims=True).astype(I32)

def pair_fields(lists, which, q):
    e0=lists[which,2*q]; e1=lists[which,2*q+1]
    return e0>>20, (e0>>12)&0xff, (e1>>12)&0xff, e0&0xfff, e1&0xfff

def agg_nodes(lists, S, v, acc, lanes=slice(None)):
    n=lists[2,0]//2
    def step(s,_):
        for u in range(GROUP):
            q=s*GROUP+u
            r,c0,c1,_,_=pair_fields(lists,0,q)
            rhs=jnp.concatenate([v[c0],v[c1]],axis=0)
            acc[r,:,lanes]+=dot(jnp.concatenate([S[2*q],S[2*q+1]],axis=1),rhs)
        return 0
    lax.fori_loop(0,pl.cdiv(n,GROUP),step,0)

def load_S(lists, S_in, S, sems):
    n=2*pl.cdiv(lists[2,0],4*GP)
    def one(i): return pltpu.make_async_copy(S_in.at[pl.ds(i*2*GP,2*GP)],S.at[pl.ds(i*2*GP,2*GP)],sems.at[i])
    def start(): lax.fori_loop(0,n,lambda i,_:(one(i).start(),0)[1],0)
    def wait(): lax.fori_loop(0,n,lambda i,_:(one(i).wait(),0)[1],0)
    return start,wait

def in_vmem(*arrays): return [pltpu.with_memory_space_constraint(x,pltpu.VMEM) for x in arrays]

def agg_rows(lists, S, v, acc, rows=slice(None)):
    n=lists[3,0]//2
    def step(s,_):
        for u in range(GROUP):
            r,c0,c1,b0,b1=pair_fields(lists,1,s*GROUP+u)
            lhs=jnp.concatenate([v[c0],v[c1]],axis=1)
            acc[r,rows]+=dot(lhs,jnp.concatenate([S[b0],S[b1]],axis=0))
        return 0
    lax.fori_loop(0,pl.cdiv(n,GROUP),step,0)

def k0(sizes, blk_l, feat, vals, S_out, lists_out, fth_out, ftl_out, af_out,
       lists_v, lists_s, ft_v, fth, ftl, af, acc, buf, even, odd, ring, sem_in, sem_f, sem_l, sem_o, sem_S):
    nb,lb,_=my_sizes(sizes)
    NB=acc.shape[0]-1; BLK=vals.shape[0]; FIN=feat.shape[0]; NBUF=buf.shape[0]; NOUT=ring.shape[0]; SL=S_out.shape[0]
    L=lists_v.shape[1]; W=2*GP
    cf=pltpu.make_async_copy(feat.at[:,0],ft_v,sem_f); cf.start()
    ids=blk_l[...]
    columns=jnp.concatenate([ids.astype(F32),jnp.zeros((6,BLK),F32)],axis=0).T.astype(I32)
    rows=columns[:,0:1]; cols=columns[:,1:2]
    order=lax.broadcasted_iota(I32,(BLK,1),0)
    l0,pos,n0=sort_list(ids[0:1],rows,order+cols*(1<<12)+rows*(1<<20),lb,BLK+(NB<<20),L)
    lists_v[0:1,:]=l0; lists_v[2:3,:]=jnp.broadcast_to(n0,(1,L))
    cl=pltpu.make_async_copy(lists_v,lists_s,sem_l.at[0]); cl.start()
    acc[...]=jnp.zeros(acc.shape,F32)
    cl.wait()
    n=2*pl.cdiv(lists_s[2,0],4*GP)
    def chunk_start(i):
        slot=lax.rem(i,NBUF)
        for k in range(W):
            b=lists_s[0,i*W+k]&0xfff
            pltpu.make_async_copy(vals.at[jnp.where(b<BLK,b,0)],buf.at[slot,k],sem_in.at[slot]).start()
    def chunk_wait(i):
        slot=lax.rem(i,NBUF)
        pltpu.make_async_copy(vals.at[pl.ds(0,W)],buf.at[slot],sem_in.at[slot]).wait()
    lax.fori_loop(0,jnp.minimum(n,NBUF),lambda i,_:(chunk_start(i),0)[1],0)
    l1,_,n1=sort_list(ids[1:2],cols,pos+rows*(1<<12)+cols*(1<<20),lb,SL+(NB<<20),L)
    lists_v[1:2,:]=l1; lists_v[3:4,:]=jnp.broadcast_to(n1,(1,L))
    co=pltpu.make_async_copy(lists_v,lists_out,sem_l.at[1]); co.start()
    cf.wait()
    def tr(i,_):
        for k in range(4):
            b=i*4+k
            x=ft_v[:,pl.ds(pl.multiple_of(b*128,128),128)]
            x=jnp.concatenate([x,jnp.zeros((128-FIN,128),F32)],axis=0).T
            h,l=split(x); fth[b]=h; ftl[b]=l
        return 0
    lax.fori_loop(0,pl.cdiv(nb,4),tr,0)
    c1=pltpu.make_async_copy(fth,fth_out,sem_o.at[0]); c1.start()
    c2=pltpu.make_async_copy(ftl,ftl_out,sem_o.at[1]); c2.start()
    def chunk_out(i): return pltpu.make_async_copy(ring.at[lax.rem(i,NOUT)],S_out.at[pl.ds(i*W,W)],sem_S.at[lax.rem(i,NOUT)])
    def convert(i,stage):
        slot=lax.rem(i,NBUF); o=lax.rem(i,NOUT)
        chunk_wait(i)
        for k in range(W):
            x=jnp.where(lists_s[0,i*W+k]&0xfff<BLK,buf[slot,k],0.0).T.astype(BF)
            stage[k]=x; ring[o,k]=x
    def dots(i,stage):
        for u in range(GP):
            r,f0,f1,_,_=pair_fields(lists_s,0,i*GP+u)
            acc[r]+=dot(jnp.concatenate([stage[2*u],stage[2*u+1]],axis=1),jnp.concatenate([fth[f0],fth[f1]],axis=0))
    def refill(i):
        chunk_out(i).start()
        @pl.when(i+NBUF<n)
        def _(): chunk_start(i+NBUF)
        @pl.when(i+1>=NOUT)
        def _(): chunk_out(i+1-NOUT).wait()
    convert(0,even); refill(0)
    def step(j,_):
        convert(2*j+1,odd); dots(2*j,even); refill(2*j+1)
        convert(2*j+2,even); dots(2*j+1,odd); refill(2*j+2)
        return 0
    lax.fori_loop(0,n//2-1,step,0)
    convert(n-1,odd); chunk_out(n-1).start(); dots(n-2,even); dots(n-1,odd)
    def fin(b,_):
        for k in range(4): af[b*4+k]=acc[b*4+k].astype(BF)
        return 0
    lax.fori_loop(0,pl.cdiv(nb,4),fin,0)
    c3=pltpu.make_async_copy(af,af_out,sem_o.at[2]); c3.start()
    lax.fori_loop(jnp.maximum(n-NOUT,0),n,lambda i,_:(chunk_out(i).wait(),0)[1],0)
    c1.wait();c2.wait();c3.wait();co.wait()

def call_k0(sizes, blk, feat, vals, NBUF=8, NOUT=4):
    FIN,_,N=feat.shape; NB=N//128; BLK=vals.shape[0]; L=pl.cdiv(BLK+NB,128)*128; W=2*GP; SL=pl.cdiv(BLK+NB,2*GROUP)*2*GROUP
    sds=jax.ShapeDtypeStruct
    ANY=pl.BlockSpec(memory_space=pltpu.HBM); VM=pl.BlockSpec(memory_space=pltpu.VMEM); SM=pl.BlockSpec(memory_space=pltpu.SMEM)
    V=pltpu.VMEM; D=pltpu.SemaphoreType.DMA
    return pl.pallas_call(k0,
        out_shape=(pltpu.HBM((SL,128,128),BF),pltpu.HBM((8,L),I32),*[pltpu.HBM((NB,128,128),BF)]*3),
        in_specs=[SM,VM,ANY,ANY],out_specs=[ANY]*5,
        scratch_shapes=[V((8,L),I32),pltpu.SMEM((8,L),I32),V((FIN,N),F32),*[V((NB,128,128),BF)]*3,V((NB+1,128,128),F32),
            V((NBUF,W,128,128),F32),V((W,128,128),BF),V((W,128,128),BF),V((NOUT,W,128,128),BF),
            D((NBUF,)),D(()),D((2,)),D((3,)),D((NOUT,))],
        compiler_params=pltpu.CompilerParams(vmem_limit_bytes=VLIM0))(sizes,blk,feat,vals)
G0=0.7978845608; G1=0.044715
EPS=1e-5
HP=64
def for_blocks(nb,U,fn,start=0):
    full=nb//U
    def many(s,_): fn(s*U,U); return 0
    def one(b,_): fn(b,1); return 0
    lax.fori_loop(start,full,many,0)
    if U>1: lax.fori_loop(full*U,nb,one,0)
def rows8(x): return jnp.sum(x.reshape(x.shape[0]//8,8,x.shape[1]),axis=0)
def blk(ref,b0,U):
    x=ref[pl.ds(b0,U)]; return x.reshape(U*x.shape[1],x.shape[2])
def put_blk(ref,b0,U,x): ref[pl.ds(b0,U)]=x.reshape((U,)+ref.shape[1:])
def gelu_half(w):
    return w+w*jnp.tanh(w*(2.0*G0+(8.0*G0*G1)*(w*w)))
def dgelu_half(w):
    q=w*w
    t=jnp.tanh(w*(2.0*G0+(8.0*G0*G1)*q))
    return (1.0+t)*(0.5+(w*(G0+(12.0*G0*G1)*q))*(1.0-t))

def moments(sums,shift,count):
    d=jnp.sum(sums[0],axis=0,keepdims=True)/count
    v=jnp.sum(sums[1],axis=0,keepdims=True)/count-d*d
    return shift+d,lax.rsqrt(v+EPS)

def slot_nodes(pairs):
    R,K=pairs.shape; G=R//2
    x=jnp.concatenate([pairs[...].astype(F32),jnp.zeros((R,128-K),F32)],axis=1)
    if R%128: x=jnp.concatenate([x,jnp.zeros((128-R%128,128),F32)],axis=0)
    x=x.T[:K].astype(I32)
    return jnp.concatenate([x[:,t*G+g:t*G+g+1] for g in range(G) for t in range(2)],axis=0)
def one_hot(slots,b):
    return jnp.where(slots==lax.broadcasted_iota(I32,(1,128),1)+b*128,1.0,0.0).astype(BF)

def kb(sizes,lists,pairs,S_in,fth_in,ftl_in,af_in,w1,w2,wh,npar,
       h1h_out,h1l_out,pre,pre1,st,h2t,lg,own_out,S,
       fth,ftl,af,h1h,h1l,acc,zz,sums,sem_i,sem_o,sem_S):
    nb,_,_=my_sizes(sizes); NB=fth.shape[0]; CP=lg.shape[1]; MY=pre1.shape[1]
    count=(nb*128).astype(F32)
    cs=[pltpu.make_async_copy(a,b,sem_i.at[i]) for i,(a,b) in enumerate(((fth_in,fth),(ftl_in,ftl),(af_in,af)))]
    for c in cs: c.start()
    S_start,S_wait=load_S(lists,S_in,S,sem_S); S_start()
    S[S_in.shape[0]]=jnp.zeros((128,128),BF)
    st[...]=jnp.zeros_like(st)
    for c in cs: c.wait()
    def first(b0,U):
        h=blk(fth,b0,U)
        x=jnp.concatenate([h,blk(ftl,b0,U),h,blk(af,b0,U)],axis=1)
        return dot_nt(x,w1[...])
    def second(b0,U):
        h=blk(h1h,b0,U); l=blk(h1l,b0,U); ah,al=split(blk(acc,b0,U))
        return dot_nt(jnp.concatenate([h,l,h,ah,al,ah],axis=1),w2[...])
    def layer(fn,mine):
        shift=jnp.sum(fn(0,1),axis=0,keepdims=True)/128.0
        sums[...]=jnp.zeros_like(sums)
        def tile(b0,U):
            y=fn(b0,U)
            put_blk(pre,b0,U,y)
            if mine:
                for k in range(U): pre1[b0+k]=y[k*128:k*128+128,:MY].T
            d=y-shift
            sums[0]+=rows8(d); sums[1]+=rows8(d*d)
        for_blocks(nb,8,tile)
        return moments(sums,shift,count)
    mean,inv=layer(first,True)
    st[0:1,:]=mean; st[1:2,:]=inv
    a=npar[0:1,:]*inv; c=npar[1:2,:]-mean*a
    a=0.5*a; c=0.5*c
    def n1(b0,U):
        h,l=split(gelu_half(blk(pre,b0,U)*a+c))
        put_blk(h1h,b0,U,h); put_blk(h1l,b0,U,l)
        put_blk(acc,b0,U,jnp.zeros((U*128,acc.shape[2]),F32))
    for_blocks(nb,4,n1)
    acc[NB]=jnp.zeros(acc.shape[1:],F32)
    outs=[pltpu.make_async_copy(x,y,sem_o.at[i]) for i,(x,y) in enumerate(((h1h,h1h_out),(h1l,h1l_out)))]
    for o in outs: o.start()
    S_wait()
    agg_nodes(lists,S,h1h,acc)
    mean2,inv2=layer(second,False)
    st[2:3,:]=mean2; st[3:4,:]=inv2
    a2=npar[2:3,:]*inv2; c2=npar[3:4,:]-mean2*a2
    a2=0.5*a2; c2=0.5*c2
    def n2(b0,U):
        h,l=split(gelu_half(blk(pre,b0,U)*a2+c2))
        r=dot_nt(h,wh[...])
        dz=r[:,:2*HP]+r[:,2*HP:]+dot_nt(l,wh[0:2*HP,:])
        zh,zl=split(dz)
        put_blk(zz,b0,U,jnp.concatenate([zh[:,HP:],zl[:,HP:]],axis=1))
        put_blk(acc,b0,U,jnp.concatenate([dz,jnp.zeros_like(dz)],axis=1))
        t=jnp.concatenate([h[:,:MY],l[:,:MY]],axis=1)
        for k in range(U): h2t[b0+k]=t[k*128:k*128+128].T
    for_blocks(nb,8,n2)
    agg_nodes(lists,S,zz,acc,slice(2*HP,4*HP))
    def fin(b0,U):
        for k in range(U):
            x=acc[b0+k]; s=x[:,2*HP:]
            y=x[:,:2*HP]+s+pltpu.roll(s,HP,1)
            acc[b0+k,:,:2*HP]=y
            lg[b0+k]=y.T[:CP]
    for_blocks(nb,8,fin)
    G=pairs.shape[0]//2; K=pairs.shape[1]
    lane=lax.broadcasted_iota(I32,(1,128),1); sub=lax.broadcasted_iota(I32,(8,1),0)
    def slot(g,_):
        for t in range(2):
            for k0 in range(0,K,8):
                o=jnp.zeros((8,128),F32)
                for k in range(8):
                    n=pairs[t*G+g,k0+k]
                    x=acc[n>>7,pl.ds(pl.multiple_of(((n>>3)&15)*8,8),8),:2*HP]
                    o=jnp.where(sub==k,jnp.sum(jnp.where(sub==(n&7),x,0.0),axis=0,keepdims=True),o)
                own_out[g,pl.ds(pl.multiple_of(t*K+k0,8),8),:]=jnp.where(lane<CP,o,0.0)
        return 0
    lax.fori_loop(0,G,slot,0)
    for o in outs: o.wait()

def call_kb(sizes,lists,S,fth,ftl,af,w1,w2,wh,npar,pairs,MY,CP):
    NB=fth.shape[0]; H=w2.shape[0]; SL=S.shape[0]; G=pairs.shape[0]//2; K=pairs.shape[1]
    sds=jax.ShapeDtypeStruct
    ANY=pl.BlockSpec(memory_space=pltpu.HBM); VM=pl.BlockSpec(memory_space=pltpu.VMEM); SM=pl.BlockSpec(memory_space=pltpu.SMEM)
    V=pltpu.VMEM
    return pl.pallas_call(kb,
        out_shape=(pltpu.HBM((NB,128,H),BF),pltpu.HBM((NB,128,H),BF),V((NB,128,H),F32),V((NB,MY,128),F32),sds((8,H),F32),V((NB,2*MY,128),BF),V((NB,CP,128),F32),V((G,2*K,128),F32),V((SL+1,128,128),BF)),
        in_specs=[SM]*3+[ANY]*4+[VM]*4,out_specs=[ANY]*2+[VM]*7,
        scratch_shapes=[V((NB,128,128),BF)]*3+[V((NB,128,H),BF)]*2+[V((NB+1,128,H),F32),V((NB,128,2*HP),BF),V((2,8,H),F32),pltpu.SemaphoreType.DMA((3,)),pltpu.SemaphoreType.DMA((2,)),pltpu.SemaphoreType.DMA((SL//(2*GP),))],
        compiler_params=pltpu.CompilerParams(vmem_limit_bytes=VLIM))(sizes,lists,pairs,S,fth,ftl,af,w1,w2,wh,npar)


def kc(sizes,lists,S,pre,pre1,h2t,lg,h1h_in,h1l_in,fth_in,ftl_in,af_in,st,own,recv,labels,pairs,wt,w2m,npar,ncol,
       g_out,
       rh,rl,rfh,rfl,raf,du,gz,acc,v4,sums,cross,RH,RS,RL,R1,R2,colsum,sem_r,CLS):
    nb,_,nodes=my_sizes(sizes); NB=pre.shape[0]; CP=lg.shape[1]; MY=ncol.shape[0]; H=pre.shape[2]; NS=rh.shape[0]; U8=rh.shape[1]
    count=(nb*128).astype(F32); total=nodes.astype(F32)
    nch=pl.cdiv(nb,U8)
    def ring(i):
        s=lax.rem(i,NS)
        return [pltpu.make_async_copy(a.at[pl.ds(i*U8,U8)],b.at[s],sem_r.at[s,k]) for k,(a,b) in enumerate(((h1h_in,rh),(h1l_in,rl),(fth_in,rfh),(ftl_in,rfl),(af_in,raf)))]
    for i in range(NS):
        @pl.when(i<nch)
        def _():
            for c in ring(i): c.start()
    for r in (sums,cross,RH,RS,RL,R1,R2,colsum): r[...]=jnp.zeros_like(r)
    acc[NB]=jnp.zeros(acc.shape[1:],F32)
    half=pairs.shape[1]
    G=pairs.shape[0]//2
    r=recv[...]
    D=own[...]-jnp.concatenate([r[:,half:],r[:,:half]],axis=1)
    pair_loss=0.5*jnp.sum(D[:,half:]*D[:,half:])
    Dh,Dl=split((D.reshape(2*G*half,128).T)[:CP]/total); D2=jnp.concatenate([Dh,Dl],axis=0)
    slots=slot_nodes(pairs)
    def soft(b0,U):
        hot=jnp.concatenate([one_hot(slots,b0+k) for k in range(U)],axis=1)
        add=dot(D2,hot); add=add[:CP]+add[CP:]
        x=jnp.concatenate([lg[b0+k] for k in range(U)],axis=1)
        lab=jnp.concatenate([labels[b0+k] for k in range(U)],axis=1)
        row=lax.broadcasted_iota(I32,(CP,1),0)
        xm=jnp.where(row<CLS,x,-1e30)
        mx=jnp.max(xm,axis=0,keepdims=True)
        e=jnp.exp(xm-mx); s=jnp.sum(e,axis=0,keepdims=True)
        hit=jnp.where(row==lab,1.0,0.0)
        c=mx+jnp.log(s)-jnp.sum(hit*x,axis=0,keepdims=True)
        g=(e/s-hit)/total+add
        h,l=split(g)
        for k in range(U):
            w=slice(k*128,k*128+128)
            cross[...]+=c[:,w]
            gz[b0+k]=jnp.concatenate([h[:,w],l[:,w]],axis=0)
            acc[b0+k,:2*CP]=jnp.zeros((2*CP,128),F32)
    for_blocks(nb,4,soft)
    agg_rows(lists,S,gz,acc,slice(0,2*CP))
    mean2=st[2:3,:]; inv2=st[3:4,:]
    a2=npar[2:3,:]*inv2; c2=npar[3:4,:]-mean2*a2
    ha2=0.5*a2; hc2=0.5*c2
    def back2(b0,U):
        th=[];tl=[];ads=[]
        z=jnp.zeros((128-2*CP,128),BF)
        for k in range(U):
            ad=acc[b0+k,:2*CP]; ah,al=split(ad[:CP]+ad[CP:]); gk=gz[b0+k]
            th.append(jnp.concatenate([gk[:CP],ah,z],axis=0).T); tl.append(jnp.concatenate([gk[CP:],al,z],axis=0).T)
            ads.append(ah)
        th=jnp.concatenate(th,axis=0); tl=jnp.concatenate(tl,axis=0)
        gh=dot(jnp.concatenate([th,tl,th],axis=1),wt[...])
        hh=jnp.concatenate([h2t[b0+k] for k in range(U)],axis=1)
        gg=jnp.concatenate([jnp.concatenate([gz[b0+k] for k in range(U)],axis=1),jnp.concatenate(ads,axis=1)],axis=0)
        RH[...]+=dot_nt(hh,gg)
        y=blk(pre,b0,U)
        d=gh*dgelu_half(y*ha2+hc2)
        put_blk(du,b0,U,d)
        sums[0]+=rows8(d); sums[1]+=rows8(d*(y-mean2))
    for_blocks(nb,8,back2)
    sb2=jnp.sum(sums[0],axis=0,keepdims=True); sg2=jnp.sum(sums[1],axis=0,keepdims=True)*inv2
    A2=-a2*inv2*sg2/count; C2=-a2*sb2/count-A2*mean2
    def proj(b0,U):
        h,l=split(blk(du,b0,U)*a2+blk(pre,b0,U)*A2+C2)
        r=dot_nt(w2m[...],h); rl2=dot_nt(w2m[0:MY,:],l)
        d=r[:MY]+r[MY:2*MY]+rl2; t=(r[2*MY:3*MY]+r[3*MY:]).astype(BF)
        gt=jnp.concatenate([h[:,:MY],l[:,:MY]],axis=1)
        for k in range(U):
            w=slice(k*128,k*128+128)
            acc[b0+k]=jnp.concatenate([d[:,w],jnp.zeros((2*MY,128),F32)],axis=0)
            v4[b0+k]=jnp.concatenate([t[:,w],gt[w].T],axis=0)
    for_blocks(nb,8,proj)
    acc[NB]=jnp.zeros(acc.shape[1:],F32)
    agg_rows(lists,S,v4,acc)
    lane=lambda x: jnp.sum(x,axis=1,keepdims=True)
    stc=st[:,:128].T[:MY]
    mean1=stc[:,0:1]; inv1=stc[:,1:2]
    a1=ncol[:,0:1]*inv1; c1=ncol[:,1:2]-mean1*a1
    ha1=0.5*a1; hc1=0.5*c1
    def back1(b0,U):
        for k in range(U):
            p=pre1[b0+k]
            d=acc[b0+k,:MY]*dgelu_half(p*ha1+hc1)
            acc[b0+k,:MY]=d
            colsum[0]+=d; colsum[1]+=d*(p-mean1)
    for_blocks(nb,4,back1)
    sb1=lane(colsum[0]); sg1=lane(colsum[1])*inv1
    A1=-a1*inv1*sg1/count; C1=-a1*sb1/count-A1*mean1
    def last(i,_):
        s=lax.rem(i,NS)
        for c in ring(i): c.wait()
        def part(b0,off,U):
            f=lambda ref: ref[s,pl.ds(off,U)].reshape(U*128,ref.shape[3])
            x=[acc[b0+k] for k in range(U)]
            gh,gl=split(jnp.concatenate([x[k][:MY]*a1+pre1[b0+k]*A1+C1 for k in range(U)],axis=1))
            R1[...]+=dot(jnp.concatenate([gh,gl],axis=0),f(rfh))
            R2[...]+=dot(gh,jnp.concatenate([f(rfl),f(raf)],axis=1))
            ah,al=split(jnp.concatenate([x[k][MY:2*MY]+x[k][2*MY:] for k in range(U)],axis=1))
            gt=jnp.concatenate([v4[b0+k,MY:] for k in range(U)],axis=1)
            RS[...]+=dot(jnp.concatenate([gt,ah,al],axis=0),f(rh))
            RL[...]+=dot(jnp.concatenate([gt[:MY],ah],axis=0),f(rl))
        @pl.when((i+1)*U8<=nb)
        def _(): part(i*U8,0,U8)
        @pl.when((i+1)*U8>nb)
        def _():
            lax.fori_loop(0,nb-i*U8,lambda k,_:(part(i*U8+k,k,1),0)[1],0)
        @pl.when(i+NS<nch)
        def _():
            for c in ring(i+NS): c.start()
        return 0
    lax.fori_loop(0,nch,last,0)
    RSv=RS[...]; RLv=RL[...]; nk=H//128
    for h in range(2):
        gs=RSv[2*h*MY:(2*h+1)*MY]+RSv[(2*h+1)*MY:(2*h+2)*MY]+RLv[h*MY:(h+1)*MY]
        for k in range(nk): g_out[(h*nk+k)*MY:(h*nk+k+1)*MY,:]=gs[:,k*128:k*128+128]
    R1v=R1[...]; R2v=R2[...]
    q=2*nk*MY
    g_out[q:q+MY,:]=R1v[:MY]+R1v[MY:]+R2v[:,:128]
    g_out[q+MY:q+2*MY,:]=R2v[:,128:]
    RHv=RH[...]; gh=RHv[:MY]+RHv[MY:]
    gh=jnp.concatenate([RHv[:MY,:CP]+RHv[:MY,CP:2*CP]+RHv[MY:,:CP],gh[:,2*CP:3*CP],sg1,sb1,jnp.zeros((MY,128-2*CP-2),F32)],axis=1)
    g_out[q+2*MY:q+3*MY,:]=gh
    loss=jnp.sum(cross[...])+pair_loss
    pad=[jnp.zeros((1,128-MY),F32)]
    g_out[q+3*MY:,:]=jnp.zeros((g_out.shape[0]-q-3*MY,128),F32)
    g_out[q+3*MY:q+3*MY+8,:]=jnp.concatenate([jnp.concatenate([sg2[:,:MY]]+pad,axis=1),jnp.concatenate([sb2[:,:MY]]+pad,axis=1),jnp.broadcast_to(loss,(1,128)),jnp.zeros((5,128),F32)],axis=0)

def call_kc(sizes,lists,S,fth,ftl,af,h1h,h1l,pre,pre1,h2t,lg,st,own,recv,labels,pairs,wt,w2m,npar,ncol,CLS,rows):
    NB=fth.shape[0]; H=pre.shape[2]; CP=lg.shape[1]; MY=ncol.shape[0]; NS=3; U8=8
    ANY=pl.BlockSpec(memory_space=pltpu.HBM); VM=pl.BlockSpec(memory_space=pltpu.VMEM); SM=pl.BlockSpec(memory_space=pltpu.SMEM)
    V=pltpu.VMEM
    return pl.pallas_call(functools.partial(kc,CLS=CLS),out_shape=jax.ShapeDtypeStruct((rows,128),F32),
        in_specs=[SM,SM]+[VM]*5+[ANY]*5+[VM]*9,out_specs=VM,
        scratch_shapes=[V((NS,U8,128,H),BF)]*2+[V((NS,U8,128,128),BF)]*3+[
            V((NB,128,H),F32),V((NB,2*CP,128),BF),V((NB+1,max(3*MY,2*CP),128),F32),V((NB,3*MY,128),BF),
            V((2,8,H),F32),V((1,128),F32),V((2*MY,3*CP),F32),V((4*MY,H),F32),V((2*MY,H),F32),V((2*MY,128),F32),V((MY,256),F32),V((2,MY,128),F32),
            pltpu.SemaphoreType.DMA((NS,5))],
        compiler_params=pltpu.CompilerParams(vmem_limit_bytes=VLIM))(sizes,lists,*in_vmem(S,pre,pre1,h2t,lg),h1h,h1l,fth,ftl,af,st,*in_vmem(own,recv),labels,pairs,wt,w2m,npar,ncol)

def at(index): return {"graph": index}
def meet(n):
    me=lax.axis_index("graph")
    barrier=pltpu.get_barrier_semaphore()
    for k in range(1,n):
        pl.semaphore_signal(barrier,inc=1,device_id=at(lax.rem(me+k,n)),device_id_type=pl.DeviceIdType.MESH)
    pl.semaphore_wait(barrier,n-1)

def kx(own,out,send,recv,n):
    me=lax.axis_index("graph")
    meet(n)
    copies=[]
    for k in range(1,n):
        peer=lax.rem(me+k,n)
        c=pltpu.make_async_remote_copy(src_ref=own.at[peer],dst_ref=out.at[me],send_sem=send.at[k-1],recv_sem=recv.at[k-1],
            device_id=at(peer),device_id_type=pl.DeviceIdType.MESH)
        c.start(); copies.append(c)
    out[me]=own[me]
    for c in copies: c.wait()

def call_kx(own,n):
    VM=pl.BlockSpec(memory_space=pltpu.VMEM)
    return pl.pallas_call(functools.partial(kx,n=n),out_shape=pltpu.VMEM(own.shape,own.dtype),in_specs=[VM],out_specs=VM,
        scratch_shapes=[pltpu.SemaphoreType.DMA((n-1,)),pltpu.SemaphoreType.DMA((n-1,))],
        compiler_params=pltpu.CompilerParams(vmem_limit_bytes=8<<20,collective_id=1,has_side_effects=True))(*in_vmem(own))

def kr(g,out,parts,send1,recv1,send2,recv2,n):
    me=lax.axis_index("graph")
    piece=g.shape[0]//n
    def rows(i): return pl.ds(pl.multiple_of(i*piece,8),piece)
    meet(n)
    copies=[]
    for k in range(1,n):
        peer=lax.rem(me+k,n)
        c=pltpu.make_async_remote_copy(src_ref=g.at[rows(peer)],dst_ref=parts.at[k-1],send_sem=send1.at[k-1],recv_sem=recv1.at[k-1],
            device_id=at(peer),device_id_type=pl.DeviceIdType.MESH)
        c.start(); copies.append(c)
    total=g[rows(me),:]
    for k,c in enumerate(copies):
        c.wait_recv(); total+=parts[k]
    out[rows(me),:]=total
    back=[]
    for k in range(1,n):
        peer=lax.rem(me+k,n)
        c=pltpu.make_async_remote_copy(src_ref=out.at[rows(me)],dst_ref=out.at[rows(me)],send_sem=send2.at[k-1],recv_sem=recv2.at[k-1],
            device_id=at(peer),device_id_type=pl.DeviceIdType.MESH)
        c.start(); back.append(c)
    for c in copies: c.wait_send()
    for c in back: c.wait()

def call_kr(g,n):
    VM=pl.BlockSpec(memory_space=pltpu.VMEM); D=pltpu.SemaphoreType.DMA((n-1,))
    return pl.pallas_call(functools.partial(kr,n=n),out_shape=jax.ShapeDtypeStruct(g.shape,g.dtype),in_specs=[VM],out_specs=VM,
        scratch_shapes=[pltpu.VMEM((n-1,g.shape[0]//n,128),F32),D,D,D,D],
        compiler_params=pltpu.CompilerParams(collective_id=2,has_side_effects=True))(g)

def kp(wf,ws,wh,npar,out,half):
    _,MY,FIN=wf.shape; H=ws.shape[2]; CLS=wh.shape[0]; CP=-(-CLS//16)*16; nk=H//128
    out[...]=jnp.zeros_like(out)
    for h in range(2):
        for k in range(nk):
            r=(h*nk+k)*MY; out[r:r+MY,:]=ws[h,:,k*128:k*128+128]
        r=2*nk*MY+h*MY; out[r:r+MY,:FIN]=wf[h]
        r=2*nk*MY+2*MY+h*CP; out[r:r+CLS,:MY]=wh[:,h,:]
        r=2*nk*MY+2*MY+2*CP+2*h; out[r:r+2,:MY]=npar[h]
    core=lax.rem(lax.axis_index("graph"),2); n=half.shape[0]
    half[...]=out[pl.ds(pl.multiple_of(core*n,8),n),:]

def call_kp(wf,ws,wh,npar):
    _,MY,FIN=wf.shape; H=ws.shape[2]; CP=-(-wh.shape[0]//16)*16
    rows=-(-(2*H//128*MY+2*MY+2*CP+8)//16)*16
    VM=pl.BlockSpec(memory_space=pltpu.VMEM)
    return pl.pallas_call(kp,out_shape=(jax.ShapeDtypeStruct((rows,128),F32),jax.ShapeDtypeStruct((rows//2,128),F32)),in_specs=[VM]*4,out_specs=[VM]*2)(wf,ws,wh,npar)

def kw(own,*refs,n_col,CP):
    halves=refs[:n_col-1]; w1_out,w2_out,wh_out,npar_out,wt_out,w2m_out,ncol_out,x,send,recv=refs[n_col-1:]
    me=lax.axis_index("graph"); core=lax.rem(me,2); twin=me+1-2*core
    barrier=pltpu.get_barrier_semaphore()
    pl.semaphore_signal(barrier,inc=1,device_id=at(twin),device_id_type=pl.DeviceIdType.MESH)
    n=own.shape[0]//2; rows=pl.ds(pl.multiple_of(core*n,8),n)
    pl.semaphore_wait(barrier,1)
    copies=[]
    for k in range(1,n_col):
        c=pltpu.make_async_remote_copy(src_ref=halves[k-1],dst_ref=x.at[k,rows],send_sem=send.at[k-1],recv_sem=recv.at[k-1],
            device_id=at(twin),device_id_type=pl.DeviceIdType.MESH)
        c.start(); copies.append(c)
    x[0]=own[...]
    for k in range(1,n_col): x[k,rows,:]=halves[k-1][...]
    for c in copies: c.wait()
    H=w1_out.shape[0]; MY=H//n_col; nk=H//128
    col=lax.axis_index("col")
    back=lax.rem(H-col*MY,H)
    heads=([],[]); norms=[]; mine=([],[])
    for k in range(n_col):
        j=k; r=slice(k*MY,k*MY+MY)
        q=2*nk*MY
        h,l=split(x[j,q:q+MY,:])
        w1_out[r,:]=jnp.concatenate([h,h,l,x[j,q+MY:q+2*MY,:].astype(BF)],axis=1)
        two=[]
        for half in range(2):
            w=jnp.concatenate([x[j,(half*nk+i)*MY:(half*nk+i+1)*MY,:] for i in range(nk)],axis=1)
            w=pltpu.roll(w,back,1)
            mine[half].append(w[:,:128])
            h,l=split(w); two+=[h,h,l]
            heads[half].append(x[j,q+2*MY+half*CP:q+2*MY+(half+1)*CP,:MY])
        w2_out[r,:]=jnp.concatenate(two,axis=1)
        norms.append(x[j,q+2*MY+2*CP:q+2*MY+2*CP+8,:MY])
    npar=jnp.concatenate(norms,axis=1)
    npar_out[...]=npar
    ncol_out[...]=npar[:,:128].T[:MY]
    (ch,cl),(dh,dl)=[split(jnp.concatenate(p,axis=1)) for p in heads]
    z=jnp.zeros((HP-CP,H),BF)
    wh_out[...]=jnp.concatenate([ch,z,dh,z,cl,z,dl,z],axis=0)
    z=jnp.zeros((128-2*CP,H),BF)
    th=jnp.concatenate([ch,dh,z],axis=0); tl=jnp.concatenate([cl,dl,z],axis=0)
    wt_out[...]=jnp.concatenate([th,th,tl],axis=0)
    for half in range(2):
        h,l=split(jnp.concatenate(mine[half],axis=0).T[:MY])
        w2m_out[2*half*MY:(2*half+2)*MY,:]=jnp.concatenate([h,l],axis=0)

def call_kw(own,halves,H,CP):
    n_col=1+len(halves); MY=H//n_col; sds=jax.ShapeDtypeStruct; VM=pl.BlockSpec(memory_space=pltpu.VMEM)
    return pl.pallas_call(functools.partial(kw,n_col=n_col,CP=CP),
        out_shape=(sds((H,512),BF),sds((H,6*H),BF),sds((4*HP,H),BF),sds((8,H),F32),sds((384,H),BF),sds((4*MY,H),BF),sds((MY,8),F32)),
        in_specs=[VM]*n_col,out_specs=[VM]*7,
        scratch_shapes=[pltpu.VMEM((n_col,)+own.shape,F32),pltpu.SemaphoreType.DMA((n_col-1,)),pltpu.SemaphoreType.DMA((n_col-1,))],
        compiler_params=pltpu.CompilerParams(collective_id=3,has_side_effects=True))(own,*halves)

def renew(weight, momentum, average, gradient):
    momentum_new = MOMENTUM * momentum + gradient
    weight_new = weight - STEP_RATE * (gradient + MOMENTUM * momentum_new)
    average_new = AVERAGE_KEEP * average + (1.0 - AVERAGE_KEEP) * weight_new
    return momentum_new, average_new, weight_new

def ku(sizes,g,*refs):
    weights,momenta,averages,outs,loss,count=refs[:4],refs[4:8],refs[8:12],refs[12:24],refs[24],refs[25]
    _,MY,FIN=weights[0].shape; H=weights[1].shape[2]; CLS=weights[2].shape[0]; CP=-(-CLS//16)*16; nk=H//128
    q=2*nk*MY
    shift=lax.axis_index("col")*MY
    def store(i,where,grad):
        for o,v in zip(outs[3*i:3*i+3],renew(weights[i][where],momenta[i][where],averages[i][where],grad)): o[where]=v
    head=g[q+2*MY:q+3*MY,:].T
    for h in range(2):
        x=jnp.concatenate([g[(h*nk+k)*MY:(h*nk+k+1)*MY,:] for k in range(nk)],axis=1)
        store(1,(h,),pltpu.roll(x,shift,1))
        store(0,(h,),g[q+h*MY:q+h*MY+MY,:FIN])
        store(2,(slice(None),h,slice(None)),head[h*CP:h*CP+CLS,:MY])
    store(3,(0,),head[2*CP:2*CP+2,:MY])
    store(3,(1,),g[q+3*MY:q+3*MY+2,:MY])
    loss[0,0]=g[q+3*MY+2,0]
    count[0,0]=my_sizes(sizes)[2].astype(F32)

def call_ku(sizes,g,weights,momenta,averages):
    VM=pl.BlockSpec(memory_space=pltpu.VMEM); SM=pl.BlockSpec(memory_space=pltpu.SMEM)
    shapes=[jax.ShapeDtypeStruct(w.shape,F32) for w in weights for _ in range(3)]
    return pl.pallas_call(ku,out_shape=(*shapes,*[jax.ShapeDtypeStruct((1,1),F32)]*2),in_specs=[SM]+[VM]*13,out_specs=[VM]*12+[SM]*2)(sizes,g,*weights,*momenta,*averages)

MOMENTUM=0.9; STEP_RATE=2.0; AVERAGE_KEEP=0.9

def per_device(n_graph, n_col, features, blocks, block_values, group_sizes, labels, pair_nodes, weight_first, weight_second, weight_head,
               norm_params, momentum_first, momentum_second, momentum_head, momentum_norms, average_first, average_second,
               average_head, average_norms):
    MY=weight_first.shape[2]; H=MY*n_col; CLS=weight_head.shape[2]; CP=-(-CLS//16)*16
    G=group_sizes.shape[0]; N=features.shape[2]; NB=N//128; PEER=pair_nodes.shape[3]
    def native(first,second,head,norms):
        return first.transpose(0,2,1),second.transpose(0,2,1),head.transpose(2,0,1),norms
    weights=native(weight_first,weight_second,weight_head,norm_params)
    momenta=native(momentum_first,momentum_second,momentum_head,momentum_norms)
    averages=native(average_first,average_second,average_head,average_norms)
    packed,half=call_kp(*weights)
    halves=[lax.ppermute(half,"col",[((j+k)%n_col,j) for j in range(n_col)]) for k in range(1,n_col)]
    sizes=group_sizes.T
    S,lists,fth,ftl,af=call_k0(sizes,blocks[0],features.transpose(1,0,2),block_values[0])
    w1,w2,wh,npar,wt,w2m,ncol=call_kw(packed,halves,H,CP)
    pairs=pair_nodes[0].reshape(2*G,PEER)
    h1h,h1l,pre,pre1,st,h2t,lg,own,S=call_kb(sizes,lists,S,fth,ftl,af,w1,w2,wh,npar,pairs,MY=MY,CP=CP)
    recv=call_kx(own,n_graph)
    unit=8*n_graph; rows=-(-(2*H//128*MY+3*MY+8)//unit)*unit
    g=call_kc(sizes,lists,S,fth,ftl,af,h1h,h1l,pre,pre1,h2t,lg,st,own,recv,labels[0].reshape(NB,1,128),pairs,wt,w2m,npar,ncol,CLS=CLS,rows=rows)
    g=call_kr(g,n_graph)
    *new,loss,count=call_ku(sizes,g,weights,momenta,averages)
    first=[x.transpose(0,2,1) for x in new[0:3]]
    second=[x.transpose(0,2,1) for x in new[3:6]]
    head=[x.transpose(1,2,0) for x in new[6:9]]
    return (loss[0,0],count[0,0],*first,*second,*head,*new[9:12])

def solution(mesh):
    P=jax.sharding.PartitionSpec
    unit=P(None,None,"col"); head=P(None,"col",None)
    weights=(unit,unit,head,unit)
    in_specs=(P("graph",None,None),P("graph",None,None),P("graph",None,None,None),P(),P("graph",None),P("graph",None,None,None))+weights*3
    out_specs=(P(),P())+(unit,)*6+(head,)*3+(unit,)*3
    return jax.shard_map(functools.partial(per_device,mesh.shape["graph"],mesh.shape["col"]),mesh=mesh,in_specs=in_specs,out_specs=out_specs,check_vma=False)
```

```python
import functools
import jax, jax.numpy as jnp
from jax import lax
from jax.experimental import pallas as pl
from jax.experimental.pallas import tpu as pltpu
BF=jnp.bfloat16; F32=jnp.float32; I32=jnp.int32
VLIM0=58<<20
VLIM=31<<20
def dot(a,b): return jnp.dot(a,b,preferred_element_type=F32)
def dot_nt(a,b): return lax.dot_general(a,b,(((1,),(1,)),((),())),preferred_element_type=F32)
def split(x):
    h=x.astype(BF); return h,(x-h.astype(F32)).astype(BF)
GROUP=32
GP=16

def my_sizes(sizes):
    me=lax.axis_index("graph")
    total=sizes[0,0]
    for g in range(1,sizes.shape[1]): total+=sizes[0,g]
    return sizes[0,me]>>7, sizes[1,me], total

def sort_list(keys_l, keys_c, enc, lb, null, L):
    BLK=keys_l.shape[1]
    b_c=lax.broadcasted_iota(I32,(BLK,1),0); b_l=lax.broadcasted_iota(I32,(1,BLK),1)
    live=b_c<lb
    r_l=lax.broadcasted_iota(I32,(1,128),1); p_l=lax.broadcasted_iota(I32,(1,L),1)
    rank=jnp.sum(jnp.where((keys_l==keys_c)&(b_l<b_c),1.0,0.0),axis=1,keepdims=True)
    cnt=jnp.sum(jnp.where((keys_c==r_l)&live,1.0,0.0),axis=0,keepdims=True)
    even=2.0*jnp.floor(0.5*cnt+0.5)
    start=jnp.sum(jnp.where(r_l<keys_c,even,0.0),axis=1,keepdims=True)
    pos=jnp.where(live,(start+rank).astype(I32),-1)
    enc=enc-null; here=pos==p_l
    lo=jnp.sum(jnp.where(here,(enc&0xfff).astype(F32),0.0),axis=0,keepdims=True).astype(I32)
    hi=jnp.sum(jnp.where(here,(enc>>12).astype(F32),0.0),axis=0,keepdims=True).astype(I32)
    return hi*4096+lo+null,pos,jnp.sum(even,axis=1,keepdims=True).astype(I32)

def pair_fields(lists, which, q):
    e0=lists[which,2*q]; e1=lists[which,2*q+1]
    return e0>>20, (e0>>12)&0xff, (e1>>12)&0xff, e0&0xfff, e1&0xfff

def agg_nodes(lists, S, v, acc, lanes=slice(None)):
    n=lists[2,0]//2
    def step(s,_):
        for u in range(GROUP):
            q=s*GROUP+u
            r,c0,c1,_,_=pair_fields(lists,0,q)
            rhs=jnp.concatenate([v[c0],v[c1]],axis=0)
            acc[r,:,lanes]+=dot(jnp.concatenate([S[2*q],S[2*q+1]],axis=1),rhs)
        return 0
    lax.fori_loop(0,pl.cdiv(n,GROUP),step,0)

def load_S(lists, S_in, S, sems):
    n=2*pl.cdiv(lists[2,0],4*GP)
    def one(i): return pltpu.make_async_copy(S_in.at[pl.ds(i*2*GP,2*GP)],S.at[pl.ds(i*2*GP,2*GP)],sems.at[i])
    def start(): lax.fori_loop(0,n,lambda i,_:(one(i).start(),0)[1],0)
    def wait(): lax.fori_loop(0,n,lambda i,_:(one(i).wait(),0)[1],0)
    return start,wait

def in_vmem(*arrays): return [pltpu.with_memory_space_constraint(x,pltpu.VMEM) for x in arrays]

def agg_rows(lists, S, v, acc, rows=slice(None)):
    n=lists[3,0]//2
    def step(s,_):
        for u in range(GROUP):
            r,c0,c1,b0,b1=pair_fields(lists,1,s*GROUP+u)
            lhs=jnp.concatenate([v[c0],v[c1]],axis=1)
            acc[r,rows]+=dot(lhs,jnp.concatenate([S[b0],S[b1]],axis=0))
        return 0
    lax.fori_loop(0,pl.cdiv(n,GROUP),step,0)

def k0(sizes, blk_l, feat, vals, S_out, lists_out, fth_out, ftl_out, af_out,
       lists_v, lists_s, ft_v, fth, ftl, af, acc, buf, even, odd, ring, sem_in, sem_f, sem_l, sem_o, sem_S):
    nb,lb,_=my_sizes(sizes)
    NB=acc.shape[0]-1; BLK=vals.shape[0]; FIN=feat.shape[0]; NBUF=buf.shape[0]; NOUT=ring.shape[0]; SL=S_out.shape[0]
    L=lists_v.shape[1]; W=2*GP
    cf=pltpu.make_async_copy(feat.at[:,0],ft_v,sem_f); cf.start()
    ids=blk_l[...]
    columns=jnp.concatenate([ids.astype(F32),jnp.zeros((6,BLK),F32)],axis=0).T.astype(I32)
    rows=columns[:,0:1]; cols=columns[:,1:2]
    order=lax.broadcasted_iota(I32,(BLK,1),0)
    l0,pos,n0=sort_list(ids[0:1],rows,order+cols*(1<<12)+rows*(1<<20),lb,BLK+(NB<<20),L)
    lists_v[0:1,:]=l0; lists_v[2:3,:]=jnp.broadcast_to(n0,(1,L))
    cl=pltpu.make_async_copy(lists_v,lists_s,sem_l.at[0]); cl.start()
    acc[...]=jnp.zeros(acc.shape,F32)
    cl.wait()
    n=2*pl.cdiv(lists_s[2,0],4*GP)
    def chunk_start(i):
        slot=lax.rem(i,NBUF)
        for k in range(W):
            b=lists_s[0,i*W+k]&0xfff
            pltpu.make_async_copy(vals.at[jnp.where(b<BLK,b,0)],buf.at[slot,k],sem_in.at[slot]).start()
    def chunk_wait(i):
        slot=lax.rem(i,NBUF)
        pltpu.make_async_copy(vals.at[pl.ds(0,W)],buf.at[slot],sem_in.at[slot]).wait()
    lax.fori_loop(0,jnp.minimum(n,NBUF),lambda i,_:(chunk_start(i),0)[1],0)
    l1,_,n1=sort_list(ids[1:2],cols,pos+rows*(1<<12)+cols*(1<<20),lb,SL+(NB<<20),L)
    lists_v[1:2,:]=l1; lists_v[3:4,:]=jnp.broadcast_to(n1,(1,L))
    co=pltpu.make_async_copy(lists_v,lists_out,sem_l.at[1]); co.start()
    cf.wait()
    def tr(i,_):
        for k in range(4):
            b=i*4+k
            x=ft_v[:,pl.ds(pl.multiple_of(b*128,128),128)]
            x=jnp.concatenate([x,jnp.zeros((128-FIN,128),F32)],axis=0).T
            h,l=split(x); fth[b]=h; ftl[b]=l
        return 0
    lax.fori_loop(0,pl.cdiv(nb,4),tr,0)
    c1=pltpu.make_async_copy(fth,fth_out,sem_o.at[0]); c1.start()
    c2=pltpu.make_async_copy(ftl,ftl_out,sem_o.at[1]); c2.start()
    def chunk_out(i): return pltpu.make_async_copy(ring.at[lax.rem(i,NOUT)],S_out.at[pl.ds(i*W,W)],sem_S.at[lax.rem(i,NOUT)])
    def convert(i,stage):
        slot=lax.rem(i,NBUF); o=lax.rem(i,NOUT)
        chunk_wait(i)
        for k in range(W):
            x=jnp.where(lists_s[0,i*W+k]&0xfff<BLK,buf[slot,k],0.0).T.astype(BF)
            stage[k]=x; ring[o,k]=x
    def dots(i,stage):
        for u in range(GP):
            r,f0,f1,_,_=pair_fields(lists_s,0,i*GP+u)
            acc[r]+=dot(jnp.concatenate([stage[2*u],stage[2*u+1]],axis=1),jnp.concatenate([fth[f0],fth[f1]],axis=0))
    def refill(i):
        chunk_out(i).start()
        @pl.when(i+NBUF<n)
        def _(): chunk_start(i+NBUF)
        @pl.when(i+1>=NOUT)
        def _(): chunk_out(i+1-NOUT).wait()
    convert(0,even); refill(0)
    def step(j,_):
        convert(2*j+1,odd); dots(2*j,even); refill(2*j+1)
        convert(2*j+2,even); dots(2*j+1,odd); refill(2*j+2)
        return 0
    lax.fori_loop(0,n//2-1,step,0)
    convert(n-1,odd); chunk_out(n-1).start(); dots(n-2,even); dots(n-1,odd)
    def fin(b,_):
        for k in range(4): af[b*4+k]=acc[b*4+k].astype(BF)
        return 0
    lax.fori_loop(0,pl.cdiv(nb,4),fin,0)
    c3=pltpu.make_async_copy(af,af_out,sem_o.at[2]); c3.start()
    lax.fori_loop(jnp.maximum(n-NOUT,0),n,lambda i,_:(chunk_out(i).wait(),0)[1],0)
    c1.wait();c2.wait();c3.wait();co.wait()

def call_k0(sizes, blk, feat, vals, NBUF=8, NOUT=4):
    FIN,_,N=feat.shape; NB=N//128; BLK=vals.shape[0]; L=pl.cdiv(BLK+NB,128)*128; W=2*GP; SL=pl.cdiv(BLK+NB,2*GROUP)*2*GROUP
    sds=jax.ShapeDtypeStruct
    ANY=pl.BlockSpec(memory_space=pltpu.HBM); VM=pl.BlockSpec(memory_space=pltpu.VMEM); SM=pl.BlockSpec(memory_space=pltpu.SMEM)
    V=pltpu.VMEM; D=pltpu.SemaphoreType.DMA
    return pl.pallas_call(k0,
        out_shape=(pltpu.HBM((SL,128,128),BF),pltpu.HBM((8,L),I32),*[pltpu.HBM((NB,128,128),BF)]*3),
        in_specs=[SM,VM,ANY,ANY],out_specs=[ANY]*5,
        scratch_shapes=[V((8,L),I32),pltpu.SMEM((8,L),I32),V((FIN,N),F32),*[V((NB,128,128),BF)]*3,V((NB+1,128,128),F32),
            V((NBUF,W,128,128),F32),V((W,128,128),BF),V((W,128,128),BF),V((NOUT,W,128,128),BF),
            D((NBUF,)),D(()),D((2,)),D((3,)),D((NOUT,))],
        compiler_params=pltpu.CompilerParams(vmem_limit_bytes=VLIM0))(sizes,blk,feat,vals)
G0=0.7978845608; G1=0.044715
EPS=1e-5
HP=64
def for_blocks(nb,U,fn,start=0):
    full=nb//U
    def many(s,_): fn(s*U,U); return 0
    def one(b,_): fn(b,1); return 0
    lax.fori_loop(start,full,many,0)
    if U>1: lax.fori_loop(full*U,nb,one,0)
def rows8(x): return jnp.sum(x.reshape(x.shape[0]//8,8,x.shape[1]),axis=0)
def blk(ref,b0,U):
    x=ref[pl.ds(b0,U)]; return x.reshape(U*x.shape[1],x.shape[2])
def put_blk(ref,b0,U,x): ref[pl.ds(b0,U)]=x.reshape((U,)+ref.shape[1:])
def gelu_half(w):
    return w+w*jnp.tanh(w*(2.0*G0+(8.0*G0*G1)*(w*w)))
def dgelu_half(w):
    q=w*w
    t=jnp.tanh(w*(2.0*G0+(8.0*G0*G1)*q))
    return (1.0+t)*(0.5+(w*(G0+(12.0*G0*G1)*q))*(1.0-t))

def moments(sums,shift,count):
    d=jnp.sum(sums[0],axis=0,keepdims=True)/count
    v=jnp.sum(sums[1],axis=0,keepdims=True)/count-d*d
    return shift+d,lax.rsqrt(v+EPS)

def slot_nodes(pairs):
    R,K=pairs.shape; G=R//2
    x=jnp.concatenate([pairs[...].astype(F32),jnp.zeros((R,128-K),F32)],axis=1)
    if R%128: x=jnp.concatenate([x,jnp.zeros((128-R%128,128),F32)],axis=0)
    x=x.T[:K].astype(I32)
    return jnp.concatenate([x[:,t*G+g:t*G+g+1] for g in range(G) for t in range(2)],axis=0)
def one_hot(slots,b):
    return jnp.where(slots==lax.broadcasted_iota(I32,(1,128),1)+b*128,1.0,0.0).astype(BF)

def prepare(x,w1_out,w2_out,wh_out,npar_out,wt_out,w2m_out,ncol_out,CP):
    n_col=len(x)
    H=w1_out.shape[0]; MY=H//n_col; nk=H//128
    col=lax.axis_index("col")
    back=lax.rem(H-col*MY,H)
    heads=([],[]); norms=[]; mine=([],[])
    for k in range(n_col):
        r=slice(k*MY,k*MY+MY)
        q=2*nk*MY
        h,l=split(x[k][q:q+MY,:])
        w1_out[r,:]=jnp.concatenate([h,h,l,x[k][q+MY:q+2*MY,:].astype(BF)],axis=1)
        two=[]
        for half in range(2):
            w=jnp.concatenate([x[k][(half*nk+i)*MY:(half*nk+i+1)*MY,:] for i in range(nk)],axis=1)
            w=pltpu.roll(w,back,1)
            mine[half].append(w[:,:128])
            h,l=split(w); two+=[h,h,l]
            heads[half].append(x[k][q+2*MY+half*CP:q+2*MY+(half+1)*CP,:MY])
        w2_out[r,:]=jnp.concatenate(two,axis=1)
        norms.append(x[k][q+2*MY+2*CP:q+2*MY+2*CP+8,:MY])
    npar=jnp.concatenate(norms,axis=1)
    npar_out[...]=npar
    ncol_out[...]=npar[:,:128].T[:MY]
    (ch,cl),(dh,dl)=[split(jnp.concatenate(p,axis=1)) for p in heads]
    z=jnp.zeros((HP-CP,H),BF)
    wh_out[...]=jnp.concatenate([ch,z,dh,z,cl,z,dl,z],axis=0)
    z=jnp.zeros((128-2*CP,H),BF)
    th=jnp.concatenate([ch,dh,z],axis=0); tl=jnp.concatenate([cl,dl,z],axis=0)
    wt_out[...]=jnp.concatenate([th,th,tl],axis=0)
    for half in range(2):
        h,l=split(jnp.concatenate(mine[half],axis=0).T[:MY])
        w2m_out[2*half*MY:(2*half+2)*MY,:]=jnp.concatenate([h,l],axis=0)

def kb(sizes,lists,pairs,S_in,fth_in,ftl_in,af_in,*refs,n_col):
    shards=refs[:n_col]
    (
       h1h_out,h1l_out,pre,pre1,st,h2t,lg,own_out,S,npar,wt,w2m,ncol,
       w1,w2,wh,fth,ftl,af,h1h,h1l,acc,zz,sums,sem_i,sem_o,sem_S)=refs[n_col:]
    nb,_,_=my_sizes(sizes); NB=fth.shape[0]; CP=lg.shape[1]; MY=pre1.shape[1]
    count=(nb*128).astype(F32)
    cs=[pltpu.make_async_copy(a,b,sem_i.at[i]) for i,(a,b) in enumerate(((fth_in,fth),(ftl_in,ftl),(af_in,af)))]
    for c in cs: c.start()
    S_start,S_wait=load_S(lists,S_in,S,sem_S); S_start()
    S[S_in.shape[0]]=jnp.zeros((128,128),BF)
    st[...]=jnp.zeros_like(st)
    prepare(shards,w1,w2,wh,npar,wt,w2m,ncol,CP)
    for c in cs: c.wait()
    def first(b0,U):
        h=blk(fth,b0,U)
        x=jnp.concatenate([h,blk(ftl,b0,U),h,blk(af,b0,U)],axis=1)
        return dot_nt(x,w1[...])
    def second(b0,U):
        h=blk(h1h,b0,U); l=blk(h1l,b0,U); ah,al=split(blk(acc,b0,U))
        return dot_nt(jnp.concatenate([h,l,h,ah,al,ah],axis=1),w2[...])
    def layer(fn,mine):
        shift=jnp.sum(fn(0,1),axis=0,keepdims=True)/128.0
        sums[...]=jnp.zeros_like(sums)
        def tile(b0,U):
            y=fn(b0,U)
            put_blk(pre,b0,U,y)
            if mine:
                for k in range(U): pre1[b0+k]=y[k*128:k*128+128,:MY].T
            d=y-shift
            sums[0]+=rows8(d); sums[1]+=rows8(d*d)
        for_blocks(nb,8,tile)
        return moments(sums,shift,count)
    mean,inv=layer(first,True)
    st[0:1,:]=mean; st[1:2,:]=inv
    a=npar[0:1,:]*inv; c=npar[1:2,:]-mean*a
    a=0.5*a; c=0.5*c
    def n1(b0,U):
        h,l=split(gelu_half(blk(pre,b0,U)*a+c))
        put_blk(h1h,b0,U,h); put_blk(h1l,b0,U,l)
        put_blk(acc,b0,U,jnp.zeros((U*128,acc.shape[2]),F32))
    for_blocks(nb,4,n1)
    acc[NB]=jnp.zeros(acc.shape[1:],F32)
    outs=[pltpu.make_async_copy(x,y,sem_o.at[i]) for i,(x,y) in enumerate(((h1h,h1h_out),(h1l,h1l_out)))]
    for o in outs: o.start()
    S_wait()
    agg_nodes(lists,S,h1h,acc)
    mean2,inv2=layer(second,False)
    st[2:3,:]=mean2; st[3:4,:]=inv2
    a2=npar[2:3,:]*inv2; c2=npar[3:4,:]-mean2*a2
    a2=0.5*a2; c2=0.5*c2
    def n2(b0,U):
        h,l=split(gelu_half(blk(pre,b0,U)*a2+c2))
        r=dot_nt(h,wh[...])
        dz=r[:,:2*HP]+r[:,2*HP:]+dot_nt(l,wh[0:2*HP,:])
        zh,zl=split(dz)
        put_blk(zz,b0,U,jnp.concatenate([zh[:,HP:],zl[:,HP:]],axis=1))
        put_blk(acc,b0,U,jnp.concatenate([dz,jnp.zeros_like(dz)],axis=1))
        t=jnp.concatenate([h[:,:MY],l[:,:MY]],axis=1)
        for k in range(U): h2t[b0+k]=t[k*128:k*128+128].T
    for_blocks(nb,8,n2)
    agg_nodes(lists,S,zz,acc,slice(2*HP,4*HP))
    def fin(b0,U):
        for k in range(U):
            x=acc[b0+k]; s=x[:,2*HP:]
            y=x[:,:2*HP]+s+pltpu.roll(s,HP,1)
            acc[b0+k,:,:2*HP]=y
            lg[b0+k]=y.T[:CP]
    for_blocks(nb,8,fin)
    G=pairs.shape[0]//2; K=pairs.shape[1]
    lane=lax.broadcasted_iota(I32,(1,128),1); sub=lax.broadcasted_iota(I32,(8,1),0)
    def slot(g,_):
        for t in range(2):
            for k0 in range(0,K,8):
                o=jnp.zeros((8,128),F32)
                for k in range(8):
                    n=pairs[t*G+g,k0+k]
                    x=acc[n>>7,pl.ds(pl.multiple_of(((n>>3)&15)*8,8),8),:2*HP]
                    o=jnp.where(sub==k,jnp.sum(jnp.where(sub==(n&7),x,0.0),axis=0,keepdims=True),o)
                own_out[g,pl.ds(pl.multiple_of(t*K+k0,8),8),:]=jnp.where(lane<CP,o,0.0)
        return 0
    lax.fori_loop(0,G,slot,0)
    for o in outs: o.wait()

def call_kb(sizes,lists,S,fth,ftl,af,shards,pairs,MY,CP):
    n_col=len(shards); NB=fth.shape[0]; H=MY*n_col; SL=S.shape[0]; G=pairs.shape[0]//2; K=pairs.shape[1]
    sds=jax.ShapeDtypeStruct
    ANY=pl.BlockSpec(memory_space=pltpu.HBM); VM=pl.BlockSpec(memory_space=pltpu.VMEM); SM=pl.BlockSpec(memory_space=pltpu.SMEM)
    V=pltpu.VMEM
    return pl.pallas_call(functools.partial(kb,n_col=n_col),
        out_shape=(pltpu.HBM((NB,128,H),BF),pltpu.HBM((NB,128,H),BF),V((NB,128,H),F32),V((NB,MY,128),F32),sds((8,H),F32),V((NB,2*MY,128),BF),V((NB,CP,128),F32),V((G,2*K,128),F32),V((SL+1,128,128),BF),sds((8,H),F32),sds((384,H),BF),sds((4*MY,H),BF),sds((MY,8),F32)),
        in_specs=[SM]*3+[ANY]*4+[VM]*n_col,out_specs=[ANY]*2+[VM]*11,
        scratch_shapes=[V((H,512),BF),V((H,6*H),BF),V((4*HP,H),BF)]+[V((NB,128,128),BF)]*3+[V((NB,128,H),BF)]*2+[V((NB+1,128,H),F32),V((NB,128,2*HP),BF),V((2,8,H),F32),pltpu.SemaphoreType.DMA((3,)),pltpu.SemaphoreType.DMA((2,)),pltpu.SemaphoreType.DMA((SL//(2*GP),))],
        compiler_params=pltpu.CompilerParams(vmem_limit_bytes=VLIM))(sizes,lists,pairs,S,fth,ftl,af,*shards)


def kc(sizes,lists,S,pre,pre1,h2t,lg,h1h_in,h1l_in,fth_in,ftl_in,af_in,st,own,recv,labels,pairs,wt,w2m,npar,ncol,
       g_out,
       rh,rl,rfh,rfl,raf,du,gz,acc,v4,sums,cross,RH,RS,RL,R1,R2,colsum,sem_r,CLS):
    nb,_,nodes=my_sizes(sizes); NB=pre.shape[0]; CP=lg.shape[1]; MY=ncol.shape[0]; H=pre.shape[2]; NS=rh.shape[0]; U8=rh.shape[1]
    count=(nb*128).astype(F32); total=nodes.astype(F32)
    nch=pl.cdiv(nb,U8)
    def ring(i):
        s=lax.rem(i,NS)
        return [pltpu.make_async_copy(a.at[pl.ds(i*U8,U8)],b.at[s],sem_r.at[s,k]) for k,(a,b) in enumerate(((h1h_in,rh),(h1l_in,rl),(fth_in,rfh),(ftl_in,rfl),(af_in,raf)))]
    for i in range(NS):
        @pl.when(i<nch)
        def _():
            for c in ring(i): c.start()
    for r in (sums,cross,RH,RS,RL,R1,R2,colsum): r[...]=jnp.zeros_like(r)
    acc[NB]=jnp.zeros(acc.shape[1:],F32)
    half=pairs.shape[1]
    G=pairs.shape[0]//2
    r=recv[...]
    D=own[...]-jnp.concatenate([r[:,half:],r[:,:half]],axis=1)
    pair_loss=0.5*jnp.sum(D[:,half:]*D[:,half:])
    Dh,Dl=split((D.reshape(2*G*half,128).T)[:CP]/total); D2=jnp.concatenate([Dh,Dl],axis=0)
    slots=slot_nodes(pairs)
    def soft(b0,U):
        hot=jnp.concatenate([one_hot(slots,b0+k) for k in range(U)],axis=1)
        add=dot(D2,hot); add=add[:CP]+add[CP:]
        x=jnp.concatenate([lg[b0+k] for k in range(U)],axis=1)
        lab=jnp.concatenate([labels[b0+k] for k in range(U)],axis=1)
        row=lax.broadcasted_iota(I32,(CP,1),0)
        xm=jnp.where(row<CLS,x,-1e30)
        mx=jnp.max(xm,axis=0,keepdims=True)
        e=jnp.exp(xm-mx); s=jnp.sum(e,axis=0,keepdims=True)
        hit=jnp.where(row==lab,1.0,0.0)
        c=mx+jnp.log(s)-jnp.sum(hit*x,axis=0,keepdims=True)
        g=(e/s-hit)/total+add
        h,l=split(g)
        for k in range(U):
            w=slice(k*128,k*128+128)
            cross[...]+=c[:,w]
            gz[b0+k]=jnp.concatenate([h[:,w],l[:,w]],axis=0)
            acc[b0+k,:2*CP]=jnp.zeros((2*CP,128),F32)
    for_blocks(nb,4,soft)
    agg_rows(lists,S,gz,acc,slice(0,2*CP))
    mean2=st[2:3,:]; inv2=st[3:4,:]
    a2=npar[2:3,:]*inv2; c2=npar[3:4,:]-mean2*a2
    ha2=0.5*a2; hc2=0.5*c2
    def back2(b0,U):
        th=[];tl=[];ads=[]
        z=jnp.zeros((128-2*CP,128),BF)
        for k in range(U):
            ad=acc[b0+k,:2*CP]; ah,al=split(ad[:CP]+ad[CP:]); gk=gz[b0+k]
            th.append(jnp.concatenate([gk[:CP],ah,z],axis=0).T); tl.append(jnp.concatenate([gk[CP:],al,z],axis=0).T)
            ads.append(ah)
        th=jnp.concatenate(th,axis=0); tl=jnp.concatenate(tl,axis=0)
        gh=dot(jnp.concatenate([th,tl,th],axis=1),wt[...])
        hh=jnp.concatenate([h2t[b0+k] for k in range(U)],axis=1)
        gg=jnp.concatenate([jnp.concatenate([gz[b0+k] for k in range(U)],axis=1),jnp.concatenate(ads,axis=1)],axis=0)
        RH[...]+=dot_nt(hh,gg)
        y=blk(pre,b0,U)
        d=gh*dgelu_half(y*ha2+hc2)
        put_blk(du,b0,U,d)
        sums[0]+=rows8(d); sums[1]+=rows8(d*(y-mean2))
    for_blocks(nb,8,back2)
    sb2=jnp.sum(sums[0],axis=0,keepdims=True); sg2=jnp.sum(sums[1],axis=0,keepdims=True)*inv2
    A2=-a2*inv2*sg2/count; C2=-a2*sb2/count-A2*mean2
    def proj(b0,U):
        h,l=split(blk(du,b0,U)*a2+blk(pre,b0,U)*A2+C2)
        r=dot_nt(w2m[...],h); rl2=dot_nt(w2m[0:MY,:],l)
        d=r[:MY]+r[MY:2*MY]+rl2; t=(r[2*MY:3*MY]+r[3*MY:]).astype(BF)
        gt=jnp.concatenate([h[:,:MY],l[:,:MY]],axis=1)
        for k in range(U):
            w=slice(k*128,k*128+128)
            acc[b0+k]=jnp.concatenate([d[:,w],jnp.zeros((2*MY,128),F32)],axis=0)
            v4[b0+k]=jnp.concatenate([t[:,w],gt[w].T],axis=0)
    for_blocks(nb,8,proj)
    acc[NB]=jnp.zeros(acc.shape[1:],F32)
    agg_rows(lists,S,v4,acc)
    lane=lambda x: jnp.sum(x,axis=1,keepdims=True)
    stc=st[:,:128].T[:MY]
    mean1=stc[:,0:1]; inv1=stc[:,1:2]
    a1=ncol[:,0:1]*inv1; c1=ncol[:,1:2]-mean1*a1
    ha1=0.5*a1; hc1=0.5*c1
    def back1(b0,U):
        for k in range(U):
            p=pre1[b0+k]
            d=acc[b0+k,:MY]*dgelu_half(p*ha1+hc1)
            acc[b0+k,:MY]=d
            colsum[0]+=d; colsum[1]+=d*(p-mean1)
    for_blocks(nb,4,back1)
    sb1=lane(colsum[0]); sg1=lane(colsum[1])*inv1
    A1=-a1*inv1*sg1/count; C1=-a1*sb1/count-A1*mean1
    def last(i,_):
        s=lax.rem(i,NS)
        for c in ring(i): c.wait()
        def part(b0,off,U):
            f=lambda ref: ref[s,pl.ds(off,U)].reshape(U*128,ref.shape[3])
            x=[acc[b0+k] for k in range(U)]
            gh,gl=split(jnp.concatenate([x[k][:MY]*a1+pre1[b0+k]*A1+C1 for k in range(U)],axis=1))
            R1[...]+=dot(jnp.concatenate([gh,gl],axis=0),f(rfh))
            R2[...]+=dot(gh,jnp.concatenate([f(rfl),f(raf)],axis=1))
            ah,al=split(jnp.concatenate([x[k][MY:2*MY]+x[k][2*MY:] for k in range(U)],axis=1))
            gt=jnp.concatenate([v4[b0+k,MY:] for k in range(U)],axis=1)
            RS[...]+=dot(jnp.concatenate([gt,ah,al],axis=0),f(rh))
            RL[...]+=dot(jnp.concatenate([gt[:MY],ah],axis=0),f(rl))
        @pl.when((i+1)*U8<=nb)
        def _(): part(i*U8,0,U8)
        @pl.when((i+1)*U8>nb)
        def _():
            lax.fori_loop(0,nb-i*U8,lambda k,_:(part(i*U8+k,k,1),0)[1],0)
        @pl.when(i+NS<nch)
        def _():
            for c in ring(i+NS): c.start()
        return 0
    lax.fori_loop(0,nch,last,0)
    RSv=RS[...]; RLv=RL[...]; nk=H//128
    for h in range(2):
        gs=RSv[2*h*MY:(2*h+1)*MY]+RSv[(2*h+1)*MY:(2*h+2)*MY]+RLv[h*MY:(h+1)*MY]
        for k in range(nk): g_out[(h*nk+k)*MY:(h*nk+k+1)*MY,:]=gs[:,k*128:k*128+128]
    R1v=R1[...]; R2v=R2[...]
    q=2*nk*MY
    g_out[q:q+MY,:]=R1v[:MY]+R1v[MY:]+R2v[:,:128]
    g_out[q+MY:q+2*MY,:]=R2v[:,128:]
    RHv=RH[...]; gh=RHv[:MY]+RHv[MY:]
    gh=jnp.concatenate([RHv[:MY,:CP]+RHv[:MY,CP:2*CP]+RHv[MY:,:CP],gh[:,2*CP:3*CP],sg1,sb1,jnp.zeros((MY,128-2*CP-2),F32)],axis=1)
    g_out[q+2*MY:q+3*MY,:]=gh
    loss=jnp.sum(cross[...])+pair_loss
    pad=[jnp.zeros((1,128-MY),F32)]
    g_out[q+3*MY:,:]=jnp.zeros((g_out.shape[0]-q-3*MY,128),F32)
    g_out[q+3*MY:q+3*MY+8,:]=jnp.concatenate([jnp.concatenate([sg2[:,:MY]]+pad,axis=1),jnp.concatenate([sb2[:,:MY]]+pad,axis=1),jnp.broadcast_to(loss,(1,128)),jnp.zeros((5,128),F32)],axis=0)

def call_kc(sizes,lists,S,fth,ftl,af,h1h,h1l,pre,pre1,h2t,lg,st,own,recv,labels,pairs,wt,w2m,npar,ncol,CLS,rows):
    NB=fth.shape[0]; H=pre.shape[2]; CP=lg.shape[1]; MY=ncol.shape[0]; NS=3; U8=8
    ANY=pl.BlockSpec(memory_space=pltpu.HBM); VM=pl.BlockSpec(memory_space=pltpu.VMEM); SM=pl.BlockSpec(memory_space=pltpu.SMEM)
    V=pltpu.VMEM
    return pl.pallas_call(functools.partial(kc,CLS=CLS),out_shape=jax.ShapeDtypeStruct((rows,128),F32),
        in_specs=[SM,SM]+[VM]*5+[ANY]*5+[VM]*9,out_specs=VM,
        scratch_shapes=[V((NS,U8,128,H),BF)]*2+[V((NS,U8,128,128),BF)]*3+[
            V((NB,128,H),F32),V((NB,2*CP,128),BF),V((NB+1,max(3*MY,2*CP),128),F32),V((NB,3*MY,128),BF),
            V((2,8,H),F32),V((1,128),F32),V((2*MY,3*CP),F32),V((4*MY,H),F32),V((2*MY,H),F32),V((2*MY,128),F32),V((MY,256),F32),V((2,MY,128),F32),
            pltpu.SemaphoreType.DMA((NS,5))],
        compiler_params=pltpu.CompilerParams(vmem_limit_bytes=VLIM))(sizes,lists,*in_vmem(S,pre,pre1,h2t,lg),h1h,h1l,fth,ftl,af,st,*in_vmem(own,recv),labels,pairs,wt,w2m,npar,ncol)

def at(index): return {"graph": index}
def meet(n):
    me=lax.axis_index("graph")
    barrier=pltpu.get_barrier_semaphore()
    for k in range(1,n):
        pl.semaphore_signal(barrier,inc=1,device_id=at(lax.rem(me+k,n)),device_id_type=pl.DeviceIdType.MESH)
    pl.semaphore_wait(barrier,n-1)

def kx(own,out,send,recv,n):
    me=lax.axis_index("graph")
    meet(n)
    copies=[]
    for k in range(1,n):
        peer=lax.rem(me+k,n)
        c=pltpu.make_async_remote_copy(src_ref=own.at[peer],dst_ref=out.at[me],send_sem=send.at[k-1],recv_sem=recv.at[k-1],
            device_id=at(peer),device_id_type=pl.DeviceIdType.MESH)
        c.start(); copies.append(c)
    out[me]=own[me]
    for c in copies: c.wait()

def call_kx(own,n):
    VM=pl.BlockSpec(memory_space=pltpu.VMEM)
    return pl.pallas_call(functools.partial(kx,n=n),out_shape=pltpu.VMEM(own.shape,own.dtype),in_specs=[VM],out_specs=VM,
        scratch_shapes=[pltpu.SemaphoreType.DMA((n-1,)),pltpu.SemaphoreType.DMA((n-1,))],
        compiler_params=pltpu.CompilerParams(vmem_limit_bytes=8<<20,collective_id=1,has_side_effects=True))(*in_vmem(own))

def kr(g,out,parts,send1,recv1,send2,recv2,n):
    me=lax.axis_index("graph")
    piece=g.shape[0]//n
    def rows(i): return pl.ds(pl.multiple_of(i*piece,8),piece)
    meet(n)
    copies=[]
    for k in range(1,n):
        peer=lax.rem(me+k,n)
        c=pltpu.make_async_remote_copy(src_ref=g.at[rows(peer)],dst_ref=parts.at[k-1],send_sem=send1.at[k-1],recv_sem=recv1.at[k-1],
            device_id=at(peer),device_id_type=pl.DeviceIdType.MESH)
        c.start(); copies.append(c)
    total=g[rows(me),:]
    for k,c in enumerate(copies):
        c.wait_recv(); total+=parts[k]
    out[rows(me),:]=total
    back=[]
    for k in range(1,n):
        peer=lax.rem(me+k,n)
        c=pltpu.make_async_remote_copy(src_ref=out.at[rows(me)],dst_ref=out.at[rows(me)],send_sem=send2.at[k-1],recv_sem=recv2.at[k-1],
            device_id=at(peer),device_id_type=pl.DeviceIdType.MESH)
        c.start(); back.append(c)
    for c in copies: c.wait_send()
    for c in back: c.wait()

def call_kr(g,n):
    VM=pl.BlockSpec(memory_space=pltpu.VMEM); D=pltpu.SemaphoreType.DMA((n-1,))
    return pl.pallas_call(functools.partial(kr,n=n),out_shape=jax.ShapeDtypeStruct(g.shape,g.dtype),in_specs=[VM],out_specs=VM,
        scratch_shapes=[pltpu.VMEM((n-1,g.shape[0]//n,128),F32),D,D,D,D],
        compiler_params=pltpu.CompilerParams(collective_id=2,has_side_effects=True))(g)

def kp(wf,ws,wh,npar,out):
    _,MY,FIN=wf.shape; H=ws.shape[2]; CLS=wh.shape[0]; CP=-(-CLS//16)*16; nk=H//128
    out[...]=jnp.zeros_like(out)
    for h in range(2):
        for k in range(nk):
            r=(h*nk+k)*MY; out[r:r+MY,:]=ws[h,:,k*128:k*128+128]
        r=2*nk*MY+h*MY; out[r:r+MY,:FIN]=wf[h]
        r=2*nk*MY+2*MY+h*CP; out[r:r+CLS,:MY]=wh[:,h,:]
        r=2*nk*MY+2*MY+2*CP+2*h; out[r:r+2,:MY]=npar[h]

def call_kp(wf,ws,wh,npar):
    _,MY,FIN=wf.shape; H=ws.shape[2]; CP=-(-wh.shape[0]//16)*16
    rows=-(-(2*H//128*MY+2*MY+2*CP+8)//16)*16
    VM=pl.BlockSpec(memory_space=pltpu.VMEM)
    return pl.pallas_call(kp,out_shape=jax.ShapeDtypeStruct((rows,128),F32),in_specs=[VM]*4,out_specs=VM)(wf,ws,wh,npar)

def renew(weight, momentum, average, gradient):
    momentum_new = MOMENTUM * momentum + gradient
    weight_new = weight - STEP_RATE * (gradient + MOMENTUM * momentum_new)
    average_new = AVERAGE_KEEP * average + (1.0 - AVERAGE_KEEP) * weight_new
    return momentum_new, average_new, weight_new

def ku(sizes,g,*refs):
    weights,momenta,averages,outs,loss,count=refs[:4],refs[4:8],refs[8:12],refs[12:24],refs[24],refs[25]
    _,MY,FIN=weights[0].shape; H=weights[1].shape[2]; CLS=weights[2].shape[0]; CP=-(-CLS//16)*16; nk=H//128
    q=2*nk*MY
    shift=lax.axis_index("col")*MY
    def store(i,where,grad):
        for o,v in zip(outs[3*i:3*i+3],renew(weights[i][where],momenta[i][where],averages[i][where],grad)): o[where]=v
    head=g[q+2*MY:q+3*MY,:].T
    for h in range(2):
        x=jnp.concatenate([g[(h*nk+k)*MY:(h*nk+k+1)*MY,:] for k in range(nk)],axis=1)
        store(1,(h,),pltpu.roll(x,shift,1))
        store(0,(h,),g[q+h*MY:q+h*MY+MY,:FIN])
        store(2,(slice(None),h,slice(None)),head[h*CP:h*CP+CLS,:MY])
    store(3,(0,),head[2*CP:2*CP+2,:MY])
    store(3,(1,),g[q+3*MY:q+3*MY+2,:MY])
    loss[0,0]=g[q+3*MY+2,0]
    count[0,0]=my_sizes(sizes)[2].astype(F32)

def call_ku(sizes,g,weights,momenta,averages):
    VM=pl.BlockSpec(memory_space=pltpu.VMEM); SM=pl.BlockSpec(memory_space=pltpu.SMEM)
    shapes=[jax.ShapeDtypeStruct(w.shape,F32) for w in weights for _ in range(3)]
    return pl.pallas_call(ku,out_shape=(*shapes,*[jax.ShapeDtypeStruct((1,1),F32)]*2),in_specs=[SM]+[VM]*13,out_specs=[VM]*12+[SM]*2)(sizes,g,*weights,*momenta,*averages)

MOMENTUM=0.9; STEP_RATE=2.0; AVERAGE_KEEP=0.9

def per_device(n_graph, n_col, features, blocks, block_values, group_sizes, labels, pair_nodes, weight_first, weight_second, weight_head,
               norm_params, momentum_first, momentum_second, momentum_head, momentum_norms, average_first, average_second,
               average_head, average_norms):
    MY=weight_first.shape[2]; H=MY*n_col; CLS=weight_head.shape[2]; CP=-(-CLS//16)*16
    G=group_sizes.shape[0]; N=features.shape[2]; NB=N//128; PEER=pair_nodes.shape[3]
    def native(first,second,head,norms):
        return first.transpose(0,2,1),second.transpose(0,2,1),head.transpose(2,0,1),norms
    weights=native(weight_first,weight_second,weight_head,norm_params)
    momenta=native(momentum_first,momentum_second,momentum_head,momentum_norms)
    averages=native(average_first,average_second,average_head,average_norms)
    packed=call_kp(*weights)
    shards=[packed]+[lax.ppermute(packed,"col",[((j+k)%n_col,j) for j in range(n_col)]) for k in range(1,n_col)]
    sizes=group_sizes.T
    S,lists,fth,ftl,af=call_k0(sizes,blocks[0],features.transpose(1,0,2),block_values[0])
    pairs=pair_nodes[0].reshape(2*G,PEER)
    h1h,h1l,pre,pre1,st,h2t,lg,own,S,npar,wt,w2m,ncol=call_kb(sizes,lists,S,fth,ftl,af,shards,pairs,MY=MY,CP=CP)
    recv=call_kx(own,n_graph)
    unit=8*n_graph; rows=-(-(2*H//128*MY+3*MY+8)//unit)*unit
    g=call_kc(sizes,lists,S,fth,ftl,af,h1h,h1l,pre,pre1,h2t,lg,st,own,recv,labels[0].reshape(NB,1,128),pairs,wt,w2m,npar,ncol,CLS=CLS,rows=rows)
    g=call_kr(g,n_graph)
    *new,loss,count=call_ku(sizes,g,weights,momenta,averages)
    first=[x.transpose(0,2,1) for x in new[0:3]]
    second=[x.transpose(0,2,1) for x in new[3:6]]
    head=[x.transpose(1,2,0) for x in new[6:9]]
    return (loss[0,0],count[0,0],*first,*second,*head,*new[9:12])

def solution(mesh):
    P=jax.sharding.PartitionSpec
    unit=P(None,None,"col"); head=P(None,"col",None)
    weights=(unit,unit,head,unit)
    in_specs=(P("graph",None,None),P("graph",None,None),P("graph",None,None,None),P(),P("graph",None),P("graph",None,None,None))+weights*3
    out_specs=(P(),P())+(unit,)*6+(head,)*3+(unit,)*3
    return jax.shard_map(functools.partial(per_device,mesh.shape["graph"],mesh.shape["col"]),mesh=mesh,in_specs=in_specs,out_specs=out_specs,check_vma=False)
```

```python
import functools
import jax, jax.numpy as jnp
from jax import lax
from jax.experimental import pallas as pl
from jax.experimental.pallas import tpu as pltpu
BF=jnp.bfloat16; F32=jnp.float32; I32=jnp.int32
VLIM0=58<<20
VLIM=31<<20
def dot(a,b): return jnp.dot(a,b,preferred_element_type=F32)
def dot_nt(a,b): return lax.dot_general(a,b,(((1,),(1,)),((),())),preferred_element_type=F32)
def split(x):
    h=x.astype(BF); return h,(x-h.astype(F32)).astype(BF)
GROUP=72
GP=16

def my_sizes(sizes):
    me=lax.axis_index("graph")
    total=sizes[0,0]
    for g in range(1,sizes.shape[1]): total+=sizes[0,g]
    return sizes[0,me]>>7, sizes[1,me], total

def sort_list(keys_l, keys_c, enc, lb, null, L):
    BLK=keys_l.shape[1]
    b_c=lax.broadcasted_iota(I32,(BLK,1),0); b_l=lax.broadcasted_iota(I32,(1,BLK),1)
    live=b_c<lb
    r_l=lax.broadcasted_iota(I32,(1,128),1); p_l=lax.broadcasted_iota(I32,(1,L),1)
    rank=jnp.sum(jnp.where((keys_l==keys_c)&(b_l<b_c),1.0,0.0),axis=1,keepdims=True)
    cnt=jnp.sum(jnp.where((keys_c==r_l)&live,1.0,0.0),axis=0,keepdims=True)
    even=2.0*jnp.floor(0.5*cnt+0.5)
    start=jnp.sum(jnp.where(r_l<keys_c,even,0.0),axis=1,keepdims=True)
    pos=jnp.where(live,(start+rank).astype(I32),-1)
    enc=enc-null; here=pos==p_l
    lo=jnp.sum(jnp.where(here,(enc&0xfff).astype(F32),0.0),axis=0,keepdims=True).astype(I32)
    hi=jnp.sum(jnp.where(here,(enc>>12).astype(F32),0.0),axis=0,keepdims=True).astype(I32)
    return hi*4096+lo+null,pos,jnp.sum(even,axis=1,keepdims=True).astype(I32)

def pair_fields(lists, which, q):
    e0=lists[which,2*q]; e1=lists[which,2*q+1]
    return e0>>20, (e0>>12)&0xff, (e1>>12)&0xff, e0&0xfff, e1&0xfff

def agg_nodes(lists, S, v, acc, lanes=slice(None)):
    n=lists[2,0]//2
    def step(s,_):
        for u in range(GROUP):
            q=s*GROUP+u
            r,c0,c1,_,_=pair_fields(lists,0,q)
            rhs=jnp.concatenate([v[c0],v[c1]],axis=0)
            acc[r,:,lanes]+=dot(jnp.concatenate([S[2*q],S[2*q+1]],axis=1),rhs)
        return 0
    lax.fori_loop(0,pl.cdiv(n,GROUP),step,0)

def load_S(lists, S_in, S, sems):
    n=2*pl.cdiv(lists[2,0],4*GP)
    def one(i): return pltpu.make_async_copy(S_in.at[pl.ds(i*2*GP,2*GP)],S.at[pl.ds(i*2*GP,2*GP)],sems.at[i])
    def start(): lax.fori_loop(0,n,lambda i,_:(one(i).start(),0)[1],0)
    def wait(): lax.fori_loop(0,n,lambda i,_:(one(i).wait(),0)[1],0)
    return start,wait

def in_vmem(*arrays): return [pltpu.with_memory_space_constraint(x,pltpu.VMEM) for x in arrays]

def agg_rows(lists, S, v, acc, rows=slice(None)):
    n=lists[3,0]//2
    def step(s,_):
        for u in range(GROUP):
            r,c0,c1,b0,b1=pair_fields(lists,1,s*GROUP+u)
            lhs=jnp.concatenate([v[c0],v[c1]],axis=1)
            acc[r,rows]+=dot(lhs,jnp.concatenate([S[b0],S[b1]],axis=0))
        return 0
    lax.fori_loop(0,pl.cdiv(n,GROUP),step,0)

def k0(sizes, blk_l, feat, vals, S_out, lists_out, fth_out, ftl_out, af_out,
       lists_v, lists_s, ft_v, fth, ftl, af, acc, buf, even, odd, ring, sem_in, sem_f, sem_l, sem_o, sem_S):
    nb,lb,_=my_sizes(sizes)
    NB=acc.shape[0]-1; BLK=vals.shape[0]; FIN=feat.shape[0]; NBUF=buf.shape[0]; NOUT=ring.shape[0]; SL=S_out.shape[0]
    L=lists_v.shape[1]; W=2*GP
    cf=pltpu.make_async_copy(feat.at[:,0],ft_v,sem_f); cf.start()
    ids=blk_l[...]
    columns=jnp.concatenate([ids.astype(F32),jnp.zeros((6,BLK),F32)],axis=0).T.astype(I32)
    rows=columns[:,0:1]; cols=columns[:,1:2]
    order=lax.broadcasted_iota(I32,(BLK,1),0)
    l0,pos,n0=sort_list(ids[0:1],rows,order+cols*(1<<12)+rows*(1<<20),lb,BLK+(NB<<20),L)
    lists_v[0:1,:]=l0; lists_v[2:3,:]=jnp.broadcast_to(n0,(1,L))
    cl=pltpu.make_async_copy(lists_v,lists_s,sem_l.at[0]); cl.start()
    acc[...]=jnp.zeros(acc.shape,F32)
    cl.wait()
    n=2*pl.cdiv(lists_s[2,0],4*GP)
    def chunk_start(i):
        slot=lax.rem(i,NBUF)
        for k in range(W):
            b=lists_s[0,i*W+k]&0xfff
            pltpu.make_async_copy(vals.at[jnp.where(b<BLK,b,0)],buf.at[slot,k],sem_in.at[slot]).start()
    def chunk_wait(i):
        slot=lax.rem(i,NBUF)
        pltpu.make_async_copy(vals.at[pl.ds(0,W)],buf.at[slot],sem_in.at[slot]).wait()
    lax.fori_loop(0,jnp.minimum(n,NBUF),lambda i,_:(chunk_start(i),0)[1],0)
    l1,_,n1=sort_list(ids[1:2],cols,pos+rows*(1<<12)+cols*(1<<20),lb,SL+(NB<<20),L)
    lists_v[1:2,:]=l1; lists_v[3:4,:]=jnp.broadcast_to(n1,(1,L))
    co=pltpu.make_async_copy(lists_v,lists_out,sem_l.at[1]); co.start()
    cf.wait()
    def tr(i,_):
        for k in range(4):
            b=i*4+k
            x=ft_v[:,pl.ds(pl.multiple_of(b*128,128),128)]
            x=jnp.concatenate([x,jnp.zeros((128-FIN,128),F32)],axis=0).T
            h,l=split(x); fth[b]=h; ftl[b]=l
        return 0
    lax.fori_loop(0,pl.cdiv(nb,4),tr,0)
    c1=pltpu.make_async_copy(fth,fth_out,sem_o.at[0]); c1.start()
    c2=pltpu.make_async_copy(ftl,ftl_out,sem_o.at[1]); c2.start()
    def chunk_out(i): return pltpu.make_async_copy(ring.at[lax.rem(i,NOUT)],S_out.at[pl.ds(i*W,W)],sem_S.at[lax.rem(i,NOUT)])
    def convert(i,stage):
        slot=lax.rem(i,NBUF); o=lax.rem(i,NOUT)
        chunk_wait(i)
        for k in range(W):
            x=jnp.where(lists_s[0,i*W+k]&0xfff<BLK,buf[slot,k],0.0).T.astype(BF)
            stage[k]=x; ring[o,k]=x
    def dots(i,stage):
        for u in range(GP):
            r,f0,f1,_,_=pair_fields(lists_s,0,i*GP+u)
            acc[r]+=dot(jnp.concatenate([stage[2*u],stage[2*u+1]],axis=1),jnp.concatenate([fth[f0],fth[f1]],axis=0))
    def refill(i):
        chunk_out(i).start()
        @pl.when(i+NBUF<n)
        def _(): chunk_start(i+NBUF)
        @pl.when(i+1>=NOUT)
        def _(): chunk_out(i+1-NOUT).wait()
    convert(0,even); refill(0)
    def step(j,_):
        convert(2*j+1,odd); dots(2*j,even); refill(2*j+1)
        convert(2*j+2,even); dots(2*j+1,odd); refill(2*j+2)
        return 0
    lax.fori_loop(0,n//2-1,step,0)
    convert(n-1,odd); chunk_out(n-1).start(); dots(n-2,even); dots(n-1,odd)
    def fin(b,_):
        for k in range(4): af[b*4+k]=acc[b*4+k].astype(BF)
        return 0
    lax.fori_loop(0,pl.cdiv(nb,4),fin,0)
    c3=pltpu.make_async_copy(af,af_out,sem_o.at[2]); c3.start()
    lax.fori_loop(jnp.maximum(n-NOUT,0),n,lambda i,_:(chunk_out(i).wait(),0)[1],0)
    c1.wait();c2.wait();c3.wait();co.wait()

def call_k0(sizes, blk, feat, vals, NBUF=8, NOUT=4):
    FIN,_,N=feat.shape; NB=N//128; BLK=vals.shape[0]; L=pl.cdiv(BLK+NB,128)*128; W=2*GP; SL=pl.cdiv(BLK+NB,2*GROUP)*2*GROUP
    sds=jax.ShapeDtypeStruct
    ANY=pl.BlockSpec(memory_space=pltpu.HBM); VM=pl.BlockSpec(memory_space=pltpu.VMEM); SM=pl.BlockSpec(memory_space=pltpu.SMEM)
    V=pltpu.VMEM; D=pltpu.SemaphoreType.DMA
    return pl.pallas_call(k0,
        out_shape=(pltpu.HBM((SL,128,128),BF),pltpu.HBM((8,L),I32),*[pltpu.HBM((NB,128,128),BF)]*3),
        in_specs=[SM,VM,ANY,ANY],out_specs=[ANY]*5,
        scratch_shapes=[V((8,L),I32),pltpu.SMEM((8,L),I32),V((FIN,N),F32),*[V((NB,128,128),BF)]*3,V((NB+1,128,128),F32),
            V((NBUF,W,128,128),F32),V((W,128,128),BF),V((W,128,128),BF),V((NOUT,W,128,128),BF),
            D((NBUF,)),D(()),D((2,)),D((3,)),D((NOUT,))],
        compiler_params=pltpu.CompilerParams(vmem_limit_bytes=VLIM0))(sizes,blk,feat,vals)
G0=0.7978845608; G1=0.044715
EPS=1e-5
HP=64
def for_blocks(nb,U,fn,start=0):
    full=nb//U
    def many(s,_): fn(s*U,U); return 0
    def one(b,_): fn(b,1); return 0
    lax.fori_loop(start,full,many,0)
    if U>1: lax.fori_loop(full*U,nb,one,0)
def rows8(x): return jnp.sum(x.reshape(x.shape[0]//8,8,x.shape[1]),axis=0)
def blk(ref,b0,U):
    x=ref[pl.ds(b0,U)]; return x.reshape(U*x.shape[1],x.shape[2])
def put_blk(ref,b0,U,x): ref[pl.ds(b0,U)]=x.reshape((U,)+ref.shape[1:])
def gelu_half(w):
    return w+w*jnp.tanh(w*(2.0*G0+(8.0*G0*G1)*(w*w)))
def dgelu_half(w):
    q=w*w
    t=jnp.tanh(w*(2.0*G0+(8.0*G0*G1)*q))
    return (1.0+t)*(0.5+(w*(G0+(12.0*G0*G1)*q))*(1.0-t))

def moments(sums,shift,count):
    d=jnp.sum(sums[0],axis=0,keepdims=True)/count
    v=jnp.sum(sums[1],axis=0,keepdims=True)/count-d*d
    return shift+d,lax.rsqrt(v+EPS)

def slot_nodes(pairs):
    R,K=pairs.shape; G=R//2
    x=jnp.concatenate([pairs[...].astype(F32),jnp.zeros((R,128-K),F32)],axis=1)
    if R%128: x=jnp.concatenate([x,jnp.zeros((128-R%128,128),F32)],axis=0)
    x=x.T[:K].astype(I32)
    return jnp.concatenate([x[:,t*G+g:t*G+g+1] for g in range(G) for t in range(2)],axis=0)
def one_hot(slots,b):
    return jnp.where(slots==lax.broadcasted_iota(I32,(1,128),1)+b*128,1.0,0.0).astype(BF)

def prepare(x,w1_out,w2_out,wh_out,npar_out,wt_out,w2m_out,ncol_out,CP):
    n_col=len(x)
    H=w1_out.shape[0]; MY=H//n_col; nk=H//128
    col=lax.axis_index("col")
    back=lax.rem(H-col*MY,H)
    heads=([],[]); norms=[]; mine=([],[])
    for k in range(n_col):
        r=slice(k*MY,k*MY+MY)
        q=2*nk*MY
        h,l=split(x[k][q:q+MY,:])
        w1_out[r,:]=jnp.concatenate([h,h,l,x[k][q+MY:q+2*MY,:].astype(BF)],axis=1)
        two=[]
        for half in range(2):
            w=jnp.concatenate([x[k][(half*nk+i)*MY:(half*nk+i+1)*MY,:] for i in range(nk)],axis=1)
            w=pltpu.roll(w,back,1)
            mine[half].append(w[:,:128])
            h,l=split(w); two+=[h,h,l]
            heads[half].append(x[k][q+2*MY+half*CP:q+2*MY+(half+1)*CP,:MY])
        w2_out[r,:]=jnp.concatenate(two,axis=1)
        norms.append(x[k][q+2*MY+2*CP:q+2*MY+2*CP+8,:MY])
    npar=jnp.concatenate(norms,axis=1)
    npar_out[...]=npar
    ncol_out[...]=npar[:,:128].T[:MY]
    (ch,cl),(dh,dl)=[split(jnp.concatenate(p,axis=1)) for p in heads]
    z=jnp.zeros((HP-CP,H),BF)
    wh_out[...]=jnp.concatenate([ch,z,dh,z,cl,z,dl,z],axis=0)
    z=jnp.zeros((128-2*CP,H),BF)
    th=jnp.concatenate([ch,dh,z],axis=0); tl=jnp.concatenate([cl,dl,z],axis=0)
    wt_out[...]=jnp.concatenate([th,th,tl],axis=0)
    for half in range(2):
        h,l=split(jnp.concatenate(mine[half],axis=0).T[:MY])
        w2m_out[2*half*MY:(2*half+2)*MY,:]=jnp.concatenate([h,l],axis=0)

def kb(sizes,lists,pairs,S_in,fth_in,ftl_in,af_in,*refs,n_col):
    shards=refs[:n_col]
    (
       h1h_out,h1l_out,pre,pre1,st,h2t,lg,own_out,S,npar,wt,w2m,ncol,
       w1,w2,wh,fth,ftl,af,h1h,h1l,acc,zz,sums,sem_i,sem_o,sem_S)=refs[n_col:]
    nb,_,_=my_sizes(sizes); NB=fth.shape[0]; CP=lg.shape[1]; MY=pre1.shape[1]
    count=(nb*128).astype(F32)
    cs=[pltpu.make_async_copy(a,b,sem_i.at[i]) for i,(a,b) in enumerate(((fth_in,fth),(ftl_in,ftl),(af_in,af)))]
    for c in cs: c.start()
    S_start,S_wait=load_S(lists,S_in,S,sem_S); S_start()
    S[S_in.shape[0]]=jnp.zeros((128,128),BF)
    st[...]=jnp.zeros_like(st)
    prepare(shards,w1,w2,wh,npar,wt,w2m,ncol,CP)
    for c in cs: c.wait()
    def first(b0,U):
        h=blk(fth,b0,U)
        x=jnp.concatenate([h,blk(ftl,b0,U),h,blk(af,b0,U)],axis=1)
        return dot_nt(x,w1[...])
    def second(b0,U):
        h=blk(h1h,b0,U); l=blk(h1l,b0,U); ah,al=split(blk(acc,b0,U))
        return dot_nt(jnp.concatenate([h,l,h,ah,al,ah],axis=1),w2[...])
    def layer(fn,mine):
        shift=jnp.sum(fn(0,1),axis=0,keepdims=True)/128.0
        sums[...]=jnp.zeros_like(sums)
        def tile(b0,U):
            y=fn(b0,U)
            put_blk(pre,b0,U,y)
            if mine:
                for k in range(U): pre1[b0+k]=y[k*128:k*128+128,:MY].T
            d=y-shift
            sums[0]+=rows8(d); sums[1]+=rows8(d*d)
        for_blocks(nb,8,tile)
        return moments(sums,shift,count)
    mean,inv=layer(first,True)
    st[0:1,:]=mean; st[1:2,:]=inv
    a=npar[0:1,:]*inv; c=npar[1:2,:]-mean*a
    a=0.5*a; c=0.5*c
    def n1(b0,U):
        h,l=split(gelu_half(blk(pre,b0,U)*a+c))
        put_blk(h1h,b0,U,h); put_blk(h1l,b0,U,l)
        put_blk(acc,b0,U,jnp.zeros((U*128,acc.shape[2]),F32))
    for_blocks(nb,8,n1)
    acc[NB]=jnp.zeros(acc.shape[1:],F32)
    outs=[pltpu.make_async_copy(x,y,sem_o.at[i]) for i,(x,y) in enumerate(((h1h,h1h_out),(h1l,h1l_out)))]
    for o in outs: o.start()
    S_wait()
    agg_nodes(lists,S,h1h,acc)
    mean2,inv2=layer(second,False)
    st[2:3,:]=mean2; st[3:4,:]=inv2
    a2=npar[2:3,:]*inv2; c2=npar[3:4,:]-mean2*a2
    a2=0.5*a2; c2=0.5*c2
    def n2(b0,U):
        h,l=split(gelu_half(blk(pre,b0,U)*a2+c2))
        r=dot_nt(h,wh[...])
        dz=r[:,:2*HP]+r[:,2*HP:]+dot_nt(l,wh[0:2*HP,:])
        zh,zl=split(dz)
        put_blk(zz,b0,U,jnp.concatenate([zh[:,HP:],zl[:,HP:]],axis=1))
        put_blk(acc,b0,U,jnp.concatenate([dz,jnp.zeros_like(dz)],axis=1))
        t=jnp.concatenate([h[:,:MY],l[:,:MY]],axis=1)
        for k in range(U): h2t[b0+k]=t[k*128:k*128+128].T
    for_blocks(nb,8,n2)
    agg_nodes(lists,S,zz,acc,slice(2*HP,4*HP))
    def fin(b0,U):
        for k in range(U):
            x=acc[b0+k]; s=x[:,2*HP:]
            y=x[:,:2*HP]+s+pltpu.roll(s,HP,1)
            acc[b0+k,:,:2*HP]=y
            lg[b0+k]=y.T[:CP]
    for_blocks(nb,8,fin)
    G=pairs.shape[0]//2; K=pairs.shape[1]
    lane=lax.broadcasted_iota(I32,(1,128),1); sub=lax.broadcasted_iota(I32,(8,1),0)
    def slot(g,_):
        for t in range(2):
            for k0 in range(0,K,8):
                o=jnp.zeros((8,128),F32)
                for k in range(8):
                    n=pairs[t*G+g,k0+k]
                    x=acc[n>>7,pl.ds(pl.multiple_of(((n>>3)&15)*8,8),8),:2*HP]
                    o=jnp.where(sub==k,jnp.sum(jnp.where(sub==(n&7),x,0.0),axis=0,keepdims=True),o)
                own_out[g,pl.ds(pl.multiple_of(t*K+k0,8),8),:]=jnp.where(lane<CP,o,0.0)
        return 0
    lax.fori_loop(0,G,slot,0)
    for o in outs: o.wait()

def call_kb(sizes,lists,S,fth,ftl,af,shards,pairs,MY,CP):
    n_col=len(shards); NB=fth.shape[0]; H=MY*n_col; SL=S.shape[0]; G=pairs.shape[0]//2; K=pairs.shape[1]
    sds=jax.ShapeDtypeStruct
    ANY=pl.BlockSpec(memory_space=pltpu.HBM); VM=pl.BlockSpec(memory_space=pltpu.VMEM); SM=pl.BlockSpec(memory_space=pltpu.SMEM)
    V=pltpu.VMEM
    return pl.pallas_call(functools.partial(kb,n_col=n_col),
        out_shape=(pltpu.HBM((NB,128,H),BF),pltpu.HBM((NB,128,H),BF),V((NB,128,H),F32),V((NB,MY,128),F32),sds((8,H),F32),V((NB,2*MY,128),BF),V((NB,CP,128),F32),V((G,2*K,128),F32),V((SL+1,128,128),BF),sds((8,H),F32),sds((384,H),BF),sds((4*MY,H),BF),sds((MY,8),F32)),
        in_specs=[SM]*3+[ANY]*4+[VM]*n_col,out_specs=[ANY]*2+[VM]*11,
        scratch_shapes=[V((H,512),BF),V((H,6*H),BF),V((4*HP,H),BF)]+[V((NB,128,128),BF)]*3+[V((NB,128,H),BF)]*2+[V((NB+1,128,H),F32),V((NB,128,2*HP),BF),V((2,8,H),F32),pltpu.SemaphoreType.DMA((3,)),pltpu.SemaphoreType.DMA((2,)),pltpu.SemaphoreType.DMA((SL//(2*GP),))],
        compiler_params=pltpu.CompilerParams(vmem_limit_bytes=VLIM))(sizes,lists,pairs,S,fth,ftl,af,*shards)


def kc(sizes,lists,S,pre,pre1,h2t,lg,h1h_in,h1l_in,fth_in,ftl_in,af_in,st,own,recv,labels,pairs,wt,w2m,npar,ncol,
       g_out,
       rh,rl,rfh,rfl,raf,du,gz,acc,v4,sums,cross,RH,RS,RL,R1,R2,colsum,sem_r,CLS):
    nb,_,nodes=my_sizes(sizes); NB=pre.shape[0]; CP=lg.shape[1]; MY=ncol.shape[0]; H=pre.shape[2]; NS=rh.shape[0]; U8=rh.shape[1]
    count=(nb*128).astype(F32); total=nodes.astype(F32)
    nch=pl.cdiv(nb,U8)
    def ring(i):
        s=lax.rem(i,NS)
        return [pltpu.make_async_copy(a.at[pl.ds(i*U8,U8)],b.at[s],sem_r.at[s,k]) for k,(a,b) in enumerate(((h1h_in,rh),(h1l_in,rl),(fth_in,rfh),(ftl_in,rfl),(af_in,raf)))]
    for i in range(NS):
        @pl.when(i<nch)
        def _():
            for c in ring(i): c.start()
    for r in (sums,cross,RH,RS,RL,R1,R2,colsum): r[...]=jnp.zeros_like(r)
    acc[NB]=jnp.zeros(acc.shape[1:],F32)
    half=pairs.shape[1]
    G=pairs.shape[0]//2
    r=recv[...]
    D=own[...]-jnp.concatenate([r[:,half:],r[:,:half]],axis=1)
    pair_loss=0.5*jnp.sum(D[:,half:]*D[:,half:])
    Dh,Dl=split((D.reshape(2*G*half,128).T)[:CP]/total); D2=jnp.concatenate([Dh,Dl],axis=0)
    slots=slot_nodes(pairs)
    def soft(b0,U):
        hot=jnp.concatenate([one_hot(slots,b0+k) for k in range(U)],axis=1)
        add=dot(D2,hot); add=add[:CP]+add[CP:]
        x=jnp.concatenate([lg[b0+k] for k in range(U)],axis=1)
        lab=jnp.concatenate([labels[b0+k] for k in range(U)],axis=1)
        row=lax.broadcasted_iota(I32,(CP,1),0)
        xm=jnp.where(row<CLS,x,-1e30)
        mx=jnp.max(xm,axis=0,keepdims=True)
        e=jnp.exp(xm-mx); s=jnp.sum(e,axis=0,keepdims=True)
        hit=jnp.where(row==lab,1.0,0.0)
        c=mx+jnp.log(s)-jnp.sum(hit*x,axis=0,keepdims=True)
        g=(e/s-hit)/total+add
        h,l=split(g)
        for k in range(U):
            w=slice(k*128,k*128+128)
            cross[...]+=c[:,w]
            gz[b0+k]=jnp.concatenate([h[:,w],l[:,w]],axis=0)
            acc[b0+k,:2*CP]=jnp.zeros((2*CP,128),F32)
    for_blocks(nb,8,soft)
    agg_rows(lists,S,gz,acc,slice(0,2*CP))
    mean2=st[2:3,:]; inv2=st[3:4,:]
    a2=npar[2:3,:]*inv2; c2=npar[3:4,:]-mean2*a2
    ha2=0.5*a2; hc2=0.5*c2
    def back2(b0,U):
        th=[];tl=[];ads=[]
        z=jnp.zeros((128-2*CP,128),BF)
        for k in range(U):
            ad=acc[b0+k,:2*CP]; ah,al=split(ad[:CP]+ad[CP:]); gk=gz[b0+k]
            th.append(jnp.concatenate([gk[:CP],ah,z],axis=0).T); tl.append(jnp.concatenate([gk[CP:],al,z],axis=0).T)
            ads.append(ah)
        th=jnp.concatenate(th,axis=0); tl=jnp.concatenate(tl,axis=0)
        gh=dot(jnp.concatenate([th,tl,th],axis=1),wt[...])
        hh=jnp.concatenate([h2t[b0+k] for k in range(U)],axis=1)
        gg=jnp.concatenate([jnp.concatenate([gz[b0+k] for k in range(U)],axis=1),jnp.concatenate(ads,axis=1)],axis=0)
        RH[...]+=dot_nt(hh,gg)
        y=blk(pre,b0,U)
        d=gh*dgelu_half(y*ha2+hc2)
        put_blk(du,b0,U,d)
        sums[0]+=rows8(d); sums[1]+=rows8(d*(y-mean2))
    for_blocks(nb,8,back2)
    sb2=jnp.sum(sums[0],axis=0,keepdims=True); sg2=jnp.sum(sums[1],axis=0,keepdims=True)*inv2
    A2=-a2*inv2*sg2/count; C2=-a2*sb2/count-A2*mean2
    def proj(b0,U):
        h,l=split(blk(du,b0,U)*a2+blk(pre,b0,U)*A2+C2)
        r=dot_nt(w2m[...],h); rl2=dot_nt(w2m[0:MY,:],l)
        d=r[:MY]+r[MY:2*MY]+rl2; t=(r[2*MY:3*MY]+r[3*MY:]).astype(BF)
        gt=jnp.concatenate([h[:,:MY],l[:,:MY]],axis=1)
        for k in range(U):
            w=slice(k*128,k*128+128)
            acc[b0+k]=jnp.concatenate([d[:,w],jnp.zeros((2*MY,128),F32)],axis=0)
            v4[b0+k]=jnp.concatenate([t[:,w],gt[w].T],axis=0)
    for_blocks(nb,8,proj)
    acc[NB]=jnp.zeros(acc.shape[1:],F32)
    agg_rows(lists,S,v4,acc)
    lane=lambda x: jnp.sum(x,axis=1,keepdims=True)
    stc=st[:,:128].T[:MY]
    mean1=stc[:,0:1]; inv1=stc[:,1:2]
    a1=ncol[:,0:1]*inv1; c1=ncol[:,1:2]-mean1*a1
    ha1=0.5*a1; hc1=0.5*c1
    def back1(b0,U):
        for k in range(U):
            p=pre1[b0+k]
            d=acc[b0+k,:MY]*dgelu_half(p*ha1+hc1)
            acc[b0+k,:MY]=d
            colsum[0]+=d; colsum[1]+=d*(p-mean1)
    for_blocks(nb,8,back1)
    sb1=lane(colsum[0]); sg1=lane(colsum[1])*inv1
    A1=-a1*inv1*sg1/count; C1=-a1*sb1/count-A1*mean1
    def last(i,_):
        s=lax.rem(i,NS)
        for c in ring(i): c.wait()
        def part(b0,off,U):
            f=lambda ref: ref[s,pl.ds(off,U)].reshape(U*128,ref.shape[3])
            x=[acc[b0+k] for k in range(U)]
            gh,gl=split(jnp.concatenate([x[k][:MY]*a1+pre1[b0+k]*A1+C1 for k in range(U)],axis=1))
            R1[...]+=dot(jnp.concatenate([gh,gl],axis=0),f(rfh))
            R2[...]+=dot(gh,jnp.concatenate([f(rfl),f(raf)],axis=1))
            ah,al=split(jnp.concatenate([x[k][MY:2*MY]+x[k][2*MY:] for k in range(U)],axis=1))
            gt=jnp.concatenate([v4[b0+k,MY:] for k in range(U)],axis=1)
            RS[...]+=dot(jnp.concatenate([gt,ah,al],axis=0),f(rh))
            RL[...]+=dot(jnp.concatenate([gt[:MY],ah],axis=0),f(rl))
        @pl.when((i+1)*U8<=nb)
        def _(): part(i*U8,0,U8)
        @pl.when((i+1)*U8>nb)
        def _():
            lax.fori_loop(0,nb-i*U8,lambda k,_:(part(i*U8+k,k,1),0)[1],0)
        @pl.when(i+NS<nch)
        def _():
            for c in ring(i+NS): c.start()
        return 0
    lax.fori_loop(0,nch,last,0)
    RSv=RS[...]; RLv=RL[...]; nk=H//128
    for h in range(2):
        gs=RSv[2*h*MY:(2*h+1)*MY]+RSv[(2*h+1)*MY:(2*h+2)*MY]+RLv[h*MY:(h+1)*MY]
        for k in range(nk): g_out[(h*nk+k)*MY:(h*nk+k+1)*MY,:]=gs[:,k*128:k*128+128]
    R1v=R1[...]; R2v=R2[...]
    q=2*nk*MY
    g_out[q:q+MY,:]=R1v[:MY]+R1v[MY:]+R2v[:,:128]
    g_out[q+MY:q+2*MY,:]=R2v[:,128:]
    RHv=RH[...]; gh=RHv[:MY]+RHv[MY:]
    loss=jnp.sum(cross[...])+pair_loss
    extra=jnp.concatenate([sg2[:,:128],sb2[:,:128],jnp.broadcast_to(loss,(1,128)),jnp.zeros((5,128),F32)],axis=0).T[:MY]
    gh=jnp.concatenate([RHv[:MY,:CP]+RHv[:MY,CP:2*CP]+RHv[MY:,:CP],gh[:,2*CP:3*CP],sg1,sb1,extra,jnp.zeros((MY,128-2*CP-10),F32)],axis=1)
    g_out[q+2*MY:q+3*MY,:]=gh
    if g_out.shape[0]>q+3*MY: g_out[q+3*MY:,:]=jnp.zeros((g_out.shape[0]-q-3*MY,128),F32)

def call_kc(sizes,lists,S,fth,ftl,af,h1h,h1l,pre,pre1,h2t,lg,st,own,recv,labels,pairs,wt,w2m,npar,ncol,CLS,rows):
    NB=fth.shape[0]; H=pre.shape[2]; CP=lg.shape[1]; MY=ncol.shape[0]; NS=3; U8=8
    ANY=pl.BlockSpec(memory_space=pltpu.HBM); VM=pl.BlockSpec(memory_space=pltpu.VMEM); SM=pl.BlockSpec(memory_space=pltpu.SMEM)
    V=pltpu.VMEM
    return pl.pallas_call(functools.partial(kc,CLS=CLS),out_shape=jax.ShapeDtypeStruct((rows,128),F32),
        in_specs=[SM,SM]+[VM]*5+[ANY]*5+[VM]*9,out_specs=VM,
        scratch_shapes=[V((NS,U8,128,H),BF)]*2+[V((NS,U8,128,128),BF)]*3+[
            V((NB,128,H),F32),V((NB,2*CP,128),BF),V((NB+1,max(3*MY,2*CP),128),F32),V((NB,3*MY,128),BF),
            V((2,8,H),F32),V((1,128),F32),V((2*MY,3*CP),F32),V((4*MY,H),F32),V((2*MY,H),F32),V((2*MY,128),F32),V((MY,256),F32),V((2,MY,128),F32),
            pltpu.SemaphoreType.DMA((NS,5))],
        compiler_params=pltpu.CompilerParams(vmem_limit_bytes=VLIM))(sizes,lists,*in_vmem(S,pre,pre1,h2t,lg),h1h,h1l,fth,ftl,af,st,*in_vmem(own,recv),labels,pairs,wt,w2m,npar,ncol)

def at(index): return {"graph": index}
def meet(n):
    me=lax.axis_index("graph")
    barrier=pltpu.get_barrier_semaphore()
    for k in range(1,n):
        pl.semaphore_signal(barrier,inc=1,device_id=at(lax.rem(me+k,n)),device_id_type=pl.DeviceIdType.MESH)
    pl.semaphore_wait(barrier,n-1)

def kx(own,out,send,recv,n):
    me=lax.axis_index("graph")
    meet(n)
    copies=[]
    for k in range(1,n):
        peer=lax.rem(me+k,n)
        c=pltpu.make_async_remote_copy(src_ref=own.at[peer],dst_ref=out.at[me],send_sem=send.at[k-1],recv_sem=recv.at[k-1],
            device_id=at(peer),device_id_type=pl.DeviceIdType.MESH)
        c.start(); copies.append(c)
    out[me]=own[me]
    for c in copies: c.wait()

def call_kx(own,n):
    VM=pl.BlockSpec(memory_space=pltpu.VMEM)
    return pl.pallas_call(functools.partial(kx,n=n),out_shape=pltpu.VMEM(own.shape,own.dtype),in_specs=[VM],out_specs=VM,
        scratch_shapes=[pltpu.SemaphoreType.DMA((n-1,)),pltpu.SemaphoreType.DMA((n-1,))],
        compiler_params=pltpu.CompilerParams(vmem_limit_bytes=8<<20,collective_id=1,has_side_effects=True))(*in_vmem(own))

def kr(g,out,parts,send1,recv1,send2,recv2,n):
    me=lax.axis_index("graph")
    piece=g.shape[0]//n
    def rows(i): return pl.ds(pl.multiple_of(i*piece,8),piece)
    meet(n)
    copies=[]
    for k in range(1,n):
        peer=lax.rem(me+k,n)
        c=pltpu.make_async_remote_copy(src_ref=g.at[rows(peer)],dst_ref=parts.at[k-1],send_sem=send1.at[k-1],recv_sem=recv1.at[k-1],
            device_id=at(peer),device_id_type=pl.DeviceIdType.MESH)
        c.start(); copies.append(c)
    total=g[rows(me),:]
    for k,c in enumerate(copies):
        c.wait_recv(); total+=parts[k]
    out[rows(me),:]=total
    back=[]
    for k in range(1,n):
        peer=lax.rem(me+k,n)
        c=pltpu.make_async_remote_copy(src_ref=out.at[rows(me)],dst_ref=out.at[rows(me)],send_sem=send2.at[k-1],recv_sem=recv2.at[k-1],
            device_id=at(peer),device_id_type=pl.DeviceIdType.MESH)
        c.start(); back.append(c)
    for c in copies: c.wait_send()
    for c in back: c.wait()

def call_kr(g,n):
    VM=pl.BlockSpec(memory_space=pltpu.VMEM); D=pltpu.SemaphoreType.DMA((n-1,))
    return pl.pallas_call(functools.partial(kr,n=n),out_shape=jax.ShapeDtypeStruct(g.shape,g.dtype),in_specs=[VM],out_specs=VM,
        scratch_shapes=[pltpu.VMEM((n-1,g.shape[0]//n,128),F32),D,D,D,D],
        compiler_params=pltpu.CompilerParams(collective_id=2,has_side_effects=True))(g)

def kp(wf,ws,wh,npar,out):
    _,MY,FIN=wf.shape; H=ws.shape[2]; CLS=wh.shape[0]; CP=-(-CLS//16)*16; nk=H//128
    out[...]=jnp.zeros_like(out)
    for h in range(2):
        for k in range(nk):
            r=(h*nk+k)*MY; out[r:r+MY,:]=ws[h,:,k*128:k*128+128]
        r=2*nk*MY+h*MY; out[r:r+MY,:FIN]=wf[h]
        r=2*nk*MY+2*MY+h*CP; out[r:r+CLS,:MY]=wh[:,h,:]
        r=2*nk*MY+2*MY+2*CP+2*h; out[r:r+2,:MY]=npar[h]

def call_kp(wf,ws,wh,npar):
    _,MY,FIN=wf.shape; H=ws.shape[2]; CP=-(-wh.shape[0]//16)*16
    rows=-(-(2*H//128*MY+2*MY+2*CP+8)//16)*16
    VM=pl.BlockSpec(memory_space=pltpu.VMEM)
    return pl.pallas_call(kp,out_shape=jax.ShapeDtypeStruct((rows,128),F32),in_specs=[VM]*4,out_specs=VM)(wf,ws,wh,npar)

def renew(weight, momentum, average, gradient):
    momentum_new = MOMENTUM * momentum + gradient
    weight_new = weight - STEP_RATE * (gradient + MOMENTUM * momentum_new)
    average_new = AVERAGE_KEEP * average + (1.0 - AVERAGE_KEEP) * weight_new
    return momentum_new, average_new, weight_new

def ku(sizes,g,*refs):
    weights,momenta,averages,outs,loss,count=refs[:4],refs[4:8],refs[8:12],refs[12:24],refs[24],refs[25]
    _,MY,FIN=weights[0].shape; H=weights[1].shape[2]; CLS=weights[2].shape[0]; CP=-(-CLS//16)*16; nk=H//128
    q=2*nk*MY
    shift=lax.axis_index("col")*MY
    def store(i,where,grad):
        for o,v in zip(outs[3*i:3*i+3],renew(weights[i][where],momenta[i][where],averages[i][where],grad)): o[where]=v
    head=g[q+2*MY:q+3*MY,:].T
    for h in range(2):
        x=jnp.concatenate([g[(h*nk+k)*MY:(h*nk+k+1)*MY,:] for k in range(nk)],axis=1)
        store(1,(h,),pltpu.roll(x,shift,1))
        store(0,(h,),g[q+h*MY:q+h*MY+MY,:FIN])
        store(2,(slice(None),h,slice(None)),head[h*CP:h*CP+CLS,:MY])
    store(3,(0,),head[2*CP:2*CP+2,:MY])
    store(3,(1,),head[2*CP+2:2*CP+4,:MY])
    loss[0,0]=g[q+2*MY,2*CP+4]
    count[0,0]=my_sizes(sizes)[2].astype(F32)

def call_ku(sizes,g,weights,momenta,averages):
    VM=pl.BlockSpec(memory_space=pltpu.VMEM); SM=pl.BlockSpec(memory_space=pltpu.SMEM)
    shapes=[jax.ShapeDtypeStruct(w.shape,F32) for w in weights for _ in range(3)]
    return pl.pallas_call(ku,out_shape=(*shapes,*[jax.ShapeDtypeStruct((1,1),F32)]*2),in_specs=[SM]+[VM]*13,out_specs=[VM]*12+[SM]*2)(sizes,g,*weights,*momenta,*averages)

MOMENTUM=0.9; STEP_RATE=2.0; AVERAGE_KEEP=0.9

def per_device(n_graph, n_col, features, blocks, block_values, group_sizes, labels, pair_nodes, weight_first, weight_second, weight_head,
               norm_params, momentum_first, momentum_second, momentum_head, momentum_norms, average_first, average_second,
               average_head, average_norms):
    MY=weight_first.shape[2]; H=MY*n_col; CLS=weight_head.shape[2]; CP=-(-CLS//16)*16
    G=group_sizes.shape[0]; N=features.shape[2]; NB=N//128; PEER=pair_nodes.shape[3]
    def native(first,second,head,norms):
        return first.transpose(0,2,1),second.transpose(0,2,1),head.transpose(2,0,1),norms
    weights=native(weight_first,weight_second,weight_head,norm_params)
    momenta=native(momentum_first,momentum_second,momentum_head,momentum_norms)
    averages=native(average_first,average_second,average_head,average_norms)
    packed=call_kp(*weights)
    shards=[packed]+[lax.ppermute(packed,"col",[((j+k)%n_col,j) for j in range(n_col)]) for k in range(1,n_col)]
    sizes=group_sizes.T
    S,lists,fth,ftl,af=call_k0(sizes,blocks[0],features.transpose(1,0,2),block_values[0])
    pairs=pair_nodes[0].reshape(2*G,PEER)
    h1h,h1l,pre,pre1,st,h2t,lg,own,S,npar,wt,w2m,ncol=call_kb(sizes,lists,S,fth,ftl,af,shards,pairs,MY=MY,CP=CP)
    recv=call_kx(own,n_graph)
    unit=8*n_graph; rows=-(-(2*H//128*MY+3*MY)//unit)*unit
    g=call_kc(sizes,lists,S,fth,ftl,af,h1h,h1l,pre,pre1,h2t,lg,st,own,recv,labels[0].reshape(NB,1,128),pairs,wt,w2m,npar,ncol,CLS=CLS,rows=rows)
    g=call_kr(g,n_graph)
    *new,loss,count=call_ku(sizes,g,weights,momenta,averages)
    first=[x.transpose(0,2,1) for x in new[0:3]]
    second=[x.transpose(0,2,1) for x in new[3:6]]
    head=[x.transpose(1,2,0) for x in new[6:9]]
    return (loss[0,0],count[0,0],*first,*second,*head,*new[9:12])

def solution(mesh):
    P=jax.sharding.PartitionSpec
    unit=P(None,None,"col"); head=P(None,"col",None)
    weights=(unit,unit,head,unit)
    in_specs=(P("graph",None,None),P("graph",None,None),P("graph",None,None,None),P(),P("graph",None),P("graph",None,None,None))+weights*3
    out_specs=(P(),P())+(unit,)*6+(head,)*3+(unit,)*3
    return jax.shard_map(functools.partial(per_device,mesh.shape["graph"],mesh.shape["col"]),mesh=mesh,in_specs=in_specs,out_specs=out_specs,check_vma=False)
```

```python
import functools
import jax, jax.numpy as jnp
from jax import lax
from jax.experimental import pallas as pl
from jax.experimental.pallas import tpu as pltpu
BF=jnp.bfloat16; F32=jnp.float32; I32=jnp.int32
VLIM0=58<<20
VLIM=31<<20
def dot(a,b): return jnp.dot(a,b,preferred_element_type=F32)
def dot_nt(a,b): return lax.dot_general(a,b,(((1,),(1,)),((),())),preferred_element_type=F32)
def split(x):
    h=x.astype(BF); return h,(x-h.astype(F32)).astype(BF)
GROUP=96
GP=16

def my_sizes(sizes):
    me=lax.axis_index("graph")
    total=sizes[0,0]
    for g in range(1,sizes.shape[1]): total+=sizes[0,g]
    return sizes[0,me]>>7, sizes[1,me], total

def sort_list(keys_l, keys_c, enc, lb, null, L):
    BLK=keys_l.shape[1]
    b_c=lax.broadcasted_iota(I32,(BLK,1),0); b_l=lax.broadcasted_iota(I32,(1,BLK),1)
    live=b_c<lb
    r_l=lax.broadcasted_iota(I32,(1,128),1); p_l=lax.broadcasted_iota(I32,(1,L),1)
    rank=jnp.sum(jnp.where((keys_l==keys_c)&(b_l<b_c),1.0,0.0),axis=1,keepdims=True)
    cnt=jnp.sum(jnp.where((keys_c==r_l)&live,1.0,0.0),axis=0,keepdims=True)
    even=2.0*jnp.floor(0.5*cnt+0.5)
    start=jnp.sum(jnp.where(r_l<keys_c,even,0.0),axis=1,keepdims=True)
    pos=jnp.where(live,(start+rank).astype(I32),-1)
    enc=enc-null; here=pos==p_l
    lo=jnp.sum(jnp.where(here,(enc&0xfff).astype(F32),0.0),axis=0,keepdims=True).astype(I32)
    hi=jnp.sum(jnp.where(here,(enc>>12).astype(F32),0.0),axis=0,keepdims=True).astype(I32)
    return hi*4096+lo+null,pos,jnp.sum(even,axis=1,keepdims=True).astype(I32)

def pair_fields(lists, which, q):
    e0=lists[which,2*q]; e1=lists[which,2*q+1]
    return e0>>20, (e0>>12)&0xff, (e1>>12)&0xff, e0&0xfff, e1&0xfff

def agg_nodes(lists, S, v, acc, lanes=slice(None)):
    n=lists[2,0]//2
    def step(s,_):
        for u in range(GROUP):
            q=s*GROUP+u
            r,c0,c1,_,_=pair_fields(lists,0,q)
            rhs=jnp.concatenate([v[c0],v[c1]],axis=0)
            acc[r,:,lanes]+=dot(jnp.concatenate([S[2*q],S[2*q+1]],axis=1),rhs)
        return 0
    lax.fori_loop(0,pl.cdiv(n,GROUP),step,0)

def load_S(lists, S_in, S, sems):
    n=2*pl.cdiv(lists[2,0],4*GP)
    def one(i): return pltpu.make_async_copy(S_in.at[pl.ds(i*2*GP,2*GP)],S.at[pl.ds(i*2*GP,2*GP)],sems.at[i])
    def start(): lax.fori_loop(0,n,lambda i,_:(one(i).start(),0)[1],0)
    def wait(): lax.fori_loop(0,n,lambda i,_:(one(i).wait(),0)[1],0)
    return start,wait

def in_vmem(*arrays): return [pltpu.with_memory_space_constraint(x,pltpu.VMEM) for x in arrays]

def agg_rows(lists, S, v, acc, rows=slice(None)):
    n=lists[3,0]//2
    def step(s,_):
        for u in range(GROUP):
            r,c0,c1,b0,b1=pair_fields(lists,1,s*GROUP+u)
            lhs=jnp.concatenate([v[c0],v[c1]],axis=1)
            acc[r,rows]+=dot(lhs,jnp.concatenate([S[b0],S[b1]],axis=0))
        return 0
    lax.fori_loop(0,pl.cdiv(n,GROUP),step,0)

def k0(sizes, blk_l, feat, vals, S_out, lists_out, fth_out, ftl_out, af_out,
       lists_v, lists_s, ft_v, fth, ftl, af, acc, buf, even, odd, ring, sem_in, sem_f, sem_l, sem_o, sem_S):
    nb,lb,_=my_sizes(sizes)
    NB=acc.shape[0]-1; BLK=vals.shape[0]; FIN=feat.shape[0]; NBUF=buf.shape[0]; NOUT=ring.shape[0]; SL=S_out.shape[0]
    L=lists_v.shape[1]; W=2*GP
    cf=pltpu.make_async_copy(feat.at[:,0],ft_v,sem_f); cf.start()
    ids=blk_l[...]
    columns=jnp.concatenate([ids.astype(F32),jnp.zeros((6,BLK),F32)],axis=0).T.astype(I32)
    rows=columns[:,0:1]; cols=columns[:,1:2]
    order=lax.broadcasted_iota(I32,(BLK,1),0)
    l0,pos,n0=sort_list(ids[0:1],rows,order+cols*(1<<12)+rows*(1<<20),lb,BLK+(NB<<20),L)
    lists_v[0:1,:]=l0; lists_v[2:3,:]=jnp.broadcast_to(n0,(1,L))
    cl=pltpu.make_async_copy(lists_v,lists_s,sem_l.at[0]); cl.start()
    acc[...]=jnp.zeros(acc.shape,F32)
    cl.wait()
    n=2*pl.cdiv(lists_s[2,0],4*GP)
    def chunk_start(i):
        slot=lax.rem(i,NBUF)
        for k in range(W):
            b=lists_s[0,i*W+k]&0xfff
            pltpu.make_async_copy(vals.at[jnp.where(b<BLK,b,0)],buf.at[slot,k],sem_in.at[slot]).start()
    def chunk_wait(i):
        slot=lax.rem(i,NBUF)
        pltpu.make_async_copy(vals.at[pl.ds(0,W)],buf.at[slot],sem_in.at[slot]).wait()
    lax.fori_loop(0,jnp.minimum(n,NBUF),lambda i,_:(chunk_start(i),0)[1],0)
    l1,_,n1=sort_list(ids[1:2],cols,pos+rows*(1<<12)+cols*(1<<20),lb,SL+(NB<<20),L)
    lists_v[1:2,:]=l1; lists_v[3:4,:]=jnp.broadcast_to(n1,(1,L))
    co=pltpu.make_async_copy(lists_v,lists_out,sem_l.at[1]); co.start()
    cf.wait()
    def tr(i,_):
        for k in range(4):
            b=i*4+k
            x=ft_v[:,pl.ds(pl.multiple_of(b*128,128),128)]
            x=jnp.concatenate([x,jnp.zeros((128-FIN,128),F32)],axis=0).T
            h,l=split(x); fth[b]=h; ftl[b]=l
        return 0
    lax.fori_loop(0,pl.cdiv(nb,4),tr,0)
    c1=pltpu.make_async_copy(fth,fth_out,sem_o.at[0]); c1.start()
    c2=pltpu.make_async_copy(ftl,ftl_out,sem_o.at[1]); c2.start()
    def chunk_out(i): return pltpu.make_async_copy(ring.at[lax.rem(i,NOUT)],S_out.at[pl.ds(i*W,W)],sem_S.at[lax.rem(i,NOUT)])
    def convert(i,stage):
        slot=lax.rem(i,NBUF); o=lax.rem(i,NOUT)
        chunk_wait(i)
        for k in range(W):
            x=jnp.where(lists_s[0,i*W+k]&0xfff<BLK,buf[slot,k],0.0).T.astype(BF)
            stage[k]=x; ring[o,k]=x
    def dots(i,stage):
        for u in range(GP):
            r,f0,f1,_,_=pair_fields(lists_s,0,i*GP+u)
            acc[r]+=dot(jnp.concatenate([stage[2*u],stage[2*u+1]],axis=1),jnp.concatenate([fth[f0],fth[f1]],axis=0))
    def refill(i):
        chunk_out(i).start()
        @pl.when(i+NBUF<n)
        def _(): chunk_start(i+NBUF)
        @pl.when(i+1>=NOUT)
        def _(): chunk_out(i+1-NOUT).wait()
    convert(0,even); refill(0)
    def step(j,_):
        convert(2*j+1,odd); dots(2*j,even); refill(2*j+1)
        convert(2*j+2,even); dots(2*j+1,odd); refill(2*j+2)
        return 0
    lax.fori_loop(0,n//2-1,step,0)
    convert(n-1,odd); chunk_out(n-1).start(); dots(n-2,even); dots(n-1,odd)
    def fin(b,_):
        for k in range(4): af[b*4+k]=acc[b*4+k].astype(BF)
        return 0
    lax.fori_loop(0,pl.cdiv(nb,4),fin,0)
    c3=pltpu.make_async_copy(af,af_out,sem_o.at[2]); c3.start()
    lax.fori_loop(jnp.maximum(n-NOUT,0),n,lambda i,_:(chunk_out(i).wait(),0)[1],0)
    c1.wait();c2.wait();c3.wait();co.wait()

def call_k0(sizes, blk, feat, vals, NBUF=8, NOUT=4):
    FIN,_,N=feat.shape; NB=N//128; BLK=vals.shape[0]; L=pl.cdiv(BLK+NB,128)*128; W=2*GP; SL=pl.cdiv(BLK+NB,2*GROUP)*2*GROUP
    sds=jax.ShapeDtypeStruct
    ANY=pl.BlockSpec(memory_space=pltpu.HBM); VM=pl.BlockSpec(memory_space=pltpu.VMEM); SM=pl.BlockSpec(memory_space=pltpu.SMEM)
    V=pltpu.VMEM; D=pltpu.SemaphoreType.DMA
    return pl.pallas_call(k0,
        out_shape=(pltpu.HBM((SL,128,128),BF),pltpu.HBM((8,L),I32),*[pltpu.HBM((NB,128,128),BF)]*3),
        in_specs=[SM,VM,ANY,ANY],out_specs=[ANY]*5,
        scratch_shapes=[V((8,L),I32),pltpu.SMEM((8,L),I32),V((FIN,N),F32),*[V((NB,128,128),BF)]*3,V((NB+1,128,128),F32),
            V((NBUF,W,128,128),F32),V((W,128,128),BF),V((W,128,128),BF),V((NOUT,W,128,128),BF),
            D((NBUF,)),D(()),D((2,)),D((3,)),D((NOUT,))],
        compiler_params=pltpu.CompilerParams(vmem_limit_bytes=VLIM0))(sizes,blk,feat,vals)
G0=0.7978845608; G1=0.044715
EPS=1e-5
HP=64
def for_blocks(nb,U,fn,start=0):
    full=nb//U
    def many(s,_): fn(s*U,U); return 0
    def one(b,_): fn(b,1); return 0
    lax.fori_loop(start,full,many,0)
    if U>1: lax.fori_loop(full*U,nb,one,0)
def rows8(x): return jnp.sum(x.reshape(x.shape[0]//8,8,x.shape[1]),axis=0)
def blk(ref,b0,U):
    x=ref[pl.ds(b0,U)]; return x.reshape(U*x.shape[1],x.shape[2])
def put_blk(ref,b0,U,x): ref[pl.ds(b0,U)]=x.reshape((U,)+ref.shape[1:])
def gelu_half(w):
    return w+w*jnp.tanh(w*(2.0*G0+(8.0*G0*G1)*(w*w)))
def dgelu_half(w):
    q=w*w
    t=jnp.tanh(w*(2.0*G0+(8.0*G0*G1)*q))
    return (1.0+t)*(0.5+(w*(G0+(12.0*G0*G1)*q))*(1.0-t))

def moments(sums,shift,count):
    d=jnp.sum(sums[0],axis=0,keepdims=True)/count
    v=jnp.sum(sums[1],axis=0,keepdims=True)/count-d*d
    return shift+d,lax.rsqrt(v+EPS)

def slot_nodes(pairs):
    R,K=pairs.shape; G=R//2
    x=jnp.concatenate([pairs[...].astype(F32),jnp.zeros((R,128-K),F32)],axis=1)
    if R%128: x=jnp.concatenate([x,jnp.zeros((128-R%128,128),F32)],axis=0)
    x=x.T[:K].astype(I32)
    return jnp.concatenate([x[:,t*G+g:t*G+g+1] for g in range(G) for t in range(2)],axis=0)
def one_hot(slots,b):
    return jnp.where(slots==lax.broadcasted_iota(I32,(1,128),1)+b*128,1.0,0.0).astype(BF)

def prepare(x,w1_out,w2_out,wh_out,npar_out,wt_out,w2m_out,ncol_out,CP):
    n_col=len(x)
    H=w1_out.shape[0]; MY=H//n_col; nk=H//128
    col=lax.axis_index("col")
    back=lax.rem(H-col*MY,H)
    heads=([],[]); norms=[]; mine=([],[])
    for k in range(n_col):
        r=slice(k*MY,k*MY+MY)
        q=2*nk*MY
        h,l=split(x[k][q:q+MY,:])
        w1_out[r,:]=jnp.concatenate([h,h,l,x[k][q+MY:q+2*MY,:].astype(BF)],axis=1)
        two=[]
        for half in range(2):
            w=jnp.concatenate([x[k][(half*nk+i)*MY:(half*nk+i+1)*MY,:] for i in range(nk)],axis=1)
            w=pltpu.roll(w,back,1)
            mine[half].append(w[:,:128])
            h,l=split(w); two+=[h,h,l]
            heads[half].append(x[k][q+2*MY+half*CP:q+2*MY+(half+1)*CP,:MY])
        w2_out[r,:]=jnp.concatenate(two,axis=1)
        norms.append(x[k][q+2*MY+2*CP:q+2*MY+2*CP+8,:MY])
    npar=jnp.concatenate(norms,axis=1)
    npar_out[...]=npar
    ncol_out[...]=npar[:,:128].T[:MY]
    (ch,cl),(dh,dl)=[split(jnp.concatenate(p,axis=1)) for p in heads]
    z=jnp.zeros((HP-CP,H),BF)
    wh_out[...]=jnp.concatenate([ch,z,dh,z,cl,z,dl,z],axis=0)
    z=jnp.zeros((128-2*CP,H),BF)
    th=jnp.concatenate([ch,dh,z],axis=0); tl=jnp.concatenate([cl,dl,z],axis=0)
    wt_out[...]=jnp.concatenate([th,th,tl],axis=0)
    for half in range(2):
        h,l=split(jnp.concatenate(mine[half],axis=0).T[:MY])
        w2m_out[2*half*MY:(2*half+2)*MY,:]=jnp.concatenate([h,l],axis=0)

def kb(sizes,lists,pairs,S_in,fth_in,ftl_in,af_in,*refs,n_col):
    shards=refs[:n_col]
    (
       h1h_out,h1l_out,pre,pre1,st,h2t,lg,own_out,S,npar,wt,w2m,ncol,
       w1,w2,wh,fth,ftl,af,h1h,h1l,acc,zz,sums,sem_i,sem_o,sem_S)=refs[n_col:]
    nb,_,_=my_sizes(sizes); NB=fth.shape[0]; CP=lg.shape[1]; MY=pre1.shape[1]
    count=(nb*128).astype(F32)
    cs=[pltpu.make_async_copy(a,b,sem_i.at[i]) for i,(a,b) in enumerate(((fth_in,fth),(ftl_in,ftl),(af_in,af)))]
    for c in cs: c.start()
    S_start,S_wait=load_S(lists,S_in,S,sem_S); S_start()
    S[S_in.shape[0]]=jnp.zeros((128,128),BF)
    st[...]=jnp.zeros_like(st)
    prepare(shards,w1,w2,wh,npar,wt,w2m,ncol,CP)
    for c in cs: c.wait()
    def first(b0,U):
        h=blk(fth,b0,U)
        x=jnp.concatenate([h,blk(ftl,b0,U),h,blk(af,b0,U)],axis=1)
        return dot_nt(x,w1[...])
    def second(b0,U):
        h=blk(h1h,b0,U); l=blk(h1l,b0,U); ah,al=split(blk(acc,b0,U))
        return dot_nt(jnp.concatenate([h,l,h,ah,al,ah],axis=1),w2[...])
    def layer(fn,mine):
        shift=jnp.sum(fn(0,1),axis=0,keepdims=True)/128.0
        sums[...]=jnp.zeros_like(sums)
        def tile(b0,U):
            y=fn(b0,U)
            put_blk(pre,b0,U,y)
            if mine:
                for k in range(U): pre1[b0+k]=y[k*128:k*128+128,:MY].T
            d=y-shift
            sums[0]+=rows8(d); sums[1]+=rows8(d*d)
        for_blocks(nb,8,tile)
        return moments(sums,shift,count)
    mean,inv=layer(first,True)
    st[0:1,:]=mean; st[1:2,:]=inv
    a=npar[0:1,:]*inv; c=npar[1:2,:]-mean*a
    a=0.5*a; c=0.5*c
    def n1(b0,U):
        h,l=split(gelu_half(blk(pre,b0,U)*a+c))
        put_blk(h1h,b0,U,h); put_blk(h1l,b0,U,l)
        put_blk(acc,b0,U,jnp.zeros((U*128,acc.shape[2]),F32))
    for_blocks(nb,8,n1)
    acc[NB]=jnp.zeros(acc.shape[1:],F32)
    outs=[pltpu.make_async_copy(x,y,sem_o.at[i]) for i,(x,y) in enumerate(((h1h,h1h_out),(h1l,h1l_out)))]
    for o in outs: o.start()
    S_wait()
    agg_nodes(lists,S,h1h,acc)
    mean2,inv2=layer(second,False)
    st[2:3,:]=mean2; st[3:4,:]=inv2
    a2=npar[2:3,:]*inv2; c2=npar[3:4,:]-mean2*a2
    a2=0.5*a2; c2=0.5*c2
    def n2(b0,U):
        h,l=split(gelu_half(blk(pre,b0,U)*a2+c2))
        r=dot_nt(h,wh[...])
        dz=r[:,:2*HP]+r[:,2*HP:]+dot_nt(l,wh[0:2*HP,:])
        zh,zl=split(dz)
        put_blk(zz,b0,U,jnp.concatenate([zh[:,HP:],zl[:,HP:]],axis=1))
        put_blk(acc,b0,U,jnp.concatenate([dz,jnp.zeros_like(dz)],axis=1))
        t=jnp.concatenate([h[:,:MY],l[:,:MY]],axis=1)
        for k in range(U): h2t[b0+k]=t[k*128:k*128+128].T
    for_blocks(nb,8,n2)
    agg_nodes(lists,S,zz,acc,slice(2*HP,4*HP))
    def fin(b0,U):
        for k in range(U):
            x=acc[b0+k]; s=x[:,2*HP:]
            y=x[:,:2*HP]+s+pltpu.roll(s,HP,1)
            acc[b0+k,:,:2*HP]=y
            lg[b0+k]=y.T[:CP]
    for_blocks(nb,16,fin)
    G=pairs.shape[0]//2; K=pairs.shape[1]
    lane=lax.broadcasted_iota(I32,(1,128),1); sub=lax.broadcasted_iota(I32,(8,1),0)
    def slot(g,_):
        for t in range(2):
            for k0 in range(0,K,8):
                o=jnp.zeros((8,128),F32)
                for k in range(8):
                    n=pairs[t*G+g,k0+k]
                    x=acc[n>>7,pl.ds(pl.multiple_of(((n>>3)&15)*8,8),8),:2*HP]
                    o=jnp.where(sub==k,jnp.sum(jnp.where(sub==(n&7),x,0.0),axis=0,keepdims=True),o)
                own_out[g,pl.ds(pl.multiple_of(t*K+k0,8),8),:]=jnp.where(lane<CP,o,0.0)
        return 0
    lax.fori_loop(0,G,slot,0)
    for o in outs: o.wait()

def call_kb(sizes,lists,S,fth,ftl,af,shards,pairs,MY,CP):
    n_col=len(shards); NB=fth.shape[0]; H=MY*n_col; SL=S.shape[0]; G=pairs.shape[0]//2; K=pairs.shape[1]
    sds=jax.ShapeDtypeStruct
    ANY=pl.BlockSpec(memory_space=pltpu.HBM); VM=pl.BlockSpec(memory_space=pltpu.VMEM); SM=pl.BlockSpec(memory_space=pltpu.SMEM)
    V=pltpu.VMEM
    return pl.pallas_call(functools.partial(kb,n_col=n_col),
        out_shape=(pltpu.HBM((NB,128,H),BF),pltpu.HBM((NB,128,H),BF),V((NB,128,H),F32),V((NB,MY,128),F32),sds((8,H),F32),V((NB,2*MY,128),BF),V((NB,CP,128),F32),V((G,2*K,128),F32),V((SL+1,128,128),BF),sds((8,H),F32),sds((384,H),BF),sds((4*MY,H),BF),sds((MY,8),F32)),
        in_specs=[SM]*3+[ANY]*4+[VM]*n_col,out_specs=[ANY]*2+[VM]*11,
        scratch_shapes=[V((H,512),BF),V((H,6*H),BF),V((4*HP,H),BF)]+[V((NB,128,128),BF)]*3+[V((NB,128,H),BF)]*2+[V((NB+1,128,H),F32),V((NB,128,2*HP),BF),V((2,8,H),F32),pltpu.SemaphoreType.DMA((3,)),pltpu.SemaphoreType.DMA((2,)),pltpu.SemaphoreType.DMA((SL//(2*GP),))],
        compiler_params=pltpu.CompilerParams(vmem_limit_bytes=VLIM))(sizes,lists,pairs,S,fth,ftl,af,*shards)


def kc(sizes,lists,S,pre,pre1,h2t,lg,h1h_in,h1l_in,fth_in,ftl_in,af_in,st,own,recv,labels,pairs,wt,w2m,npar,ncol,
       g_out,
       rh,rl,rfh,rfl,raf,du,gz,acc,v4,sums,cross,RH,RS,RL,R1,R2,colsum,sem_r,CLS):
    nb,_,nodes=my_sizes(sizes); NB=pre.shape[0]; CP=lg.shape[1]; MY=ncol.shape[0]; H=pre.shape[2]; NS=rh.shape[0]; U8=rh.shape[1]
    count=(nb*128).astype(F32); total=nodes.astype(F32)
    nch=pl.cdiv(nb,U8)
    def ring(i):
        s=lax.rem(i,NS)
        return [pltpu.make_async_copy(a.at[pl.ds(i*U8,U8)],b.at[s],sem_r.at[s,k]) for k,(a,b) in enumerate(((h1h_in,rh),(h1l_in,rl),(fth_in,rfh),(ftl_in,rfl),(af_in,raf)))]
    for i in range(NS):
        @pl.when(i<nch)
        def _():
            for c in ring(i): c.start()
    for r in (sums,cross,RH,RS,RL,R1,R2,colsum): r[...]=jnp.zeros_like(r)
    acc[NB]=jnp.zeros(acc.shape[1:],F32)
    half=pairs.shape[1]
    G=pairs.shape[0]//2
    r=recv[...]
    D=own[...]-jnp.concatenate([r[:,half:],r[:,:half]],axis=1)
    pair_loss=0.5*jnp.sum(D[:,half:]*D[:,half:])
    Dh,Dl=split((D.reshape(2*G*half,128).T)[:CP]/total); D2=jnp.concatenate([Dh,Dl],axis=0)
    slots=slot_nodes(pairs)
    def soft(b0,U):
        hot=jnp.concatenate([one_hot(slots,b0+k) for k in range(U)],axis=1)
        add=dot(D2,hot); add=add[:CP]+add[CP:]
        x=jnp.concatenate([lg[b0+k] for k in range(U)],axis=1)
        lab=jnp.concatenate([labels[b0+k] for k in range(U)],axis=1)
        row=lax.broadcasted_iota(I32,(CP,1),0)
        xm=jnp.where(row<CLS,x,-1e30)
        mx=jnp.max(xm,axis=0,keepdims=True)
        e=jnp.exp(xm-mx); s=jnp.sum(e,axis=0,keepdims=True)
        hit=jnp.where(row==lab,1.0,0.0)
        c=mx+jnp.log(s)-jnp.sum(hit*x,axis=0,keepdims=True)
        g=(e/s-hit)/total+add
        h,l=split(g)
        for k in range(U):
            w=slice(k*128,k*128+128)
            cross[...]+=c[:,w]
            gz[b0+k]=jnp.concatenate([h[:,w],l[:,w]],axis=0)
            acc[b0+k,:2*CP]=jnp.zeros((2*CP,128),F32)
    for_blocks(nb,8,soft)
    agg_rows(lists,S,gz,acc,slice(0,2*CP))
    mean2=st[2:3,:]; inv2=st[3:4,:]
    a2=npar[2:3,:]*inv2; c2=npar[3:4,:]-mean2*a2
    ha2=0.5*a2; hc2=0.5*c2
    def back2(b0,U):
        th=[];tl=[];ads=[]
        z=jnp.zeros((128-2*CP,128),BF)
        for k in range(U):
            ad=acc[b0+k,:2*CP]; ah,al=split(ad[:CP]+ad[CP:]); gk=gz[b0+k]
            th.append(jnp.concatenate([gk[:CP],ah,z],axis=0).T); tl.append(jnp.concatenate([gk[CP:],al,z],axis=0).T)
            ads.append(ah)
        th=jnp.concatenate(th,axis=0); tl=jnp.concatenate(tl,axis=0)
        gh=dot(jnp.concatenate([th,tl,th],axis=1),wt[...])
        hh=jnp.concatenate([h2t[b0+k] for k in range(U)],axis=1)
        gg=jnp.concatenate([jnp.concatenate([gz[b0+k] for k in range(U)],axis=1),jnp.concatenate(ads,axis=1)],axis=0)
        RH[...]+=dot_nt(hh,gg)
        y=blk(pre,b0,U)
        d=gh*dgelu_half(y*ha2+hc2)
        put_blk(du,b0,U,d)
        sums[0]+=rows8(d); sums[1]+=rows8(d*(y-mean2))
    for_blocks(nb,8,back2)
    sb2=jnp.sum(sums[0],axis=0,keepdims=True); sg2=jnp.sum(sums[1],axis=0,keepdims=True)*inv2
    A2=-a2*inv2*sg2/count; C2=-a2*sb2/count-A2*mean2
    def proj(b0,U):
        h,l=split(blk(du,b0,U)*a2+blk(pre,b0,U)*A2+C2)
        r=dot_nt(w2m[...],h); rl2=dot_nt(w2m[0:MY,:],l)
        d=r[:MY]+r[MY:2*MY]+rl2; t=(r[2*MY:3*MY]+r[3*MY:]).astype(BF)
        gt=jnp.concatenate([h[:,:MY],l[:,:MY]],axis=1)
        for k in range(U):
            w=slice(k*128,k*128+128)
            acc[b0+k]=jnp.concatenate([d[:,w],jnp.zeros((2*MY,128),F32)],axis=0)
            v4[b0+k]=jnp.concatenate([t[:,w],gt[w].T],axis=0)
    for_blocks(nb,8,proj)
    acc[NB]=jnp.zeros(acc.shape[1:],F32)
    agg_rows(lists,S,v4,acc)
    lane=lambda x: jnp.sum(x,axis=1,keepdims=True)
    stc=st[:,:128].T[:MY]
    mean1=stc[:,0:1]; inv1=stc[:,1:2]
    a1=ncol[:,0:1]*inv1; c1=ncol[:,1:2]-mean1*a1
    ha1=0.5*a1; hc1=0.5*c1
    def back1(b0,U):
        for k in range(U):
            p=pre1[b0+k]
            d=acc[b0+k,:MY]*dgelu_half(p*ha1+hc1)
            acc[b0+k,:MY]=d
            colsum[0]+=d; colsum[1]+=d*(p-mean1)
    for_blocks(nb,8,back1)
    sb1=lane(colsum[0]); sg1=lane(colsum[1])*inv1
    A1=-a1*inv1*sg1/count; C1=-a1*sb1/count-A1*mean1
    def last(i,_):
        s=lax.rem(i,NS)
        for c in ring(i): c.wait()
        def part(b0,off,U):
            f=lambda ref: ref[s,pl.ds(off,U)].reshape(U*128,ref.shape[3])
            x=[acc[b0+k] for k in range(U)]
            gh,gl=split(jnp.concatenate([x[k][:MY]*a1+pre1[b0+k]*A1+C1 for k in range(U)],axis=1))
            R1[...]+=dot(jnp.concatenate([gh,gl],axis=0),f(rfh))
            R2[...]+=dot(gh,jnp.concatenate([f(rfl),f(raf)],axis=1))
            ah,al=split(jnp.concatenate([x[k][MY:2*MY]+x[k][2*MY:] for k in range(U)],axis=1))
            gt=jnp.concatenate([v4[b0+k,MY:] for k in range(U)],axis=1)
            RS[...]+=dot(jnp.concatenate([gt,ah,al],axis=0),f(rh))
            RL[...]+=dot(jnp.concatenate([gt[:MY],ah],axis=0),f(rl))
        @pl.when((i+1)*U8<=nb)
        def _(): part(i*U8,0,U8)
        @pl.when((i+1)*U8>nb)
        def _():
            lax.fori_loop(0,nb-i*U8,lambda k,_:(part(i*U8+k,k,1),0)[1],0)
        @pl.when(i+NS<nch)
        def _():
            for c in ring(i+NS): c.start()
        return 0
    lax.fori_loop(0,nch,last,0)
    RSv=RS[...]; RLv=RL[...]; nk=H//128
    for h in range(2):
        gs=RSv[2*h*MY:(2*h+1)*MY]+RSv[(2*h+1)*MY:(2*h+2)*MY]+RLv[h*MY:(h+1)*MY]
        for k in range(nk): g_out[(h*nk+k)*MY:(h*nk+k+1)*MY,:]=gs[:,k*128:k*128+128]
    R1v=R1[...]; R2v=R2[...]
    q=2*nk*MY
    g_out[q:q+MY,:]=R1v[:MY]+R1v[MY:]+R2v[:,:128]
    g_out[q+MY:q+2*MY,:]=R2v[:,128:]
    RHv=RH[...]; gh=RHv[:MY]+RHv[MY:]
    loss=jnp.sum(cross[...])+pair_loss
    extra=jnp.concatenate([sg2[:,:128],sb2[:,:128],jnp.broadcast_to(loss,(1,128)),jnp.zeros((5,128),F32)],axis=0).T[:MY]
    gh=jnp.concatenate([RHv[:MY,:CP]+RHv[:MY,CP:2*CP]+RHv[MY:,:CP],gh[:,2*CP:3*CP],sg1,sb1,extra,jnp.zeros((MY,128-2*CP-10),F32)],axis=1)
    g_out[q+2*MY:q+3*MY,:]=gh
    if g_out.shape[0]>q+3*MY: g_out[q+3*MY:,:]=jnp.zeros((g_out.shape[0]-q-3*MY,128),F32)

def call_kc(sizes,lists,S,fth,ftl,af,h1h,h1l,pre,pre1,h2t,lg,st,own,recv,labels,pairs,wt,w2m,npar,ncol,CLS,rows):
    NB=fth.shape[0]; H=pre.shape[2]; CP=lg.shape[1]; MY=ncol.shape[0]; NS=3; U8=8
    ANY=pl.BlockSpec(memory_space=pltpu.HBM); VM=pl.BlockSpec(memory_space=pltpu.VMEM); SM=pl.BlockSpec(memory_space=pltpu.SMEM)
    V=pltpu.VMEM
    return pl.pallas_call(functools.partial(kc,CLS=CLS),out_shape=V((rows,128),F32),
        in_specs=[SM,SM]+[VM]*5+[ANY]*5+[VM]*9,out_specs=VM,
        scratch_shapes=[V((NS,U8,128,H),BF)]*2+[V((NS,U8,128,128),BF)]*3+[
            V((NB,128,H),F32),V((NB,2*CP,128),BF),V((NB+1,max(3*MY,2*CP),128),F32),V((NB,3*MY,128),BF),
            V((2,8,H),F32),V((1,128),F32),V((2*MY,3*CP),F32),V((4*MY,H),F32),V((2*MY,H),F32),V((2*MY,128),F32),V((MY,256),F32),V((2,MY,128),F32),
            pltpu.SemaphoreType.DMA((NS,5))],
        compiler_params=pltpu.CompilerParams(vmem_limit_bytes=VLIM))(sizes,lists,*in_vmem(S,pre,pre1,h2t,lg),h1h,h1l,fth,ftl,af,st,*in_vmem(own,recv),labels,pairs,wt,w2m,npar,ncol)

def at(index): return {"graph": index}
def meet(n):
    me=lax.axis_index("graph")
    barrier=pltpu.get_barrier_semaphore()
    for k in range(1,n):
        pl.semaphore_signal(barrier,inc=1,device_id=at(lax.rem(me+k,n)),device_id_type=pl.DeviceIdType.MESH)
    pl.semaphore_wait(barrier,n-1)

def kx(own,out,send,recv,n):
    me=lax.axis_index("graph")
    meet(n)
    copies=[]
    for k in range(1,n):
        peer=lax.rem(me+k,n)
        c=pltpu.make_async_remote_copy(src_ref=own.at[peer],dst_ref=out.at[me],send_sem=send.at[k-1],recv_sem=recv.at[k-1],
            device_id=at(peer),device_id_type=pl.DeviceIdType.MESH)
        c.start(); copies.append(c)
    out[me]=own[me]
    for c in copies: c.wait()

def call_kx(own,n):
    VM=pl.BlockSpec(memory_space=pltpu.VMEM)
    return pl.pallas_call(functools.partial(kx,n=n),out_shape=pltpu.VMEM(own.shape,own.dtype),in_specs=[VM],out_specs=VM,
        scratch_shapes=[pltpu.SemaphoreType.DMA((n-1,)),pltpu.SemaphoreType.DMA((n-1,))],
        compiler_params=pltpu.CompilerParams(vmem_limit_bytes=8<<20,collective_id=1,has_side_effects=True))(*in_vmem(own))

def kr(g,out,parts,send1,recv1,send2,recv2,n):
    me=lax.axis_index("graph")
    piece=g.shape[0]//n
    def rows(i): return pl.ds(pl.multiple_of(i*piece,8),piece)
    meet(n)
    copies=[]
    for k in range(1,n):
        peer=lax.rem(me+k,n)
        c=pltpu.make_async_remote_copy(src_ref=g.at[rows(peer)],dst_ref=parts.at[k-1],send_sem=send1.at[k-1],recv_sem=recv1.at[k-1],
            device_id=at(peer),device_id_type=pl.DeviceIdType.MESH)
        c.start(); copies.append(c)
    total=g[rows(me),:]
    for k,c in enumerate(copies):
        c.wait_recv(); total+=parts[k]
    out[rows(me),:]=total
    back=[]
    for k in range(1,n):
        peer=lax.rem(me+k,n)
        c=pltpu.make_async_remote_copy(src_ref=out.at[rows(me)],dst_ref=out.at[rows(me)],send_sem=send2.at[k-1],recv_sem=recv2.at[k-1],
            device_id=at(peer),device_id_type=pl.DeviceIdType.MESH)
        c.start(); back.append(c)
    for c in copies: c.wait_send()
    for c in back: c.wait()

def call_kr(g,n):
    VM=pl.BlockSpec(memory_space=pltpu.VMEM); D=pltpu.SemaphoreType.DMA((n-1,))
    return pl.pallas_call(functools.partial(kr,n=n),out_shape=jax.ShapeDtypeStruct(g.shape,g.dtype),in_specs=[VM],out_specs=VM,
        scratch_shapes=[pltpu.VMEM((n-1,g.shape[0]//n,128),F32),D,D,D,D],
        compiler_params=pltpu.CompilerParams(vmem_limit_bytes=8<<20,collective_id=2,has_side_effects=True))(*in_vmem(g))

def kp(wf,ws,wh,npar,out):
    _,MY,FIN=wf.shape; H=ws.shape[2]; CLS=wh.shape[0]; CP=-(-CLS//16)*16; nk=H//128
    out[...]=jnp.zeros_like(out)
    for h in range(2):
        for k in range(nk):
            r=(h*nk+k)*MY; out[r:r+MY,:]=ws[h,:,k*128:k*128+128]
        r=2*nk*MY+h*MY; out[r:r+MY,:FIN]=wf[h]
        r=2*nk*MY+2*MY+h*CP; out[r:r+CLS,:MY]=wh[:,h,:]
        r=2*nk*MY+2*MY+2*CP+2*h; out[r:r+2,:MY]=npar[h]

def call_kp(wf,ws,wh,npar):
    _,MY,FIN=wf.shape; H=ws.shape[2]; CP=-(-wh.shape[0]//16)*16
    rows=-(-(2*H//128*MY+2*MY+2*CP+8)//16)*16
    VM=pl.BlockSpec(memory_space=pltpu.VMEM)
    return pl.pallas_call(kp,out_shape=jax.ShapeDtypeStruct((rows,128),F32),in_specs=[VM]*4,out_specs=VM)(wf,ws,wh,npar)

def renew(weight, momentum, average, gradient):
    momentum_new = MOMENTUM * momentum + gradient
    weight_new = weight - STEP_RATE * (gradient + MOMENTUM * momentum_new)
    average_new = AVERAGE_KEEP * average + (1.0 - AVERAGE_KEEP) * weight_new
    return momentum_new, average_new, weight_new

def ku(sizes,g,*refs):
    weights,momenta,averages,outs,loss,count=refs[:4],refs[4:8],refs[8:12],refs[12:24],refs[24],refs[25]
    _,MY,FIN=weights[0].shape; H=weights[1].shape[2]; CLS=weights[2].shape[0]; CP=-(-CLS//16)*16; nk=H//128
    q=2*nk*MY
    shift=lax.axis_index("col")*MY
    def store(i,where,grad):
        for o,v in zip(outs[3*i:3*i+3],renew(weights[i][where],momenta[i][where],averages[i][where],grad)): o[where]=v
    head=g[q+2*MY:q+3*MY,:].T
    for h in range(2):
        x=jnp.concatenate([g[(h*nk+k)*MY:(h*nk+k+1)*MY,:] for k in range(nk)],axis=1)
        store(1,(h,),pltpu.roll(x,shift,1))
        store(0,(h,),g[q+h*MY:q+h*MY+MY,:FIN])
        store(2,(slice(None),h,slice(None)),head[h*CP:h*CP+CLS,:MY])
    store(3,(0,),head[2*CP:2*CP+2,:MY])
    store(3,(1,),head[2*CP+2:2*CP+4,:MY])
    loss[0,0]=g[q+2*MY,2*CP+4]
    count[0,0]=my_sizes(sizes)[2].astype(F32)

def call_ku(sizes,g,weights,momenta,averages):
    VM=pl.BlockSpec(memory_space=pltpu.VMEM); SM=pl.BlockSpec(memory_space=pltpu.SMEM)
    shapes=[jax.ShapeDtypeStruct(w.shape,F32) for w in weights for _ in range(3)]
    return pl.pallas_call(ku,out_shape=(*shapes,*[jax.ShapeDtypeStruct((1,1),F32)]*2),in_specs=[SM]+[VM]*13,out_specs=[VM]*12+[SM]*2)(sizes,g,*weights,*momenta,*averages)

MOMENTUM=0.9; STEP_RATE=2.0; AVERAGE_KEEP=0.9

def per_device(n_graph, n_col, features, blocks, block_values, group_sizes, labels, pair_nodes, weight_first, weight_second, weight_head,
               norm_params, momentum_first, momentum_second, momentum_head, momentum_norms, average_first, average_second,
               average_head, average_norms):
    MY=weight_first.shape[2]; H=MY*n_col; CLS=weight_head.shape[2]; CP=-(-CLS//16)*16
    G=group_sizes.shape[0]; N=features.shape[2]; NB=N//128; PEER=pair_nodes.shape[3]
    def native(first,second,head,norms):
        return first.transpose(0,2,1),second.transpose(0,2,1),head.transpose(2,0,1),norms
    weights=native(weight_first,weight_second,weight_head,norm_params)
    momenta=native(momentum_first,momentum_second,momentum_head,momentum_norms)
    averages=native(average_first,average_second,average_head,average_norms)
    packed=call_kp(*weights)
    shards=[packed]+[lax.ppermute(packed,"col",[((j+k)%n_col,j) for j in range(n_col)]) for k in range(1,n_col)]
    sizes=group_sizes.T
    S,lists,fth,ftl,af=call_k0(sizes,blocks[0],features.transpose(1,0,2),block_values[0])
    pairs=pair_nodes[0].reshape(2*G,PEER)
    h1h,h1l,pre,pre1,st,h2t,lg,own,S,npar,wt,w2m,ncol=call_kb(sizes,lists,S,fth,ftl,af,shards,pairs,MY=MY,CP=CP)
    recv=call_kx(own,n_graph)
    unit=8*n_graph; rows=-(-(2*H//128*MY+3*MY)//unit)*unit
    g=call_kc(sizes,lists,S,fth,ftl,af,h1h,h1l,pre,pre1,h2t,lg,st,own,recv,labels[0].reshape(NB,1,128),pairs,wt,w2m,npar,ncol,CLS=CLS,rows=rows)
    g=call_kr(g,n_graph)
    *new,loss,count=call_ku(sizes,g,weights,momenta,averages)
    first=[x.transpose(0,2,1) for x in new[0:3]]
    second=[x.transpose(0,2,1) for x in new[3:6]]
    head=[x.transpose(1,2,0) for x in new[6:9]]
    return (loss[0,0],count[0,0],*first,*second,*head,*new[9:12])

def solution(mesh):
    P=jax.sharding.PartitionSpec
    unit=P(None,None,"col"); head=P(None,"col",None)
    weights=(unit,unit,head,unit)
    in_specs=(P("graph",None,None),P("graph",None,None),P("graph",None,None,None),P(),P("graph",None),P("graph",None,None,None))+weights*3
    out_specs=(P(),P())+(unit,)*6+(head,)*3+(unit,)*3
    return jax.shard_map(functools.partial(per_device,mesh.shape["graph"],mesh.shape["col"]),mesh=mesh,in_specs=in_specs,out_specs=out_specs,check_vma=False)
```
